32 devices in a mesh: wide: 8 (over z, x), narrow: 4 (over y, core).
Axes of the slice: x: 2, y: 2, z: 4, core: 2. Of those that a mesh axis runs over, the one named last changes fastest.
Arguments:
- activations: bfloat16 [64, 512, 512], P('wide', 'narrow'), may hold values from -6 to 6
- cotangent: bfloat16 [64, 512, 512], P('wide', 'narrow'), may hold values from -6 to 6
- doc_lengths: int32 [64, 5], P('wide'), may hold values from 1 to 508, as said below
- expand_weight: float32 [512, 3072], P('wide'), may hold values from -0.25 to 0.25
- expand_momentum: float32 [512, 3072], P('wide'), may hold values from -0.0009765625 to 0.0009765625
- expand_variance: float32 [512, 3072], P('wide'), may hold values from 1.9054879e-10 to 1.5243903e-09
- expand_average: float32 [512, 3072], P('wide'), may hold values from -0.25 to 0.25
- shrink_weight: float32 [1536, 512], P('wide'), may hold values from -0.3125 to 0.3125
- shrink_momentum: float32 [1536, 512], P('wide'), may hold values from -0.0009765625 to 0.0009765625
- shrink_variance: float32 [1536, 512], P('wide'), may hold values from 1.9054879e-10 to 1.5243903e-09
- shrink_average: float32 [1536, 512], P('wide'), may hold values from -0.3125 to 0.3125
- spatial_weight: float32 [512, 512], P('wide'), may hold values from -0.5 to 0.5
- spatial_momentum: float32 [512, 512], P('wide'), may hold values from -0.0009765625 to 0.0009765625
- spatial_variance: float32 [512, 512], P('wide'), may hold values from 1.9054879e-10 to 1.5243903e-09
- spatial_average: float32 [512, 512], P('wide'), may hold values from -0.5 to 0.5
- norm_gains: float32 [2048], P('wide'), may hold values from 0.3 to 3.5
- gains_momentum: float32 [2048], P('wide'), may hold values from -0.0029296875 to 0.0029296875
- gains_variance: float32 [2048], P('wide'), may hold values from 1.1432927e-09 to 9.527439e-09
- gains_average: float32 [2048], P('wide'), may hold values from 0.5 to 1.5
- spatial_bias: float32 [512], P('wide'), may hold values from 0.5 to 1.5
- bias_momentum: float32 [512], P('wide'), may hold values from -0.0029296875 to 0.0029296875
- bias_variance: float32 [512], P('wide'), may hold values from 1.1432927e-09 to 9.527439e-09
- bias_average: float32 [512], P('wide'), may hold values from 0.5 to 1.5
Outputs:
- layer_out: bfloat16 [64, 512, 512], P('wide', 'narrow')
- input_grad: float32 [64, 512, 512], P('wide', 'narrow')
- grad_norm: float32 [], replicated
- expand_grad: float32 [512, 3072], P('wide')
- expand_moment: float32 [512, 3072], P('wide')
- expand_square: float32 [512, 3072], P('wide')
- expand_updated: float32 [512, 3072], P('wide')
- expand_smoothed: float32 [512, 3072], P('wide')
- shrink_grad: float32 [1536, 512], P('wide')
- shrink_moment: float32 [1536, 512], P('wide')
- shrink_square: float32 [1536, 512], P('wide')
- shrink_updated: float32 [1536, 512], P('wide')
- shrink_smoothed: float32 [1536, 512], P('wide')
- spatial_grad: float32 [512, 512], P('wide')
- spatial_moment: float32 [512, 512], P('wide')
- spatial_square: float32 [512, 512], P('wide')
- spatial_updated: float32 [512, 512], P('wide')
- spatial_smoothed: float32 [512, 512], P('wide')
- gains_grad: float32 [2048], P('wide')
- gains_moment: float32 [2048], P('wide')
- gains_square: float32 [2048], P('wide')
- gains_updated: float32 [2048], P('wide')
- gains_smoothed: float32 [2048], P('wide')
- bias_grad: float32 [512], P('wide')
- bias_moment: float32 [512], P('wide')
- bias_square: float32 [512], P('wide')
- bias_updated: float32 [512], P('wide')
- bias_smoothed: float32 [512], P('wide')
The draws below stay inside these ranges and needn't reach their ends.
Inputs may be any that keep to these rules, and one draw needn't show every extreme that they name: `doc_lengths`: every row's entries sum to 512 and its last entry is 1 or more. In each aligned block of 8 rows one row has a document from slot 1 to slot 508.
All inputs are finite; a program needn't handle non-finite values.
Results may differ from the reference program's by a relative error of at most 0.012.
Values may be sent and summed in bfloat16 or wider, within the bound.
No kernel may reach another device: no remote copies, remote signals or barrier semaphores. Data moves between devices by JAX's collectives and lax.ppermute only.
A program may use at most 128 MiB of HBM per device.

```python
import math
import jax
import jax.numpy as jnp
from jax import lax

D = 512
FF = 3072
ROW = 512
ROWS_G = 8
DOCS = 5
STEP = 10
HALF = 1536
ROWS = 64
PARAMS = 2624000


def draw_doc_lengths(key, part):
    key = jax.random.fold_in(key, 23)
    first_key, second_key = jax.random.split(key)
    draw_weights = jax.random.randint(first_key, (ROWS, DOCS), 1, 8, dtype=jnp.int32)
    weight_total = jnp.sum(draw_weights, axis=1, keepdims=True, dtype=jnp.int32)
    shares = 1 + (ROW - DOCS) * draw_weights // weight_total
    remainder = ROW - jnp.sum(shares, axis=1, keepdims=True, dtype=jnp.int32)
    column = jnp.arange(DOCS, dtype=jnp.int32)[None, :]
    shares = jnp.where(column == 0, shares + remainder, shares)
    groups = ROWS // ROWS_G
    chosen = jax.random.randint(second_key, (groups,), 0, ROWS_G, dtype=jnp.int32)
    row_index = jnp.arange(ROWS, dtype=jnp.int32)
    is_chosen = row_index % ROWS_G == chosen[row_index // ROWS_G]
    long_row = jnp.where(column == 1, ROW - DOCS + 1, 1).astype(jnp.int32)
    return jnp.where(is_chosen[:, None], long_row, shares).astype(jnp.int32)


def draw_norm_gains(key, part):
    key = jax.random.fold_in(key, 11)
    places = jnp.arange(D + HALF).astype(jnp.float32)
    position = jnp.where(places < D, places / D, (places - D) / HALF)
    factor = jax.random.uniform(key, (D + HALF,), jnp.float32, 0.65, 1.35)
    rising = 0.6 + 1.2 * position
    return (rising * factor).astype(jnp.float32)


def spiked(drawn, rng, source, target, parts, factor):
    owner, partner = [(jnp.arange(drawn.shape[dim]) // (drawn.shape[dim] // parts)).reshape([-1 if axis == dim else 1 for axis in range(drawn.ndim)]) for dim in (source, target)]
    chosen = jax.random.permutation(rng, parts)[partner]
    strong = (owner == chosen) | (owner == (partner + parts // 2) % parts)
    return jnp.where(strong, factor * drawn, drawn)


def block_scale(stream_key, extent, pieces, least, top_value):
    loudness, own = 1.0, jax.random.fold_in(stream_key, 6)
    for dim, shards_of in pieces:
        heights = jnp.exp(jax.random.uniform(jax.random.fold_in(own, dim), (shards_of,), jnp.float32, least / len(pieces), top_value / len(pieces)))
        loudness = loudness * jnp.repeat(heights, extent[dim] // shards_of).reshape([-1 if axis == dim else 1 for axis in range(len(extent))])
    return loudness


def scatter_about(rng, shape, deviation, most, cuts=(), held_as=jnp.bfloat16):
    array = jax.random.normal(rng, shape, jnp.float32) * deviation
    if len(cuts) > 0:
        array = block_scale(rng, shape, cuts, -0.22, 0.18) * array
    return jnp.clip(array, min=-most, max=most).astype(held_as)


def bell_draw_with(own_key, extent, width, bound, cuts, heavy, kind=jnp.bfloat16):
    entries = width * jax.random.normal(own_key, extent, jnp.float32)
    if cuts:
        entries = entries * block_scale(own_key, extent, cuts, -0.22, 0.18)
    return jnp.clip(spiked(entries, jax.random.fold_in(own_key, 3), *heavy), -bound, bound).astype(kind)


def setup_inputs(seed: int = 0) -> dict:
    key_of = jax.random.split(jax.random.key(seed), 24)
    activations = bell_draw_with(key_of[0], (ROWS, ROW, D), 1.0, 6.0, ((0, 8), (1, 4)), (0, 2, 8, 2.0))
    cotangent = scatter_about(key_of[1], (ROWS, ROW, D), 1.0, 6.0, ((0, 8), (1, 4)))
    doc_lengths = draw_doc_lengths(jax.random.fold_in(key_of[23], 71), 0)
    expand_weight = scatter_about(key_of[3], (D, FF), D ** -0.5, 0.25, ((0, 8),), jnp.float32)
    expand_momentum = scatter_about(key_of[4], (D, FF), (0.11 * PARAMS ** -0.5), 0.0009765625, ((0, 8),), jnp.float32)
    expand_variance = jnp.clip(jnp.exp(math.log(1.5243902806716392e-09) - 2.0794415 * jax.random.uniform(key_of[5], (D, FF), jnp.float32) ** block_scale(key_of[5], (D, FF), ((0, 8),), -0.2, 0.2)), 1.905487850839549e-10, 1.5243902806716392e-09)
    expand_average = scatter_about(key_of[6], (D, FF), D ** -0.5, 0.25, ((0, 8),), jnp.float32)
    shrink_weight = scatter_about(key_of[7], (HALF, D), (HALF // 4) ** -0.5, 0.3125, ((0, 8),), jnp.float32)
    shrink_momentum = scatter_about(key_of[8], (HALF, D), (0.11 * PARAMS ** -0.5), 0.0009765625, ((0, 8),), jnp.float32)
    shrink_variance = jnp.clip(jnp.exp(math.log(1.5243902806716392e-09) - 2.0794415 * jax.random.uniform(key_of[9], (HALF, D), jnp.float32) ** block_scale(key_of[9], (HALF, D), ((0, 8),), -0.2, 0.2)), 1.905487850839549e-10, 1.5243902806716392e-09)
    shrink_average = scatter_about(key_of[10], (HALF, D), (HALF // 4) ** -0.5, 0.3125, ((0, 8),), jnp.float32)
    spatial_weight = scatter_about(key_of[11], (ROW, ROW), (ROW // 4) ** -0.5, 0.5, ((0, 8),), jnp.float32)
    spatial_momentum = scatter_about(key_of[12], (ROW, ROW), (0.11 * PARAMS ** -0.5), 0.0009765625, ((0, 8),), jnp.float32)
    spatial_variance = jnp.clip(jnp.exp(math.log(1.5243902806716392e-09) - 2.0794415 * jax.random.uniform(key_of[13], (ROW, ROW), jnp.float32) ** block_scale(key_of[13], (ROW, ROW), ((0, 8),), -0.2, 0.2)), 1.905487850839549e-10, 1.5243902806716392e-09)
    spatial_average = scatter_about(key_of[14], (ROW, ROW), (ROW // 4) ** -0.5, 0.5, ((0, 8),), jnp.float32)
    norm_gains = draw_norm_gains(jax.random.fold_in(key_of[23], 71), 0)
    gains_momentum = scatter_about(key_of[16], (D + HALF,), (0.3 * PARAMS ** -0.5), 0.0029296875, ((0, 8),), jnp.float32)
    gains_variance = jnp.clip(jnp.exp(math.log(9.52743928195332e-09) - 2.1202636 * jax.random.uniform(key_of[17], (D + HALF,), jnp.float32) ** block_scale(key_of[17], (D + HALF,), ((0, 8),), -0.2, 0.2)), 1.1432926827481538e-09, 9.52743928195332e-09)
    gains_average = jnp.clip(1.0 + 0.1 * jax.random.normal(key_of[18], (D + HALF,), jnp.float32), 0.5, 1.5)
    spatial_bias = jnp.clip(0.5 + 1.0 * jax.random.uniform(key_of[19], (ROW,), jnp.float32) ** block_scale(key_of[19], (ROW,), ((0, 8),), -0.2, 0.2), 0.5, 1.5)
    bias_momentum = scatter_about(key_of[20], (ROW,), (0.3 * PARAMS ** -0.5), 0.0029296875, ((0, 8),), jnp.float32)
    bias_variance = jnp.clip(jnp.exp(math.log(9.52743928195332e-09) - 2.1202636 * jax.random.uniform(key_of[21], (ROW,), jnp.float32) ** block_scale(key_of[21], (ROW,), ((0, 8),), -0.2, 0.2)), 1.1432926827481538e-09, 9.52743928195332e-09)
    bias_average = jnp.clip(0.5 + 1.0 * jax.random.uniform(key_of[22], (ROW,), jnp.float32) ** block_scale(key_of[22], (ROW,), ((0, 8),), -0.2, 0.2), 0.5, 1.5)
    return {"activations": activations, "cotangent": cotangent, "doc_lengths": doc_lengths, "expand_weight": expand_weight, "expand_momentum": expand_momentum, "expand_variance": expand_variance, "expand_average": expand_average, "shrink_weight": shrink_weight, "shrink_momentum": shrink_momentum, "shrink_variance": shrink_variance, "shrink_average": shrink_average, "spatial_weight": spatial_weight, "spatial_momentum": spatial_momentum, "spatial_variance": spatial_variance, "spatial_average": spatial_average, "norm_gains": norm_gains, "gains_momentum": gains_momentum, "gains_variance": gains_variance, "gains_average": gains_average, "spatial_bias": spatial_bias, "bias_momentum": bias_momentum, "bias_variance": bias_variance, "bias_average": bias_average}


LAYER_EPS = 1e-05
CLIP_LIMIT = 1.0
BETA_FIRST = 0.9
BETA_SECOND = 0.999
ADAM_EPS = 1e-08
RATE_MATRIX = 0.03
RATE_VECTOR = 0.2
DECAY_MATRIX = 0.1
EMA_DECAY = 0.9999

@jax.custom_vjp
def low(v):
    return lax.optimization_barrier(v.astype(jnp.bfloat16)).astype(jnp.float32)

@jax.custom_vjp
def low_back(v):
    return v

def low_keep(v):
    return (low(v), None)

def low_pass(kept, grad):
    return (grad,)

def back_keep(v):
    return (v, None)

def back_low(kept, grad):
    return (low(grad),)
low.defvjp(low_keep, low_pass)
low_back.defvjp(back_keep, back_low)

def layer_normal(values, scales):
    centre = lax.optimization_barrier(jnp.mean(values, axis=-1, keepdims=True))
    shifted = values - centre
    spread = lax.optimization_barrier(jnp.mean(shifted * shifted, axis=-1, keepdims=True))
    return shifted * lax.rsqrt(spread + LAYER_EPS) * scales

def row_masks(lengths):
    bounds = jnp.cumsum(lengths, axis=1, dtype=jnp.int32)
    places = jnp.arange(ROW, dtype=jnp.int32)
    doc_ids = lax.optimization_barrier(jnp.sum((places[None, :, None] >= bounds[:, None, :]).astype(jnp.int32), axis=2, dtype=jnp.int32))
    live_slots = places[None, :] < bounds[:, DOCS - 2][:, None]
    same_doc = (doc_ids[:, :, None] == doc_ids[:, None, :]) & live_slots[:, :, None] & live_slots[:, None, :]
    return (same_doc.astype(jnp.float32), live_slots.astype(jnp.float32))

def forward(activations, lengths, expand_weight, shrink_weight, spatial_weight, norm_gains, spatial_bias):
    highest = lax.Precision.HIGHEST
    expand_low = low(expand_weight)
    shrink_low = low(shrink_weight)
    spatial_low = low(spatial_weight)
    gains_low = low(norm_gains)
    bias_low = low(spatial_bias)
    first_gain = gains_low[:D]
    second_gain = gains_low[D:]
    same_doc, live_slots = row_masks(lengths)
    normed = low(layer_normal(activations, first_gain))
    hidden = low_back(jnp.einsum('rpd,df->rpf', normed, expand_low, precision=highest))
    active = jax.nn.gelu(hidden)
    content = active[..., :HALF]
    gating = active[..., HALF:]
    gate_normed = low_back(low(layer_normal(gating, second_gain)))
    mixed_raw = jnp.einsum('rij,rjc->ric', same_doc * spatial_low[None], gate_normed, precision=highest)
    mixed_raw = mixed_raw + live_slots[:, :, None] * bias_low[None, :, None]
    mixed_vals = low_back(low(mixed_raw))
    gated = low(content * mixed_vals)
    return activations + jnp.einsum('rph,hd->rpd', gated, shrink_low, precision=highest)

def adam_update(weight, gradient, momentum, variance, average, clip_scale, step_rate, decay_rate):
    ema_rate = min(EMA_DECAY, (1.0 + STEP) / (10.0 + STEP))
    clipped = clip_scale * gradient
    moment = BETA_FIRST * momentum + (1.0 - BETA_FIRST) * clipped
    square = BETA_SECOND * variance + (1.0 - BETA_SECOND) * clipped * clipped
    first_hat = moment / (1.0 - BETA_FIRST ** STEP)
    second_hat = square / (1.0 - BETA_SECOND ** STEP)
    updated = weight - step_rate * (first_hat / (jnp.sqrt(second_hat) + ADAM_EPS) + decay_rate * weight)
    smoothed = ema_rate * average + (1.0 - ema_rate) * updated
    return (clipped, moment, square, updated, smoothed)

def reference(activations, cotangent, doc_lengths, expand_weight, expand_momentum, expand_variance, expand_average, shrink_weight, shrink_momentum, shrink_variance, shrink_average, spatial_weight, spatial_momentum, spatial_variance, spatial_average, norm_gains, gains_momentum, gains_variance, gains_average, spatial_bias, bias_momentum, bias_variance, bias_average):
    rows_total = activations.shape[0]
    block_rows = math.gcd(rows_total, 8)
    block_count = rows_total // block_rows
    acts_blocks = activations.astype(jnp.float32).reshape(block_count, block_rows, ROW, D)
    cots_blocks = cotangent.astype(jnp.float32).reshape(block_count, block_rows, ROW, D)
    lens_blocks = doc_lengths.reshape(block_count, block_rows, DOCS)

    def block_step(totals, inputs):
        block_acts, block_cots, block_lens = inputs

        def apply_block(acts_in, expand_in, shrink_in, spatial_in, gains_in, bias_in):
            return forward(acts_in, block_lens, expand_in, shrink_in, spatial_in, gains_in, bias_in)
        outputs, pullback = jax.vjp(apply_block, block_acts, expand_weight, shrink_weight, spatial_weight, norm_gains, spatial_bias)
        gradients = pullback(block_cots)
        new_totals = (totals[0] + gradients[1], totals[1] + gradients[2], totals[2] + gradients[3], totals[3] + gradients[4], totals[4] + gradients[5])
        return (new_totals, (outputs.astype(jnp.bfloat16), gradients[0]))
    zero_totals = (jnp.zeros(expand_weight.shape, jnp.float32), jnp.zeros(shrink_weight.shape, jnp.float32), jnp.zeros(spatial_weight.shape, jnp.float32), jnp.zeros(norm_gains.shape, jnp.float32), jnp.zeros(spatial_bias.shape, jnp.float32))
    totals, (out_blocks, grad_blocks) = lax.scan(block_step, zero_totals, (acts_blocks, cots_blocks, lens_blocks))
    layer_out = out_blocks.reshape(rows_total, ROW, D)
    input_grad = grad_blocks.reshape(rows_total, ROW, D)
    expand_raw, shrink_raw, spatial_raw, gains_raw, bias_raw = totals
    square_total = jnp.sum(expand_raw * expand_raw) + jnp.sum(shrink_raw * shrink_raw) + jnp.sum(spatial_raw * spatial_raw) + jnp.sum(gains_raw * gains_raw) + jnp.sum(bias_raw * bias_raw)
    grad_norm = jnp.sqrt(square_total)
    clip_scale = CLIP_LIMIT / jnp.maximum(grad_norm, CLIP_LIMIT)
    expand_grad, expand_moment, expand_square, expand_updated, expand_smoothed = adam_update(expand_weight, expand_raw, expand_momentum, expand_variance, expand_average, clip_scale, RATE_MATRIX, DECAY_MATRIX)
    shrink_grad, shrink_moment, shrink_square, shrink_updated, shrink_smoothed = adam_update(shrink_weight, shrink_raw, shrink_momentum, shrink_variance, shrink_average, clip_scale, RATE_MATRIX, DECAY_MATRIX)
    spatial_grad, spatial_moment, spatial_square, spatial_updated, spatial_smoothed = adam_update(spatial_weight, spatial_raw, spatial_momentum, spatial_variance, spatial_average, clip_scale, RATE_MATRIX, DECAY_MATRIX)
    gains_grad, gains_moment, gains_square, gains_updated, gains_smoothed = adam_update(norm_gains, gains_raw, gains_momentum, gains_variance, gains_average, clip_scale, RATE_VECTOR, 0.0)
    bias_grad, bias_moment, bias_square, bias_updated, bias_smoothed = adam_update(spatial_bias, bias_raw, bias_momentum, bias_variance, bias_average, clip_scale, RATE_VECTOR, 0.0)
    return (layer_out, input_grad, grad_norm, expand_grad, expand_moment, expand_square, expand_updated, expand_smoothed, shrink_grad, shrink_moment, shrink_square, shrink_updated, shrink_smoothed, spatial_grad, spatial_moment, spatial_square, spatial_updated, spatial_smoothed, gains_grad, gains_moment, gains_square, gains_updated, gains_smoothed, bias_grad, bias_moment, bias_square, bias_updated, bias_smoothed)
```

```python
import functools

import jax
import jax.numpy as jnp
from jax import lax
from jax.experimental import pallas as pl
from jax.experimental.pallas import tpu as pltpu
from jax.sharding import PartitionSpec as P

D = 512
FF = 3072
ROW = 512
DOCS = 5
STEP = 10
HALF = 1536

LAYER_EPS = 1e-05
CLIP_LIMIT = 1.0
BETA_FIRST = 0.9
BETA_SECOND = 0.999
ADAM_EPS = 1e-08
RATE_MATRIX = 0.03
RATE_VECTOR = 0.2
DECAY_MATRIX = 0.1
EMA_DECAY = 0.9999

F32 = jnp.float32
BF16 = jnp.bfloat16
GELU_A = 0.7978845608028654
GELU_B = GELU_A * 0.044715
LANES = 128
CHUNK = 64
BLOCK = 16
VMEM_LIMIT = 16 * 1024 * 1024

PIECES = ((0, 0), (1, 0), (0, 1), (1, 1))
WIDTH = 256
SPLIT = 1024
VECTOR_LANES = 128


def gelu_gate(hidden):
    squares = hidden * hidden
    gate = 0.5 * jnp.tanh(hidden * (GELU_A + GELU_B * squares)) + 0.5
    return squares, gate


def gelu_slope(hidden, squares, gate):
    return gate * (1.0 + hidden * (1.0 - gate) * (2.0 * GELU_A + 6.0 * GELU_B * squares))


def doc_ids(places, lens_ref, row):
    bound = jnp.int32(0)
    ids = jnp.zeros(places.shape, jnp.int32)
    for k in range(DOCS - 1):
        bound = bound + lens_ref[row, k]
        ids = ids + (places >= bound).astype(jnp.int32)
    return ids


def doc_mask(start, rows, lens_ref, row):
    across = doc_ids(lax.broadcasted_iota(jnp.int32, (1, ROW), 1), lens_ref, row)
    down = doc_ids(lax.broadcasted_iota(jnp.int32, (rows, 1), 0) + start, lens_ref, row)
    live = down != DOCS - 1
    return jnp.where(live, down, -1) == across, live


def dot(left, right, dims=((1,), (0,))):
    return lax.dot_general(left, right, (dims, ((), ())), preferred_element_type=F32)


def run(start, size):
    return pl.ds(pl.multiple_of(start, size), size)


def fetch_weights(sources, moves, tree):
    if not tree:
        for source, (_, _, _, target, _, _, _, sem) in zip(sources, moves):
            pltpu.make_async_copy(source, target, sem).start()
        return
    wide, core = lax.axis_index("wide"), lax.axis_index("narrow") & 1
    for base, first, count, target, height, unit, shift, sem in moves:
        for i, (x_off, core_off) in enumerate(PIECES):
            for step in range(4):
                start = (wide ^ (2 * step + x_off)) * height + (core ^ core_off) * unit + shift
                pltpu.make_async_copy(
                    sources[base + i].at[step, :, pl.ds(first, count)], target.at[run(start, 32), :], sem
                ).start()


def wait_weights(targets):
    for target, sem in targets:
        pltpu.make_async_copy(target, target, sem).wait()


def cut_kernel(acts_ref, cots_ref, core_out, pair_out, sems):
    rows_here = core_out.shape[1]
    narrow = lax.axis_index("narrow")
    copies = []
    for i, ref in enumerate((acts_ref, cots_ref)):
        for j, target in ((1, core_out.at[i]), (2, pair_out.at[0, i]), (3, pair_out.at[1, i])):
            source = ref.at[pl.ds((narrow ^ j) * rows_here, rows_here)]
            copies.append(pltpu.make_async_copy(source, target, sems.at[len(copies)]))
    for copy in copies:
        copy.start()
    for copy in copies:
        copy.wait()


def pack_first_kernel(expand_ref, spatial_ref, gains_ref, bias_ref, out_ref, expand, spatial, gains, bias, sems):
    rows = run((lax.axis_index("narrow") & 1) * 32, 32)
    copies = [
        pltpu.make_async_copy(expand_ref.at[rows, pl.ds(HALF, HALF)], expand, sems.at[0]),
        pltpu.make_async_copy(spatial_ref.at[rows, :], spatial, sems.at[1]),
        pltpu.make_async_copy(gains_ref, gains, sems.at[2]),
        pltpu.make_async_copy(bias_ref, bias, sems.at[3]),
    ]
    for copy in copies:
        copy.start()
    for copy in copies:
        copy.wait()
    vectors = jnp.concatenate(
        [
            gains[...],
            jnp.concatenate([bias[...], jnp.zeros((1, LANES - 64), F32)], axis=1),
            jnp.zeros((29, LANES), F32),
        ],
        axis=0,
    )
    out_ref[:, HALF + ROW :] = vectors.astype(BF16)
    out_ref[:, :HALF] = expand[...].astype(BF16)
    out_ref[:, HALF : HALF + ROW] = spatial[...].astype(BF16)


def pack_second_kernel(expand_ref, shrink_ref, expand_out, shrink_out, expand, shrink, sems):
    core = lax.axis_index("narrow") & 1
    copies = [
        pltpu.make_async_copy(expand_ref.at[run(core * 32, 32), pl.ds(0, HALF)], expand, sems.at[0]),
        pltpu.make_async_copy(shrink_ref.at[run(core * 96, 32 * 3), :], shrink, sems.at[1]),
    ]
    for copy in copies:
        copy.start()
    for copy in copies:
        copy.wait()
    expand_out[...] = expand[...].astype(BF16)
    for k in range(3):
        shrink_out[:, k * D : (k + 1) * D] = shrink[k * 32 : (k + 1) * 32, :].astype(BF16)


def stack_kernel(*refs):
    for i, ref in enumerate(refs[:-1]):
        refs[-1][i] = ref[...]


def add_kernel(*refs):
    total = refs[0][...] + refs[1][...]
    if len(refs) == 5:
        total = total + (refs[2][...] + refs[3][...])
    refs[-1][...] = total


def fetch_kernel(*refs):
    count = (len(refs) - 1) // 2
    copies = [pltpu.make_async_copy(refs[i], refs[count + i], refs[-1].at[i]) for i in range(count)]
    for copy in copies:
        copy.start()
    for copy in copies:
        copy.wait()


def gating_kernel(tree, count, members, lens_ref, own_ref, core_ref, side_ref, forward_ref, *refs):
    parts = [core_ref.at[0], side_ref.at[0, 0], forward_ref.at[1, 0]]
    sources, small_sources = refs[:count], refs[count : count + 2]
    (
        normed_ref, xhat_ref, scale_ref, gate_ref, slope_ref, rstd_ref, mixed_ref, spatial_ref, gains_ref, weight,
        small, acts, active, sums, bias_col, sems,
    ) = refs[count + 2 :]
    wide, narrow = lax.axis_index("wide"), lax.axis_index("narrow")
    rows_here, quarter = acts.shape[1:3]

    pltpu.make_async_copy(own_ref.at[pl.ds(narrow * rows_here, rows_here)], acts.at[narrow], sems.at[3]).start()
    for j, part in enumerate(parts):
        pltpu.make_async_copy(part, acts.at[narrow ^ (j + 1)], sems.at[3]).start()
    fetch_weights(
        sources,
        [
            (0, 0, HALF, weight, 64, 32, 0, sems.at[0]),
            (0, HALF, ROW, spatial_ref, 64, 32, 0, sems.at[1]),
        ],
        tree,
    )
    if tree:
        for x_off in range(2):
            for step in range(4):
                pltpu.make_async_copy(
                    small_sources[x_off].at[step, pl.ds(0, BLOCK), pl.ds(HALF + ROW, 128)],
                    small.at[wide ^ (2 * step + x_off)],
                    sems.at[2],
                ).start()
    else:
        pltpu.make_async_copy(small_sources[0], small, sems.at[2]).start()
    wait_weights([(weight, sems.at[0]), (spatial_ref, sems.at[1]), (small, sems.at[2]), (acts, sems.at[3])])
    diagonal = lax.broadcasted_iota(jnp.int32, (64, 128), 0) == lax.broadcasted_iota(jnp.int32, (64, 128), 1)
    for owner in range(8):
        values = small[owner].astype(F32)
        for k in range(2):
            gains_ref[:, owner * 256 + k * 128 : owner * 256 + (k + 1) * 128] = jnp.broadcast_to(
                values[k : k + 1, :], (8, 128)
            )
        column = jnp.sum(jnp.where(diagonal, values[2:3, :], 0.0), axis=1, keepdims=True)
        bias_col[owner * 64 : (owner + 1) * 64, :] = jnp.broadcast_to(column, (64, 128))

    def do_row(row, carry):
        for member in range(members):
            here = slice(member * quarter, (member + 1) * quarter)
            values = acts[member, row].astype(F32)
            shifted = values - jnp.mean(values, axis=1, keepdims=True)
            scale = lax.rsqrt(jnp.mean(shifted * shifted, axis=1, keepdims=True) + LAYER_EPS)
            xhat = shifted * scale
            scale_ref[row, here, :] = jnp.broadcast_to(scale, (quarter, 128))
            xhat_ref[row, here, :] = xhat.astype(BF16)
            normed_ref[row, here, :] = (xhat * gains_ref[0:1, :D]).astype(BF16)

        normed = normed_ref[row]
        for c in range(0, HALF, WIDTH):
            hidden = dot(normed, weight[:, c : c + WIDTH])
            for p in range(0, ROW, CHUNK):
                here = slice(p, p + CHUNK)
                values = hidden[here]
                squares, gate = gelu_gate(values)
                slope_ref[row, here, c : c + WIDTH] = gelu_slope(values, squares, gate).astype(BF16)
                result = values * gate
                active[here, c : c + WIDTH] = result
                total = result[:, :LANES] + result[:, LANES:]
                sums[here, :] = total if c == 0 else sums[here, :] + total
        for p in range(0, ROW, CHUNK):
            here = slice(p, p + CHUNK)
            centre = jnp.sum(sums[here, :], axis=1, keepdims=True) * (1.0 / HALF)
            total = jnp.zeros((CHUNK, LANES), F32)
            for c in range(0, HALF, LANES):
                shifted = active[here, c : c + LANES] - centre
                total = total + shifted * shifted
            scale = lax.rsqrt(jnp.sum(total, axis=1, keepdims=True) * (1.0 / HALF) + LAYER_EPS)
            rstd_ref[row, here, :] = jnp.broadcast_to(scale, (CHUNK, 128))
            for c in range(0, HALF, LANES):
                vhat = (active[here, c : c + LANES] - centre) * scale
                gate_ref[row, here, c : c + LANES] = (vhat * gains_ref[0:1, D + c : D + c + LANES]).astype(BF16)

        same, live = doc_mask(0, ROW, lens_ref, narrow * rows_here + row)
        masked = jnp.where(same, spatial_ref[...], jnp.zeros((), BF16))
        bias = jnp.where(live, bias_col[:, 0:1], 0.0)
        for c in range(0, HALF, WIDTH):
            mixed_ref[row, :, c : c + WIDTH] = (dot(masked, gate_ref[row, :, c : c + WIDTH]) + bias).astype(BF16)
        return carry

    lax.fori_loop(0, rows_here, do_row, 0)


def emit_blocks(order, read, columns, first, keep_near, keep_far, send):
    wide, narrow = lax.axis_index("wide"), lax.axis_index("narrow")
    for core in range(2):
        for one in range(2):
            for two in range(2):
                for step in range(4):
                    x_off, y_off = (one, two) if order == "x" else (two, one)
                    values = read(wide ^ (2 * step + x_off), narrow ^ (2 * y_off + core)).astype(BF16)
                    place = pl.ds(first, columns)
                    if core == 1:
                        send[one, two, step, :, place] = values
                    elif one == 1:
                        keep_far[two, step, :, place] = values
                    else:
                        keep_near[two, step, :, place] = values


def reader(matrix, height, part, shift, columns):
    def read(owner, member):
        return matrix[run(owner * height + member * part + shift, BLOCK), columns]

    return read


def content_up_kernel(tree, normed_ref, *refs):
    sources, (content_ref, slope_ref, weight, sem) = refs[:-4], refs[-4:]
    tokens = normed_ref.shape[0] * normed_ref.shape[1]
    if tree:
        fetch_weights(sources, [(0, 0, HALF, weight, 64, 32, 0, sem)], tree)
    else:
        pltpu.make_async_copy(sources[0], weight, sem).start()
    wait_weights([(weight, sem)])

    def do_channels(k, carry):
        channels = run(k * WIDTH, WIDTH)
        hidden = dot(normed_ref[...].reshape(tokens, D), weight[:, channels])
        for p in range(0, tokens, CHUNK):
            r, here = p // ROW, slice(p % ROW, p % ROW + CHUNK)
            values = hidden[p : p + CHUNK]
            squares, gate = gelu_gate(values)
            content_ref[r, here, channels] = (values * gate).astype(BF16)
            slope_ref[r, here, channels] = gelu_slope(values, squares, gate).astype(BF16)
        return carry

    lax.fori_loop(0, HALF // WIDTH, do_channels, 0)


def content_down_kernel(
    tree, count, members, lens_ref, content_ref, slope_ref, mixed_ref, own_ref, core_ref, side_ref, forward_ref, *refs
):
    parts = [core_ref.at[1], side_ref.at[0, 1], forward_ref.at[1, 1]]
    sources = refs[:count]
    gated_ref, grad_ref, grad_mixed_ref, bias_ref, shrink = refs[count : count + 5]
    raws = refs[count + 5 : count + (8 if tree else 6)]
    cots, sums, tall_sum, sems = refs[count + 5 + len(raws) :]
    narrow = lax.axis_index("narrow")
    rows_here, quarter = core_ref.shape[1:3]
    tokens = rows_here * ROW

    if tree:
        fetch_weights(sources, [(0, k * D, D, shrink, 192, 96, k * 32, sems.at[0]) for k in range(3)], tree)
    else:
        pltpu.make_async_copy(sources[0], shrink, sems.at[0]).start()
    for r in range(rows_here):
        for j in range(members):
            source = own_ref.at[narrow * rows_here + r] if j == 0 else parts[j - 1].at[r]
            place = run(r * ROW + (narrow ^ j) * quarter, quarter)
            pltpu.make_async_copy(source, cots.at[place, :], sems.at[1]).start()
    sums[...] = jnp.zeros_like(sums)
    wait_weights([(shrink, sems.at[0]), (cots, sems.at[1])])

    def do_channels(k, carry):
        channels = run(k * WIDTH, WIDTH)
        grad_gated = dot(cots[...], shrink[channels, :], ((1,), (1,)))
        for p in range(0, tokens, CHUNK):
            r, here = p // ROW, slice(p % ROW, p % ROW + CHUNK)
            grads = grad_gated[p : p + CHUNK]
            content = content_ref[r, here, channels].astype(F32)
            mixed = mixed_ref[r, here, channels].astype(F32)
            slope = slope_ref[r, here, channels].astype(F32)
            gated_ref[r, here, channels] = (content * mixed).astype(BF16)
            grad_ref[r, here, channels] = (grads * mixed * slope).astype(BF16)
            grad_mixed = (grads * content).astype(BF16)
            grad_mixed_ref[r, here, channels] = grad_mixed
            total = grad_mixed.astype(F32)
            sums[p : p + CHUNK, :] += total[:, :LANES] + total[:, LANES:]
        tall_sum[channels, :] = dot(gated_ref[:, :, channels].reshape(tokens, WIDTH), cots[...], ((0,), (0,)))
        return carry

    lax.fori_loop(0, HALF // WIDTH, do_channels, 0)
    for r in range(rows_here):
        _, live = doc_mask(0, ROW, lens_ref, narrow * rows_here + r)
        part = jnp.where(live, sums[r * ROW : (r + 1) * ROW, :], 0.0)
        bias_ref[...] = part if r == 0 else bias_ref[...] + part
    if tree:
        for j in range(3):
            emit_blocks("y", reader(tall_sum, 192, 48, j * BLOCK, slice(0, D)), D, j * D, *raws)
    else:
        raws[0][...] = tall_sum[...]


def content_sum_kernel(tree, normed_ref, grad_ref, *refs):
    raws, normed_turned, wide_sum = refs[:-2], refs[-2], refs[-1]
    tokens = normed_ref.shape[0] * normed_ref.shape[1]
    normed_turned[...] = normed_ref[...].reshape(tokens, D).T
    for c in range(0, HALF, D):
        wide_sum[...] = dot(normed_turned[...], grad_ref[:, :, c : c + D].reshape(tokens, D))
        if tree:
            emit_blocks("x", reader(wide_sum, 64, 16, 0, slice(0, D)), D, c, *raws)
        else:
            raws[0][:, c : c + D] = wide_sum[...]


def spatial_sum_kernel(lens_ref, grad_mixed_ref, gate_ref, square_ref):
    rows_here = grad_mixed_ref.shape[0]
    narrow = lax.axis_index("narrow")
    for row in range(rows_here):
        same, _ = doc_mask(0, ROW, lens_ref, narrow * rows_here + row)
        products = jnp.where(same, dot(grad_mixed_ref[row], gate_ref[row], ((1,), (1,))), 0.0)
        square_ref[...] = products if row == 0 else square_ref[...] + products


def gate_back_kernel(
    lens_ref, grad_mixed_ref, gate_ref, slope_ref, rstd_ref, spatial_ref, gains_ref, bias_ref,
    grad_ref, vectors_ref, turned, grad_gate, first_sums, second_sums, second, inverse,
):
    rows_here = grad_mixed_ref.shape[0]
    narrow = lax.axis_index("narrow")
    turned[...] = spatial_ref[...].T
    second[...] = jnp.zeros_like(second)
    inverse[...] = 1.0 / gains_ref[:, D:]

    def do_row(row, carry):
        same, _ = doc_mask(0, ROW, lens_ref, narrow * rows_here + row)
        masked = jnp.where(same, turned[...], jnp.zeros((), BF16))
        for c in range(0, HALF, WIDTH):
            grads_all = dot(masked, grad_mixed_ref[row, :, c : c + WIDTH])
            vector = jnp.zeros((8, WIDTH), F32)
            for p in range(0, ROW, CHUNK):
                here = slice(p, p + CHUNK)
                low = grads_all[here].astype(BF16)
                grad_gate[here, c : c + WIDTH] = low
                grads = low.astype(F32)
                products = grads * gate_ref[row, here, c : c + WIDTH].astype(F32)
                vector = vector + jnp.sum(products.reshape(CHUNK // 8, 8, WIDTH), axis=0)
                scaled = grads * gains_ref[0:1, D + c : D + c + WIDTH]
                first = scaled[:, :LANES] + scaled[:, LANES:]
                other = products[:, :LANES] + products[:, LANES:]
                first_sums[here, :] = first if c == 0 else first_sums[here, :] + first
                second_sums[here, :] = other if c == 0 else second_sums[here, :] + other
            second[:, c : c + WIDTH] += vector
        for p in range(0, ROW, CHUNK):
            here = slice(p, p + CHUNK)
            scale = rstd_ref[row, here, 0:1]
            first_mean = jnp.sum(first_sums[here, :], axis=1, keepdims=True) * (1.0 / HALF) * scale
            second_mean = jnp.sum(second_sums[here, :], axis=1, keepdims=True) * (1.0 / HALF) * scale
            for c in range(0, HALF, LANES):
                place = slice(c, c + LANES)
                scaled = grad_gate[here, place].astype(F32) * gains_ref[0:1, D + c : D + c + LANES] * scale
                vhat = gate_ref[row, here, place].astype(F32) * inverse[0:1, place]
                slope = slope_ref[row, here, place].astype(F32)
                grad_ref[row, here, place] = ((scaled - first_mean - vhat * second_mean) * slope).astype(BF16)
        return carry

    lax.fori_loop(0, rows_here, do_row, 0)
    vectors_ref[...] = jnp.zeros_like(vectors_ref)
    diagonal = lax.broadcasted_iota(jnp.int32, (64, 128), 0) == lax.broadcasted_iota(jnp.int32, (64, 128), 1)
    for owner in range(8):
        for k in range(2 if owner >= 2 else 0):
            c = (owner - 2) * 256 + k * 128
            total = jnp.sum(second[:, c : c + 128], axis=0, keepdims=True)
            vectors_ref[owner, k : k + 1, :] = total * inverse[0:1, c : c + 128]
        column = jnp.sum(bias_ref[owner * 64 : (owner + 1) * 64, :], axis=1, keepdims=True)
        vectors_ref[owner, 2:3, :] = jnp.sum(jnp.where(diagonal, column, 0.0), axis=0, keepdims=True)


def gate_sum_kernel(tree, normed_ref, grad_ref, square_ref, vectors_ref, *refs):
    raws, normed_turned, wide_sum = refs[:-2], refs[-2], refs[-1]
    tokens = normed_ref.shape[0] * normed_ref.shape[1]
    rest = HALF - SPLIT
    normed_turned[...] = normed_ref[...].reshape(tokens, D).T
    if tree:
        emit_blocks("y", reader(square_ref, 64, 16, 0, slice(0, ROW)), ROW, rest, *raws[3:])
        emit_blocks("y", lambda owner, member: vectors_ref[owner], VECTOR_LANES, rest + ROW, *raws[3:])
    else:
        raws[1][...] = square_ref[...]
        raws[2][...] = vectors_ref[...]
    for c in range(0, HALF, D):
        wide_sum[...] = dot(normed_turned[...], grad_ref[:, :, c : c + D].reshape(tokens, D))
        if not tree:
            raws[0][:, c : c + D] = wide_sum[...]
        elif c < SPLIT:
            emit_blocks("x", reader(wide_sum, 64, 16, 0, slice(0, D)), D, c, *raws[:3])
        else:
            emit_blocks("y", reader(wide_sum, 64, 16, 0, slice(0, D)), D, c - SPLIT, *raws[3:])


def layer_kernel(gated_ref, shrink, own_ref, core_ref, pair_ref, total):
    members, rows_here, quarter = total.shape[:3]
    narrow = lax.axis_index("narrow")
    for row in range(rows_here):
        added = dot(gated_ref[row], shrink[...])
        for member in range(members):
            total[member ^ narrow, row] = added[member * quarter : (member + 1) * quarter].astype(BF16)
    own_ref[...] = total[0]
    core_ref[...] = total[1]
    pair_ref[0] = total[2]
    pair_ref[1] = total[3]


def back_kernel(
    gate_grad_ref, content_grad_ref, gate_weight, weight, xhat_ref, scale_ref, gains_ref, layer_core, layer_pair,
    own_ref, core_ref, pair_ref, total,
):
    members, rows_here, quarter = total.shape[:3]
    narrow = lax.axis_index("narrow")
    for row in range(rows_here):
        grad_normed = dot(gate_grad_ref[row], gate_weight[...], ((1,), (1,))) + dot(
            content_grad_ref[row], weight[...], ((1,), (1,))
        )
        for member in range(members):
            here = slice(member * quarter, (member + 1) * quarter)
            xhat = xhat_ref[row, here, :].astype(F32)
            scaled = grad_normed[here] * gains_ref[0:1, :D]
            first_mean = jnp.mean(scaled, axis=1, keepdims=True)
            second_mean = jnp.mean(scaled * xhat, axis=1, keepdims=True)
            scale = scale_ref[row, here, 0:1]
            total[member ^ narrow, row] = ((scaled - first_mean - xhat * second_mean) * scale).astype(BF16)
    own_ref[...] = total[0]
    core_ref[0] = total[1]
    core_ref[1] = layer_core[...]
    for j in range(2):
        pair_ref[j, 0] = total[2 + j]
        pair_ref[j, 1] = layer_pair[j]


def give_kernel(
    cots_ref, acts_ref, grad_own, layer_own, core_ref, side_ref, forward_ref, grad_out, layer_out, grads, layers, sems
):
    rows_here = grad_own.shape[0]
    narrow = lax.axis_index("narrow")
    stores = []
    for kind, (base, own, total, out) in enumerate(
        ((cots_ref, grad_own, grads, grad_out), (acts_ref, layer_own, layers, layer_out))
    ):
        parts = [own, core_ref.at[kind], side_ref.at[0, kind], forward_ref.at[1, kind]]
        for j, part in enumerate(parts):
            rows = pl.ds((narrow ^ j) * rows_here, rows_here)
            total[j] = (base[rows].astype(F32) + part[...].astype(F32)).astype(total.dtype)
            stores.append(pltpu.make_async_copy(total.at[j], out.at[rows], sems.at[kind, j]))
            stores[-1].start()
    for store in stores:
        store.wait()


def sum_three(near_ref, came_ref, far_ref, half, columns):
    values = near_ref[half, :, :, columns].astype(F32) + came_ref[0, half, :, :, columns].astype(F32)
    return values + far_ref[half, :, :, columns].astype(F32)


def side_kernel(*refs):
    inputs, outputs = refs[:12], refs[12:]
    for i, out_ref in enumerate(outputs):
        first = 0
        for group in range(2):
            near, came, far = inputs[6 * i + 3 * group : 6 * i + 3 * group + 3]
            width = near.shape[3]
            for c in range(0, width, LANES):
                out_ref[:, :, first + c : first + c + LANES] = sum_three(
                    near, came, far, 1, slice(c, c + LANES)
                ).astype(BF16)
            first += width


def fold_kernel(*refs):
    inputs, sides, outputs = refs[:12], refs[12:14], refs[14:]
    base = 0
    for i in range(2):
        first = 0
        for group in range(2):
            near, came, far = inputs[6 * i + 3 * group : 6 * i + 3 * group + 3]
            width = near.shape[3]
            for c in range(0, width, LANES):
                place = slice(first + c, first + c + LANES)
                total = sum_three(near, came, far, 0, slice(c, c + LANES)) + sides[i][:, :, place].astype(F32)
                there = slice(base + first + c, base + first + c + LANES)
                outputs[0][:, there] = total[0]
                for step in range(1, 4):
                    outputs[step][:, there] = total[step].astype(BF16)
            first += width
        base += first


def norm_kernel(mine_ref, one_ref, two_ref, three_ref, weight_ref, gains_ref, low_ref, message_ref):
    wide, narrow = lax.axis_index("wide"), lax.axis_index("narrow")
    columns = mine_ref.shape[1]
    squares = jnp.zeros((BLOCK, LANES), F32)
    products = jnp.zeros((BLOCK, LANES), F32)
    here = run(narrow * BLOCK, BLOCK)
    for c in range(0, columns, LANES):
        place = slice(c, c + LANES)
        total = mine_ref[:, place]
        for ref in (one_ref, two_ref, three_ref):
            total = total + ref[:, place].astype(F32)
        low = total.astype(BF16)
        low_ref[:, place] = low
        value = low.astype(F32)
        square = value * value
        squares = squares + (square if c < columns - LANES else jnp.where(narrow == 0, square, 0.0))
        at = expand_column(c)
        if at is not None:
            weight = weight_ref[here, at : at + LANES].astype(BF16).astype(F32)
            products = products + value * weight
    first = wide * 64 + narrow * BLOCK
    lanes = lax.broadcasted_iota(jnp.int32, (BLOCK, D), 1)
    diagonal = lanes == lax.broadcasted_iota(jnp.int32, (BLOCK, D), 0) + first
    gain = jnp.sum(jnp.where(diagonal, gains_ref[0:1, :D], 0.0), axis=1, keepdims=True)
    first_raw = jnp.sum(products, axis=1, keepdims=True) / gain
    total = jnp.sum(squares) + jnp.sum(first_raw * first_raw)
    places = jnp.sum(jnp.where(diagonal, first_raw, 0.0), axis=0, keepdims=True)
    message_ref[...] = jnp.full(message_ref.shape, total, F32)
    for k in range(D // LANES):
        message_ref[k : k + 1, :] = places[:, k * LANES : (k + 1) * LANES]


def expand_column(c):
    right = HALF + SPLIT
    turn = right + HALF
    if c < right:
        return c
    if turn <= c < turn + HALF - SPLIT:
        return c - HALF
    return None


def adam_kernel(message_ref, own_ref, side_ref, other_ref, *refs):
    states, vectors, outputs, vector_outputs, norm_ref = refs[:12], refs[12:20], refs[20:35], refs[35:45], refs[45]
    results, blocks, sem = refs[46:61], refs[61], refs[62]
    wide, narrow = lax.axis_index("wide"), lax.axis_index("narrow")
    norm = jnp.sqrt(message_ref[4:5, :])
    norm_ref[0, 0] = jnp.max(norm)
    clip = CLIP_LIMIT / jnp.maximum(norm, CLIP_LIMIT)
    right = HALF + SPLIT
    turn = right + HALF
    blocks[narrow] = own_ref[...]
    blocks[narrow ^ 1] = other_ref[0]
    blocks[narrow ^ 2] = side_ref[...]
    blocks[narrow ^ 3] = other_ref[1]

    def update(which, gradient, rows, place):
        weight, momentum, variance, average = [ref[rows, place] for ref in states[4 * which : 4 * which + 4]]
        updates = adam_update(
            weight, gradient.astype(F32), momentum, variance, average, clip, RATE_MATRIX, DECAY_MATRIX
        )
        for ref, value in zip(results[5 * which : 5 * which + 5], updates):
            ref[rows, place] = value

    def do_member(member, carry):
        thin = run(member * BLOCK, BLOCK)
        for c in range(0, turn + HALF - SPLIT + ROW, LANES):
            gradient = blocks[member, :, c : c + LANES]
            at = expand_column(c)
            if at is not None:
                update(0, gradient, thin, slice(at, at + LANES))
            elif c < turn:
                k, at = (c - right) // D, (c - right) % D
                update(1, gradient, run(member * 48 + k * BLOCK, BLOCK), slice(at, at + LANES))
            else:
                at = c - turn - (HALF - SPLIT)
                update(2, gradient, thin, slice(at, at + LANES))
        for i in range(15):
            rows = run(member * 48, 48) if 5 <= i < 10 else thin
            pltpu.make_async_copy(results[i].at[rows, :], outputs[i].at[rows, :], sem.at[i]).start()
        return carry

    lax.fori_loop(0, 4, do_member, 0)
    own = blocks[0, :, turn + HALF - SPLIT + ROW :].astype(F32)
    gains = jnp.where(wide == 0, message_ref[0:2, :], jnp.where(wide == 1, message_ref[2:4, :], own[0:2, :]))
    for which, gradient in ((0, gains), (1, own[2:3, :64])):
        weight, momentum, variance, average = [ref[...] for ref in vectors[4 * which : 4 * which + 4]]
        updates = adam_update(
            weight, gradient, momentum, variance, average, clip[:, : gradient.shape[1]], RATE_VECTOR, 0.0
        )
        for ref, value in zip(vector_outputs[5 * which : 5 * which + 5], updates):
            ref[...] = value
    for i in range(15):
        pltpu.make_async_copy(results[i], outputs[i], sem.at[i]).wait()


def call_kernel(kernel, name, args, in_specs, out_types, scratch, flops, limit=VMEM_LIMIT):
    vmem = pl.BlockSpec(memory_space=pltpu.VMEM)
    specs = [kind[1] if isinstance(kind, tuple) else vmem for kind in out_types]
    types = [
        kind[0] if isinstance(kind, tuple) else pltpu.VMEM(kind.shape, kind.dtype) for kind in out_types
    ]
    in_specs = [vmem if spec is None else spec for spec in in_specs]
    args = [
        pltpu.with_memory_space_constraint(value, pltpu.HBM) if spec.memory_space == pltpu.HBM else value
        for value, spec in zip(args, in_specs)
    ]
    results = pl.pallas_call(
        kernel,
        name=name,
        in_specs=in_specs,
        out_specs=specs,
        out_shape=types,
        scratch_shapes=scratch,
        compiler_params=pltpu.CompilerParams(vmem_limit_bytes=limit),
        cost_estimate=pl.CostEstimate(flops=int(flops), bytes_accessed=int(flops / 500), transcendentals=0),
    )(*args)
    return list(results)


def swap_with(value, axis, size, bit):
    return lax.ppermute(value, axis, [(i, i ^ bit) for i in range(size)])


def after(value, *others):
    return lax.optimization_barrier((value,) + others)[0]


def sum_core(keep_far, came):
    return (keep_far.astype(F32) + came[1].astype(F32)).astype(BF16)


def adam_update(weight, gradient, momentum, variance, average, clip_scale, step_rate, decay_rate):
    ema_rate = min(EMA_DECAY, (1.0 + STEP) / (10.0 + STEP))
    clipped = clip_scale * gradient
    moment = BETA_FIRST * momentum + (1.0 - BETA_FIRST) * clipped
    square = BETA_SECOND * variance + (1.0 - BETA_SECOND) * clipped * clipped
    first_hat = moment / (1.0 - BETA_FIRST**STEP)
    second_hat = square / (1.0 - BETA_SECOND**STEP)
    updated = weight - step_rate * (
        first_hat / (jnp.sqrt(second_hat) + ADAM_EPS) + decay_rate * weight
    )
    smoothed = ema_rate * average + (1.0 - ema_rate) * updated
    return (clipped, moment, square, updated, smoothed)


def on_device(
    activations,
    cotangent,
    doc_lengths,
    expand_weight,
    expand_momentum,
    expand_variance,
    expand_average,
    shrink_weight,
    shrink_momentum,
    shrink_variance,
    shrink_average,
    spatial_weight,
    spatial_momentum,
    spatial_variance,
    spatial_average,
    norm_gains,
    gains_momentum,
    gains_variance,
    gains_average,
    spatial_bias,
    bias_momentum,
    bias_variance,
    bias_average,
):
    narrow_size, wide_size = lax.axis_size("narrow"), lax.axis_size("wide")
    wide, narrow = lax.axis_index("wide"), lax.axis_index("narrow")
    group_rows, quarter = activations.shape[0], activations.shape[1]
    rows = group_rows // narrow_size
    tokens = rows * ROW
    tree = (wide_size, narrow_size) == (8, 4)
    smem = pl.BlockSpec(memory_space=pltpu.SMEM)
    anywhere = pl.BlockSpec(memory_space=pl.ANY)
    stored = pl.BlockSpec(memory_space=pltpu.HBM)
    shape = jax.ShapeDtypeStruct
    dma = pltpu.SemaphoreType.DMA
    part = shape((rows, quarter, D), BF16)
    product = 2 * tokens * HALF * D
    cross_x = lambda value: swap_with(value, "wide", wide_size, 1)
    cross_y = lambda value: swap_with(value, "narrow", narrow_size, 2)
    cross_core = lambda value: swap_with(value, "narrow", narrow_size, 1)

    def trade(core_part, pair):
        side = cross_y(pair)
        return [cross_core(core_part), side, cross_core(side)]

    def stack(values):
        kind = shape((len(values), *values[0].shape), values[0].dtype)
        return call_kernel(stack_kernel, "stack", values, [None] * len(values), [kind], [], product // 64)[0]

    def add(*values):
        kind = shape(values[0].shape, values[0].dtype)
        return call_kernel(add_kernel, "add", values, [None] * len(values), [kind], [], product // 64)[0]

    pair = shape((2, *part.shape), BF16)

    def cut(acts, cots):
        return call_kernel(
            cut_kernel,
            "cut",
            [acts, cots],
            [stored] * 2,
            [(pair, stored), (shape((2, *pair.shape), BF16), stored)],
            [dma((6,))],
            product // 64,
        )

    if tree:
        first_own = call_kernel(
            pack_first_kernel,
            "pack_first",
            [expand_weight, spatial_weight, norm_gains.reshape(2, LANES), spatial_bias.reshape(1, 64)],
            [stored] * 4,
            [shape((32, HALF + ROW + VECTOR_LANES), BF16)],
            [pltpu.VMEM((32, HALF), F32), pltpu.VMEM((32, ROW), F32), pltpu.VMEM((2, LANES), F32)]
            + [pltpu.VMEM((1, 64), F32), dma((4,))],
            product // 64,
        )[0]
        over_z = lambda own: [swap_with(own, "wide", wide_size, 2 * s) for s in range(1, 4)]
        came_z = over_z(first_own)
        core_cut, pair_cut = cut(after(activations, first_own), cotangent)
        side_came = cross_y(pair_cut)
        expand_own, shrink_own = call_kernel(
            pack_second_kernel,
            "pack_second",
            [expand_weight, shrink_weight],
            [stored, stored],
            [shape((32, HALF), BF16)] * 2,
            [pltpu.VMEM((32, HALF), F32), pltpu.VMEM((96, D), F32), dma((2,))],
            product // 64,
        )
        *came_z, core_came, _, expand_own = lax.optimization_barrier(
            (*came_z, cross_core(core_cut), pair_cut, expand_own)
        )
        first_near = stack([first_own, *came_z])
        first_across = cross_x(first_near)
        expand_own = after(expand_own, first_near)
        *came_z, side_came = lax.optimization_barrier((*over_z(expand_own), side_came))
        expand_near = stack([expand_own, *came_z])
        expand_across = cross_x(after(expand_near, first_across))
        shrink_own = after(shrink_own, expand_near)
        shrink_came = over_z(shrink_own)
        near_core = cross_core(after(first_near, expand_near))
        across_core = cross_core(after(first_across, expand_near))
        forward_came = cross_core(after(side_came, expand_near))
        first_pieces = [after(first_near, expand_near), first_across, near_core, across_core]
        small_pieces = first_pieces[:2]
        near_other = cross_core(expand_near)
        count = len(PIECES)
    else:
        gather = lambda value: lax.all_gather(value.astype(BF16), "wide", axis=0, tiled=True)
        expand_low = gather(expand_weight)
        gains_low, bias_low = gather(norm_gains), gather(spatial_bias)
        small = jnp.concatenate(
            [
                gains_low.reshape(8, 2, 128),
                jnp.pad(bias_low.reshape(8, 1, 64), ((0, 0), (0, 0), (0, 64))),
                jnp.zeros((8, 13, 128), BF16),
            ],
            axis=1,
        )
        first_pieces = [expand_low[:, HALF:], gather(spatial_weight)]
        small_pieces = [small, small]
        expand_pieces, shrink_pieces = [expand_low[:, :HALF]], [gather(shrink_weight)]
        core_came, side_came, forward_came = trade(*cut(activations, cotangent))
        count = 2

    low_d, low_half = shape((rows, ROW, D), BF16), shape((rows, ROW, HALF), BF16)
    thin = shape((rows, ROW, 128), F32)
    weight_type = shape((D, HALF), BF16)

    normed, xhat, scale, gate_normed, slope, rstd, mixed, spatial_low, gains, gate_weight = call_kernel(
        functools.partial(gating_kernel, tree, count, narrow_size),
        "gating",
        [doc_lengths, activations, core_came, side_came, forward_came] + list(first_pieces) + list(small_pieces),
        [smem, stored] + [anywhere] * (narrow_size - 1 + count + 2),
        [low_d, low_d, thin, low_half, low_half, thin, low_half]
        + [shape((ROW, ROW), BF16), shape((8, D + HALF), F32), weight_type],
        [
            pltpu.VMEM((8, BLOCK, 128), BF16),
            pltpu.VMEM((narrow_size, *part.shape), BF16),
            pltpu.VMEM((ROW, HALF), F32),
            pltpu.VMEM((ROW, 128), F32),
            pltpu.VMEM((ROW, 128), F32),
            dma((4,)),
        ],
        product // 64,
    )

    if tree:
        *shrink_came, expand_across, _ = lax.optimization_barrier((*shrink_came, expand_across, normed))
        shrink_near = stack([shrink_own, *shrink_came])
        shrink_across = cross_x(shrink_near)
        expand_pieces = [expand_near, expand_across, near_other, cross_core(expand_across)]
    content, content_slope, content_weight = call_kernel(
        functools.partial(content_up_kernel, tree),
        "content_up",
        [normed, *expand_pieces],
        [None] + [anywhere] * len(expand_pieces),
        [low_half, low_half, weight_type],
        [dma(())],
        product // 64,
    )
    if tree:
        shrink_across, _ = lax.optimization_barrier((shrink_across, content))
        shrink_pieces = [shrink_near, shrink_across, cross_core(shrink_near), cross_core(shrink_across)]

    def raw_outputs(column_list, plain):
        if tree:
            return [
                shape(size, BF16)
                for columns in column_list
                for size in ((2, 4, BLOCK, columns), (2, 4, BLOCK, columns), (2, 2, 4, BLOCK, columns))
            ]
        return [shape(size, F32) for size in plain]

    gated, content_grad, grad_mixed, bias_part, shrink_low, *shrink_raws = call_kernel(
        functools.partial(content_down_kernel, tree, len(shrink_pieces), narrow_size),
        "content_down",
        [doc_lengths, content, content_slope, mixed, cotangent, core_came, side_came, forward_came, *shrink_pieces],
        [smem, None, None, None, stored] + [anywhere] * (narrow_size - 1 + len(shrink_pieces)),
        [low_half, low_half, low_half, shape((ROW, 128), F32), shape((HALF, D), BF16)]
        + raw_outputs((HALF,), ((HALF, D),)),
        [
            pltpu.VMEM((tokens, D), BF16),
            pltpu.VMEM((tokens, 128), F32),
            pltpu.VMEM((HALF, D), F32),
            dma((2,)),
        ],
        product // 64,
    )
    if tree:
        came = {"shrink": cross_core(shrink_raws[2])}
    sum_scratch = [pltpu.VMEM((D, tokens), BF16), pltpu.VMEM((D, D), F32)]
    content_raws = call_kernel(
        functools.partial(content_sum_kernel, tree),
        "content_sum",
        [normed, content_grad],
        [None] * 2,
        raw_outputs((HALF,), ((D, HALF),)),
        sum_scratch,
        product // 64,
    )
    mixed_late = grad_mixed
    if tree:
        came["shrink"], content_raws[0] = lax.optimization_barrier((came["shrink"], content_raws[0]))
        came["content"] = cross_core(content_raws[2])
        far = {"shrink": sum_core(shrink_raws[1], came["shrink"])}
        came_far = {"shrink": cross_y(far["shrink"])}
        mixed_late = after(grad_mixed, far["shrink"])
    square_sum = call_kernel(
        spatial_sum_kernel,
        "spatial_sum",
        [doc_lengths, mixed_late, gate_normed],
        [smem, None, None],
        [shape((ROW, ROW), F32)],
        [],
        product // 64,
    )[0]
    if tree:
        came["content"], square_sum = lax.optimization_barrier((came["content"], square_sum))
        far["content"] = sum_core(content_raws[1], came["content"])
        came_far["content"] = cross_x(far["content"])
        mixed_late = after(grad_mixed, far["content"])

    gate_grad, vectors = call_kernel(
        gate_back_kernel,
        "gate_back",
        [doc_lengths, mixed_late, gate_normed, slope, rstd, spatial_low, gains, bias_part],
        [smem] + [None] * 7,
        [low_half, shape((8, BLOCK, 128), F32)],
        [
            pltpu.VMEM((ROW, ROW), BF16),
            pltpu.VMEM((ROW, HALF), BF16),
            pltpu.VMEM((ROW, 128), F32),
            pltpu.VMEM((ROW, 128), F32),
            pltpu.VMEM((8, HALF), F32),
            pltpu.VMEM((8, HALF), F32),
        ],
        product // 64,
    )
    normed_late = normed
    if tree:
        came_far["shrink"], normed_late = lax.optimization_barrier((came_far["shrink"], normed))
    second_raws = call_kernel(
        functools.partial(gate_sum_kernel, tree),
        "gate_sum",
        [normed_late, gate_grad, square_sum, vectors],
        [None] * 4,
        raw_outputs((SPLIT, HALF - SPLIT + ROW + VECTOR_LANES), ((D, HALF), (ROW, ROW), (8, BLOCK, 128))),
        sum_scratch,
        product // 64,
    )
    gated_late = gated
    if tree:
        second_raws[2], second_raws[5], came_far["content"] = lax.optimization_barrier(
            (second_raws[2], second_raws[5], came_far["content"])
        )
        second_came = [cross_core(second_raws[i]) for i in (2, 5)]
        gated_late = after(gated, second_raws[0], came_far["content"])
    part_scratch = pltpu.VMEM((narrow_size, *part.shape), BF16)
    layer_own, layer_core, layer_pair = call_kernel(
        layer_kernel,
        "layer",
        [gated_late, shrink_low],
        [None] * 2,
        [part, part, pair],
        [part_scratch],
        product // 64,
    )
    grad_late = gate_grad
    if tree:
        *second_came, layer_own = lax.optimization_barrier((*second_came, layer_own))
        second_far = [sum_core(second_raws[1], second_came[0]), sum_core(second_raws[4], second_came[1])]
        second_came_far = [cross_x(second_far[0]), cross_y(second_far[1])]
        grad_late = after(gate_grad, *second_far)
    grad_own, core_back, pair_back = call_kernel(
        back_kernel,
        "back",
        [grad_late, content_grad, gate_weight, content_weight, xhat, scale, gains, layer_core, layer_pair],
        [None] * 9,
        [part, pair, shape((2, *pair.shape), BF16)],
        [part_scratch],
        product // 64,
    )

    def give(cots_base, acts_base, returned):
        whole = (group_rows, quarter, D)
        return call_kernel(
            give_kernel,
            "give",
            [cots_base, acts_base, grad_own, layer_own, *returned],
            [None] * 7,
            [(shape(whole, F32), stored), (shape(whole, BF16), stored)],
            [
                pltpu.VMEM((narrow_size, *part.shape), F32),
                pltpu.VMEM((narrow_size, *part.shape), BF16),
                dma((2, narrow_size)),
            ],
            product // 64,
        )

    if tree:
        columns = HALF + HALF + SPLIT + (HALF - SPLIT) + ROW + VECTOR_LANES
        half_columns = HALF + SPLIT
        (*all_far, grad_own) = lax.optimization_barrier(
            (came_far["content"], second_came_far[0], came_far["shrink"], second_came_far[1], grad_own)
        )
        terms = []
        for near, near_came, far_came in zip(
            (content_raws[0], second_raws[0], shrink_raws[0], second_raws[3]),
            (came["content"], second_came[0], came["shrink"], second_came[1]),
            all_far,
        ):
            terms += [near, near_came, far_came]
        sides = call_kernel(
            side_kernel,
            "side",
            terms,
            [None] * 12,
            [shape((4, BLOCK, half_columns), BF16), shape((4, BLOCK, columns - half_columns), BF16)],
            [],
            product // 64,
        )
        came_side = [cross_y(sides[0]), cross_x(sides[1])]
        *came_side, core_back = lax.optimization_barrier((*came_side, cross_core(core_back)))
        mine, *sent = call_kernel(
            fold_kernel,
            "fold",
            terms + came_side,
            [None] * 14,
            [shape((BLOCK, columns), F32)] + [shape((BLOCK, columns), BF16)] * 3,
            [],
            product // 64,
        )
        came_z = [swap_with(sent[s - 1], "wide", wide_size, 2 * s) for s in range(1, 4)]
        matrices = [expand_weight, expand_momentum, expand_variance, expand_average]
        matrices += [shrink_weight, shrink_momentum, shrink_variance, shrink_average]
        matrices += [spatial_weight, spatial_momentum, spatial_variance, spatial_average]
        fetched = [*matrices, cotangent, activations]
        states = call_kernel(
            fetch_kernel,
            "fetch",
            list(lax.optimization_barrier((*fetched, sent[0]))[:14]),
            [stored] * 14,
            [shape(value.shape, value.dtype) for value in fetched],
            [dma((14,))],
            product // 64,
        )
        states, bases = states[:12], states[12:]
        side_back = cross_y(after(pair_back, sent[0]))
        *came_z, first_state = lax.optimization_barrier((*came_z, states[0]))
        low, message = call_kernel(
            norm_kernel,
            "norm",
            [mine, *came_z, first_state, gains],
            [None] * 6,
            [shape((BLOCK, columns), BF16), shape((8, LANES), F32)],
            [],
            product // 64,
        )
        side = cross_y(low)
        message = add(message, cross_core(message))
        message = add(message, cross_x(message))
        *arrived, side, side_back = lax.optimization_barrier((*over_z(message), side, side_back))
        message = add(message, *arrived)
        other = cross_core(stack([low, side]))
        returned = [core_back, side_back, cross_core(side_back)]
        input_grad, layer_out = give(*bases, returned)
        arrived, layer_out, input_grad = lax.optimization_barrier((cross_y(message), layer_out, input_grad))
        message = add(message, arrived)
        as_rows = lambda value: value.reshape(-1, min(value.shape[0], LANES))
        vector_states = [norm_gains, gains_momentum, gains_variance, gains_average]
        vector_states += [spatial_bias, bias_momentum, bias_variance, bias_average]
        vector_kinds = [shape((2, LANES), F32)] * 5 + [shape((1, 64), F32)] * 5
        *updates, norm_row = call_kernel(
            adam_kernel,
            "adam",
            [message, low, side, other, *states] + [as_rows(value) for value in vector_states],
            [None] * 24,
            [(shape(value.shape, F32), stored) for value in (matrices[0], matrices[4], matrices[8]) for _ in range(5)]
            + [(kind, pl.BlockSpec(memory_space=pltpu.VMEM)) for kind in vector_kinds]
            + [(shape((1, 1), F32), smem)],
            [pltpu.VMEM(value.shape, F32) for value in (matrices[0], matrices[4], matrices[8]) for _ in range(5)]
            + [pltpu.VMEM((4, BLOCK, columns), BF16), dma((15,))],
            product // 64,
        )
        grad_norm = norm_row[0, 0]
        results = [layer_out, input_grad, grad_norm, *updates[:15]]
        return tuple(results + [value.reshape(-1) for value in updates[15:]])

    returned = trade(core_back, pair_back)
    input_grad, layer_out = give(cotangent, activations, returned)
    gains_size, bias_size = norm_gains.shape[0], spatial_bias.shape[0]
    vectors = lax.psum(second_raws[2], ("narrow", "wide"))
    totals = lax.psum(
        (jnp.concatenate([content_raws[0], second_raws[0]], axis=1), shrink_raws[0], second_raws[1]), "narrow"
    )
    expand_shard, shrink_shard, spatial_shard = [
        lax.psum_scatter(total, "wide", scatter_dimension=0, tiled=True) for total in totals
    ]
    second_shard = lax.dynamic_slice_in_dim(vectors[:, :2].reshape(-1), wide * gains_size, gains_size)
    bias_shard = lax.dynamic_slice_in_dim(vectors[:, 2, :64].reshape(-1), wide * bias_size, bias_size)
    low_weight = expand_weight.astype(BF16).astype(F32)
    height = expand_weight.shape[0]
    first_gain = lax.dynamic_slice_in_dim(gains[0], wide * height, height)
    first_raw = jnp.sum(low_weight * expand_shard, axis=1) / first_gain
    squares = [expand_shard, shrink_shard, spatial_shard, second_shard, bias_shard, first_raw]
    square_total = lax.psum(sum(jnp.sum(value * value) for value in squares), "wide")
    first_all = lax.all_gather(first_raw, "wide", axis=0, tiled=True)
    first_all = jnp.concatenate([first_all, jnp.zeros((HALF,), F32)])
    gains_shard = second_shard + lax.dynamic_slice_in_dim(first_all, wide * gains_size, gains_size)
    grad_norm = jnp.sqrt(square_total)
    clip_scale = CLIP_LIMIT / jnp.maximum(grad_norm, CLIP_LIMIT)
    results = [layer_out, input_grad, grad_norm]
    for weight, shard, momentum, variance, average, rate, decay in (
        (expand_weight, expand_shard, expand_momentum, expand_variance, expand_average, RATE_MATRIX, DECAY_MATRIX),
        (shrink_weight, shrink_shard, shrink_momentum, shrink_variance, shrink_average, RATE_MATRIX, DECAY_MATRIX),
        (spatial_weight, spatial_shard, spatial_momentum, spatial_variance, spatial_average, RATE_MATRIX, DECAY_MATRIX),
        (norm_gains, gains_shard, gains_momentum, gains_variance, gains_average, RATE_VECTOR, 0.0),
        (spatial_bias, bias_shard, bias_momentum, bias_variance, bias_average, RATE_VECTOR, 0.0),
    ):
        results += adam_update(weight, shard, momentum, variance, average, clip_scale, rate, decay)
    return tuple(results)


def solution(mesh):
    tokens, matrix, vector = P("wide", "narrow", None), P("wide", None), P("wide")
    return jax.shard_map(
        on_device,
        mesh=mesh,
        in_specs=(tokens, tokens) + (matrix,) * 13 + (vector,) * 8,
        out_specs=(tokens, tokens, P()) + (matrix,) * 15 + (vector,) * 10,
        check_vma=False,
    )
```

```python
import functools

import jax
import jax.numpy as jnp
from jax import lax
from jax.experimental import pallas as pl
from jax.experimental.pallas import tpu as pltpu
from jax.sharding import PartitionSpec as P

D = 512
FF = 3072
ROW = 512
DOCS = 5
STEP = 10
HALF = 1536

LAYER_EPS = 1e-05
CLIP_LIMIT = 1.0
BETA_FIRST = 0.9
BETA_SECOND = 0.999
ADAM_EPS = 1e-08
RATE_MATRIX = 0.03
RATE_VECTOR = 0.2
DECAY_MATRIX = 0.1
EMA_DECAY = 0.9999

F32 = jnp.float32
BF16 = jnp.bfloat16
GELU_A = 0.7978845608028654
GELU_B = GELU_A * 0.044715
LANES = 128
CHUNK = 64
BLOCK = 16
VMEM_LIMIT = 16 * 1024 * 1024

PIECES = ((0, 0), (1, 0), (0, 1), (1, 1))
WIDTH = 256
SPLIT = 1024
VECTOR_LANES = 128


def gelu_gate(hidden):
    squares = hidden * hidden
    gate = 0.5 * jnp.tanh(hidden * (GELU_A + GELU_B * squares)) + 0.5
    return squares, gate


def gelu_slope(hidden, squares, gate):
    return gate * (1.0 + hidden * (1.0 - gate) * (2.0 * GELU_A + 6.0 * GELU_B * squares))


def doc_ids(places, lens_ref, row):
    bound = jnp.int32(0)
    ids = jnp.zeros(places.shape, jnp.int32)
    for k in range(DOCS - 1):
        bound = bound + lens_ref[row, k]
        ids = ids + (places >= bound).astype(jnp.int32)
    return ids


def doc_mask(start, rows, lens_ref, row):
    across = doc_ids(lax.broadcasted_iota(jnp.int32, (1, ROW), 1), lens_ref, row)
    down = doc_ids(lax.broadcasted_iota(jnp.int32, (rows, 1), 0) + start, lens_ref, row)
    live = down != DOCS - 1
    return jnp.where(live, down, -1) == across, live


def dot(left, right, dims=((1,), (0,))):
    return lax.dot_general(left, right, (dims, ((), ())), preferred_element_type=F32)


def run(start, size):
    return pl.ds(pl.multiple_of(start, size), size)


def fetch_weights(sources, moves, tree):
    if not tree:
        for source, (_, _, _, target, _, _, _, sem) in zip(sources, moves):
            pltpu.make_async_copy(source, target, sem).start()
        return
    wide, core = lax.axis_index("wide"), lax.axis_index("narrow") & 1
    for base, first, count, target, height, unit, shift, sem in moves:
        for i, (x_off, core_off) in enumerate(PIECES):
            for step in range(4):
                start = (wide ^ (2 * step + x_off)) * height + (core ^ core_off) * unit + shift
                pltpu.make_async_copy(
                    sources[base + i].at[step, :, pl.ds(first, count)], target.at[run(start, 32), :], sem
                ).start()


def wait_weights(targets):
    for target, sem in targets:
        pltpu.make_async_copy(target, target, sem).wait()


def cut_kernel(acts_ref, cots_ref, core_out, pair_out, sems):
    rows_here = core_out.shape[1]
    narrow = lax.axis_index("narrow")
    copies = []
    for i, ref in enumerate((acts_ref, cots_ref)):
        for j, target in ((1, core_out.at[i]), (2, pair_out.at[0, i]), (3, pair_out.at[1, i])):
            source = ref.at[pl.ds((narrow ^ j) * rows_here, rows_here)]
            copies.append(pltpu.make_async_copy(source, target, sems.at[len(copies)]))
    for copy in copies:
        copy.start()
    for copy in copies:
        copy.wait()


def pack_first_kernel(expand_ref, spatial_ref, gains_ref, bias_ref, out_ref, expand, spatial, gains, bias, sems):
    rows = run((lax.axis_index("narrow") & 1) * 32, 32)
    copies = [
        pltpu.make_async_copy(expand_ref.at[rows, pl.ds(HALF, HALF)], expand, sems.at[0]),
        pltpu.make_async_copy(spatial_ref.at[rows, :], spatial, sems.at[1]),
        pltpu.make_async_copy(gains_ref, gains, sems.at[2]),
        pltpu.make_async_copy(bias_ref, bias, sems.at[3]),
    ]
    for copy in copies:
        copy.start()
    for copy in copies:
        copy.wait()
    vectors = jnp.concatenate(
        [
            gains[...],
            jnp.concatenate([bias[...], jnp.zeros((1, LANES - 64), F32)], axis=1),
            jnp.zeros((29, LANES), F32),
        ],
        axis=0,
    )
    out_ref[:, HALF + ROW :] = vectors.astype(BF16)
    out_ref[:, :HALF] = expand[...].astype(BF16)
    out_ref[:, HALF : HALF + ROW] = spatial[...].astype(BF16)


def pack_second_kernel(expand_ref, shrink_ref, expand_out, shrink_out, expand, shrink, sems):
    core = lax.axis_index("narrow") & 1
    copies = [
        pltpu.make_async_copy(expand_ref.at[run(core * 32, 32), pl.ds(0, HALF)], expand, sems.at[0]),
        pltpu.make_async_copy(shrink_ref.at[run(core * 96, 32 * 3), :], shrink, sems.at[1]),
    ]
    for copy in copies:
        copy.start()
    for copy in copies:
        copy.wait()
    expand_out[...] = expand[...].astype(BF16)
    for k in range(3):
        shrink_out[:, k * D : (k + 1) * D] = shrink[k * 32 : (k + 1) * 32, :].astype(BF16)


def stack_kernel(*refs):
    for i, ref in enumerate(refs[:-1]):
        refs[-1][i] = ref[...]


def add_kernel(*refs):
    total = refs[0][...] + refs[1][...]
    if len(refs) == 5:
        total = total + (refs[2][...] + refs[3][...])
    refs[-1][...] = total


def fetch_kernel(*refs):
    count = (len(refs) - 1) // 2
    copies = [pltpu.make_async_copy(refs[i], refs[count + i], refs[-1].at[i]) for i in range(count)]
    for copy in copies:
        copy.start()
    for copy in copies:
        copy.wait()


def gating_kernel(tree, count, members, own_ref, core_ref, side_ref, forward_ref, *refs):
    parts = [core_ref.at[0], side_ref.at[0, 0], forward_ref.at[1, 0]]
    sources, small_sources = refs[:count], refs[count : count + 2]
    (
        normed_ref, xhat_ref, scale_ref, gate_ref, slope_ref, rstd_ref, spatial_ref, gains_ref, bias_col, weight,
        small, acts, active, sums, sems,
    ) = refs[count + 2 :]
    wide, narrow = lax.axis_index("wide"), lax.axis_index("narrow")
    rows_here, quarter = acts.shape[1:3]

    pltpu.make_async_copy(own_ref.at[pl.ds(narrow * rows_here, rows_here)], acts.at[narrow], sems.at[3]).start()
    for j, part in enumerate(parts):
        pltpu.make_async_copy(part, acts.at[narrow ^ (j + 1)], sems.at[3]).start()
    fetch_weights(
        sources,
        [
            (0, 0, HALF, weight, 64, 32, 0, sems.at[0]),
            (0, HALF, ROW, spatial_ref, 64, 32, 0, sems.at[1]),
        ],
        tree,
    )
    if tree:
        for x_off in range(2):
            for step in range(4):
                pltpu.make_async_copy(
                    small_sources[x_off].at[step, pl.ds(0, BLOCK), pl.ds(HALF + ROW, 128)],
                    small.at[wide ^ (2 * step + x_off)],
                    sems.at[2],
                ).start()
    else:
        pltpu.make_async_copy(small_sources[0], small, sems.at[2]).start()
    wait_weights([(weight, sems.at[0]), (spatial_ref, sems.at[1]), (small, sems.at[2]), (acts, sems.at[3])])
    diagonal = lax.broadcasted_iota(jnp.int32, (64, 128), 0) == lax.broadcasted_iota(jnp.int32, (64, 128), 1)
    for owner in range(8):
        values = small[owner].astype(F32)
        for k in range(2):
            gains_ref[:, owner * 256 + k * 128 : owner * 256 + (k + 1) * 128] = jnp.broadcast_to(
                values[k : k + 1, :], (8, 128)
            )
        column = jnp.sum(jnp.where(diagonal, values[2:3, :], 0.0), axis=1, keepdims=True)
        bias_col[owner * 64 : (owner + 1) * 64, :] = jnp.broadcast_to(column, (64, 128))

    def do_row(row, carry):
        for member in range(members):
            here = slice(member * quarter, (member + 1) * quarter)
            values = acts[member, row].astype(F32)
            shifted = values - jnp.mean(values, axis=1, keepdims=True)
            scale = lax.rsqrt(jnp.mean(shifted * shifted, axis=1, keepdims=True) + LAYER_EPS)
            xhat = shifted * scale
            scale_ref[row, here, :] = jnp.broadcast_to(scale, (quarter, 128))
            xhat_ref[row, here, :] = xhat.astype(BF16)
            normed_ref[row, here, :] = (xhat * gains_ref[0:1, :D]).astype(BF16)

        normed = normed_ref[row]
        for c in range(0, HALF, WIDTH):
            hidden = dot(normed, weight[:, c : c + WIDTH])
            for p in range(0, ROW, CHUNK):
                here = slice(p, p + CHUNK)
                values = hidden[here]
                squares, gate = gelu_gate(values)
                slope_ref[row, here, c : c + WIDTH] = gelu_slope(values, squares, gate).astype(BF16)
                result = values * gate
                active[here, c : c + WIDTH] = result
                total = result[:, :LANES] + result[:, LANES:]
                sums[here, :] = total if c == 0 else sums[here, :] + total
        for p in range(0, ROW, CHUNK):
            here = slice(p, p + CHUNK)
            centre = jnp.sum(sums[here, :], axis=1, keepdims=True) * (1.0 / HALF)
            total = jnp.zeros((CHUNK, LANES), F32)
            for c in range(0, HALF, LANES):
                shifted = active[here, c : c + LANES] - centre
                total = total + shifted * shifted
            scale = lax.rsqrt(jnp.sum(total, axis=1, keepdims=True) * (1.0 / HALF) + LAYER_EPS)
            rstd_ref[row, here, :] = jnp.broadcast_to(scale, (CHUNK, 128))
            for c in range(0, HALF, LANES):
                vhat = (active[here, c : c + LANES] - centre) * scale
                gate_ref[row, here, c : c + LANES] = (vhat * gains_ref[0:1, D + c : D + c + LANES]).astype(BF16)

        return carry

    lax.fori_loop(0, rows_here, do_row, 0)


def mixing_kernel(lens_ref, spatial_ref, gate_ref, bias_col, mixed_ref):
    rows_here = gate_ref.shape[0]
    narrow = lax.axis_index("narrow")
    for row in range(rows_here):
        same, live = doc_mask(0, ROW, lens_ref, narrow * rows_here + row)
        masked = jnp.where(same, spatial_ref[...], jnp.zeros((), BF16))
        bias = jnp.where(live, bias_col[:, 0:1], 0.0)
        for c in range(0, HALF, D):
            mixed_ref[row, :, c : c + D] = (dot(masked, gate_ref[row, :, c : c + D]) + bias).astype(BF16)


def emit_blocks(order, read, columns, first, keep_near, keep_far, send):
    wide, narrow = lax.axis_index("wide"), lax.axis_index("narrow")
    for core in range(2):
        for one in range(2):
            for two in range(2):
                for step in range(4):
                    x_off, y_off = (one, two) if order == "x" else (two, one)
                    values = read(wide ^ (2 * step + x_off), narrow ^ (2 * y_off + core)).astype(BF16)
                    place = pl.ds(first, columns)
                    if core == 1:
                        send[one, two, step, :, place] = values
                    elif one == 1:
                        keep_far[two, step, :, place] = values
                    else:
                        keep_near[two, step, :, place] = values


def reader(matrix, height, part, shift, columns):
    def read(owner, member):
        return matrix[run(owner * height + member * part + shift, BLOCK), columns]

    return read


def content_up_kernel(tree, normed_ref, *refs):
    sources, (content_ref, slope_ref, weight, sem) = refs[:-4], refs[-4:]
    tokens = normed_ref.shape[0] * normed_ref.shape[1]
    if tree:
        fetch_weights(sources, [(0, 0, HALF, weight, 64, 32, 0, sem)], tree)
    else:
        pltpu.make_async_copy(sources[0], weight, sem).start()
    wait_weights([(weight, sem)])

    def do_channels(k, carry):
        channels = run(k * WIDTH, WIDTH)
        hidden = dot(normed_ref[...].reshape(tokens, D), weight[:, channels])
        for p in range(0, tokens, CHUNK):
            r, here = p // ROW, slice(p % ROW, p % ROW + CHUNK)
            values = hidden[p : p + CHUNK]
            squares, gate = gelu_gate(values)
            content_ref[r, here, channels] = (values * gate).astype(BF16)
            slope_ref[r, here, channels] = gelu_slope(values, squares, gate).astype(BF16)
        return carry

    lax.fori_loop(0, HALF // WIDTH, do_channels, 0)


def content_down_kernel(
    tree, count, members, lens_ref, content_ref, slope_ref, mixed_ref, own_ref, core_ref, side_ref, forward_ref, *refs
):
    parts = [core_ref.at[1], side_ref.at[0, 1], forward_ref.at[1, 1]]
    sources = refs[:count]
    gated_ref, grad_ref, grad_mixed_ref, bias_ref, shrink = refs[count : count + 5]
    raws = refs[count + 5 : count + (8 if tree else 6)]
    cots, sums, tall_sum, sems = refs[count + 5 + len(raws) :]
    narrow = lax.axis_index("narrow")
    rows_here, quarter = core_ref.shape[1:3]
    tokens = rows_here * ROW

    if tree:
        fetch_weights(sources, [(0, k * D, D, shrink, 192, 96, k * 32, sems.at[0]) for k in range(3)], tree)
    else:
        pltpu.make_async_copy(sources[0], shrink, sems.at[0]).start()
    for r in range(rows_here):
        for j in range(members):
            source = own_ref.at[narrow * rows_here + r] if j == 0 else parts[j - 1].at[r]
            place = run(r * ROW + (narrow ^ j) * quarter, quarter)
            pltpu.make_async_copy(source, cots.at[place, :], sems.at[1]).start()
    sums[...] = jnp.zeros_like(sums)
    wait_weights([(shrink, sems.at[0]), (cots, sems.at[1])])

    def do_channels(k, carry):
        channels = run(k * WIDTH, WIDTH)
        grad_gated = dot(cots[...], shrink[channels, :], ((1,), (1,)))
        for p in range(0, tokens, CHUNK):
            r, here = p // ROW, slice(p % ROW, p % ROW + CHUNK)
            grads = grad_gated[p : p + CHUNK]
            content = content_ref[r, here, channels].astype(F32)
            mixed = mixed_ref[r, here, channels].astype(F32)
            slope = slope_ref[r, here, channels].astype(F32)
            gated_ref[r, here, channels] = (content * mixed).astype(BF16)
            grad_ref[r, here, channels] = (grads * mixed * slope).astype(BF16)
            grad_mixed = (grads * content).astype(BF16)
            grad_mixed_ref[r, here, channels] = grad_mixed
            total = grad_mixed.astype(F32)
            sums[p : p + CHUNK, :] += total[:, :LANES] + total[:, LANES:]
        tall_sum[channels, :] = dot(gated_ref[:, :, channels].reshape(tokens, WIDTH), cots[...], ((0,), (0,)))
        return carry

    lax.fori_loop(0, HALF // WIDTH, do_channels, 0)
    for r in range(rows_here):
        _, live = doc_mask(0, ROW, lens_ref, narrow * rows_here + r)
        part = jnp.where(live, sums[r * ROW : (r + 1) * ROW, :], 0.0)
        bias_ref[...] = part if r == 0 else bias_ref[...] + part
    if tree:
        for j in range(3):
            emit_blocks("y", reader(tall_sum, 192, 48, j * BLOCK, slice(0, D)), D, j * D, *raws)
    else:
        raws[0][...] = tall_sum[...]


def content_sum_kernel(tree, normed_ref, grad_ref, *refs):
    raws, normed_turned, wide_sum = refs[:-2], refs[-2], refs[-1]
    tokens = normed_ref.shape[0] * normed_ref.shape[1]
    normed_turned[...] = normed_ref[...].reshape(tokens, D).T
    for c in range(0, HALF, D):
        wide_sum[...] = dot(normed_turned[...], grad_ref[:, :, c : c + D].reshape(tokens, D))
        if tree:
            emit_blocks("x", reader(wide_sum, 64, 16, 0, slice(0, D)), D, c, *raws)
        else:
            raws[0][:, c : c + D] = wide_sum[...]


def spatial_sum_kernel(lens_ref, grad_mixed_ref, gate_ref, square_ref):
    rows_here = grad_mixed_ref.shape[0]
    narrow = lax.axis_index("narrow")
    for row in range(rows_here):
        same, _ = doc_mask(0, ROW, lens_ref, narrow * rows_here + row)
        products = jnp.where(same, dot(grad_mixed_ref[row], gate_ref[row], ((1,), (1,))), 0.0)
        square_ref[...] = products if row == 0 else square_ref[...] + products


def gate_back_kernel(
    lens_ref, grad_mixed_ref, gate_ref, slope_ref, rstd_ref, spatial_ref, gains_ref, bias_ref,
    grad_ref, vectors_ref, turned, grad_gate, first_sums, second_sums, second, inverse,
):
    rows_here = grad_mixed_ref.shape[0]
    narrow = lax.axis_index("narrow")
    turned[...] = spatial_ref[...].T
    second[...] = jnp.zeros_like(second)
    inverse[...] = 1.0 / gains_ref[:, D:]

    def do_row(row, carry):
        same, _ = doc_mask(0, ROW, lens_ref, narrow * rows_here + row)
        masked = jnp.where(same, turned[...], jnp.zeros((), BF16))
        for c in range(0, HALF, WIDTH):
            grads_all = dot(masked, grad_mixed_ref[row, :, c : c + WIDTH])
            vector = jnp.zeros((8, WIDTH), F32)
            for p in range(0, ROW, CHUNK):
                here = slice(p, p + CHUNK)
                low = grads_all[here].astype(BF16)
                grad_gate[here, c : c + WIDTH] = low
                grads = low.astype(F32)
                products = grads * gate_ref[row, here, c : c + WIDTH].astype(F32)
                vector = vector + jnp.sum(products.reshape(CHUNK // 8, 8, WIDTH), axis=0)
                scaled = grads * gains_ref[0:1, D + c : D + c + WIDTH]
                first = scaled[:, :LANES] + scaled[:, LANES:]
                other = products[:, :LANES] + products[:, LANES:]
                first_sums[here, :] = first if c == 0 else first_sums[here, :] + first
                second_sums[here, :] = other if c == 0 else second_sums[here, :] + other
            second[:, c : c + WIDTH] += vector
        for p in range(0, ROW, CHUNK):
            here = slice(p, p + CHUNK)
            scale = rstd_ref[row, here, 0:1]
            first_mean = jnp.sum(first_sums[here, :], axis=1, keepdims=True) * (1.0 / HALF) * scale
            second_mean = jnp.sum(second_sums[here, :], axis=1, keepdims=True) * (1.0 / HALF) * scale
            for c in range(0, HALF, LANES):
                place = slice(c, c + LANES)
                scaled = grad_gate[here, place].astype(F32) * gains_ref[0:1, D + c : D + c + LANES] * scale
                vhat = gate_ref[row, here, place].astype(F32) * inverse[0:1, place]
                slope = slope_ref[row, here, place].astype(F32)
                grad_ref[row, here, place] = ((scaled - first_mean - vhat * second_mean) * slope).astype(BF16)
        return carry

    lax.fori_loop(0, rows_here, do_row, 0)
    vectors_ref[...] = jnp.zeros_like(vectors_ref)
    diagonal = lax.broadcasted_iota(jnp.int32, (64, 128), 0) == lax.broadcasted_iota(jnp.int32, (64, 128), 1)
    for owner in range(8):
        for k in range(2 if owner >= 2 else 0):
            c = (owner - 2) * 256 + k * 128
            total = jnp.sum(second[:, c : c + 128], axis=0, keepdims=True)
            vectors_ref[owner, k : k + 1, :] = total * inverse[0:1, c : c + 128]
        column = jnp.sum(bias_ref[owner * 64 : (owner + 1) * 64, :], axis=1, keepdims=True)
        vectors_ref[owner, 2:3, :] = jnp.sum(jnp.where(diagonal, column, 0.0), axis=0, keepdims=True)


def gate_sum_kernel(tree, normed_ref, grad_ref, square_ref, vectors_ref, *refs):
    raws, normed_turned, wide_sum = refs[:-2], refs[-2], refs[-1]
    tokens = normed_ref.shape[0] * normed_ref.shape[1]
    rest = HALF - SPLIT
    normed_turned[...] = normed_ref[...].reshape(tokens, D).T
    if tree:
        emit_blocks("y", reader(square_ref, 64, 16, 0, slice(0, ROW)), ROW, rest, *raws[3:])
        emit_blocks("y", lambda owner, member: vectors_ref[owner], VECTOR_LANES, rest + ROW, *raws[3:])
    else:
        raws[1][...] = square_ref[...]
        raws[2][...] = vectors_ref[...]
    for c in range(0, HALF, D):
        wide_sum[...] = dot(normed_turned[...], grad_ref[:, :, c : c + D].reshape(tokens, D))
        if not tree:
            raws[0][:, c : c + D] = wide_sum[...]
        elif c < SPLIT:
            emit_blocks("x", reader(wide_sum, 64, 16, 0, slice(0, D)), D, c, *raws[:3])
        else:
            emit_blocks("y", reader(wide_sum, 64, 16, 0, slice(0, D)), D, c - SPLIT, *raws[3:])


def layer_kernel(gated_ref, shrink, own_ref, core_ref, pair_ref, total):
    members, rows_here, quarter = total.shape[:3]
    narrow = lax.axis_index("narrow")
    for row in range(rows_here):
        added = dot(gated_ref[row], shrink[...])
        for member in range(members):
            total[member ^ narrow, row] = added[member * quarter : (member + 1) * quarter].astype(BF16)
    own_ref[...] = total[0]
    core_ref[...] = total[1]
    pair_ref[0] = total[2]
    pair_ref[1] = total[3]


def back_kernel(
    gate_grad_ref, content_grad_ref, gate_weight, weight, xhat_ref, scale_ref, gains_ref, layer_core, layer_pair,
    own_ref, core_ref, pair_ref, total,
):
    members, rows_here, quarter = total.shape[:3]
    narrow = lax.axis_index("narrow")
    for row in range(rows_here):
        grad_normed = dot(gate_grad_ref[row], gate_weight[...], ((1,), (1,))) + dot(
            content_grad_ref[row], weight[...], ((1,), (1,))
        )
        for member in range(members):
            here = slice(member * quarter, (member + 1) * quarter)
            xhat = xhat_ref[row, here, :].astype(F32)
            scaled = grad_normed[here] * gains_ref[0:1, :D]
            first_mean = jnp.mean(scaled, axis=1, keepdims=True)
            second_mean = jnp.mean(scaled * xhat, axis=1, keepdims=True)
            scale = scale_ref[row, here, 0:1]
            total[member ^ narrow, row] = ((scaled - first_mean - xhat * second_mean) * scale).astype(BF16)
    own_ref[...] = total[0]
    core_ref[0] = total[1]
    core_ref[1] = layer_core[...]
    for j in range(2):
        pair_ref[j, 0] = total[2 + j]
        pair_ref[j, 1] = layer_pair[j]


def give_kernel(
    cots_ref, acts_ref, grad_own, layer_own, core_ref, side_ref, forward_ref, grad_out, layer_out, grads, layers, sems
):
    rows_here = grad_own.shape[0]
    narrow = lax.axis_index("narrow")
    stores = []
    for kind, (base, own, total, out) in enumerate(
        ((cots_ref, grad_own, grads, grad_out), (acts_ref, layer_own, layers, layer_out))
    ):
        parts = [own, core_ref.at[kind], side_ref.at[0, kind], forward_ref.at[1, kind]]
        for j, part in enumerate(parts):
            rows = pl.ds((narrow ^ j) * rows_here, rows_here)
            total[j] = (base[rows].astype(F32) + part[...].astype(F32)).astype(total.dtype)
            stores.append(pltpu.make_async_copy(total.at[j], out.at[rows], sems.at[kind, j]))
            stores[-1].start()
    for store in stores:
        store.wait()


def sum_three(near_ref, came_ref, far_ref, half, columns):
    values = near_ref[half, :, :, columns].astype(F32) + came_ref[0, half, :, :, columns].astype(F32)
    return values + far_ref[half, :, :, columns].astype(F32)


def side_kernel(*refs):
    for i, out_ref in enumerate(refs[6:]):
        near, came, far = refs[3 * i : 3 * i + 3]
        for c in range(0, near.shape[3], LANES):
            out_ref[:, :, c : c + LANES] = sum_three(near, came, far, 1, slice(c, c + LANES)).astype(BF16)


def fold_kernel(*refs):
    sides, outputs = refs[12:16], refs[16:]
    first = 0
    for i in range(4):
        near, came, far = refs[3 * i : 3 * i + 3]
        for c in range(0, near.shape[3], LANES):
            place = slice(c, c + LANES)
            total = sum_three(near, came, far, 0, place) + sides[i][:, :, place].astype(F32)
            there = slice(first + c, first + c + LANES)
            outputs[0][:, there] = total[0]
            for step in range(1, 4):
                outputs[step][:, there] = total[step].astype(BF16)
        first += near.shape[3]


def norm_kernel(mine_ref, one_ref, two_ref, three_ref, weight_ref, gains_ref, low_ref, message_ref):
    wide, narrow = lax.axis_index("wide"), lax.axis_index("narrow")
    columns = mine_ref.shape[1]
    squares = jnp.zeros((BLOCK, LANES), F32)
    products = jnp.zeros((BLOCK, LANES), F32)
    here = run(narrow * BLOCK, BLOCK)
    for c in range(0, columns, LANES):
        place = slice(c, c + LANES)
        total = mine_ref[:, place]
        for ref in (one_ref, two_ref, three_ref):
            total = total + ref[:, place].astype(F32)
        low = total.astype(BF16)
        low_ref[:, place] = low
        value = low.astype(F32)
        square = value * value
        squares = squares + (square if c < columns - LANES else jnp.where(narrow == 0, square, 0.0))
        at = expand_column(c)
        if at is not None:
            weight = weight_ref[here, at : at + LANES].astype(BF16).astype(F32)
            products = products + value * weight
    first = wide * 64 + narrow * BLOCK
    lanes = lax.broadcasted_iota(jnp.int32, (BLOCK, D), 1)
    diagonal = lanes == lax.broadcasted_iota(jnp.int32, (BLOCK, D), 0) + first
    gain = jnp.sum(jnp.where(diagonal, gains_ref[0:1, :D], 0.0), axis=1, keepdims=True)
    first_raw = jnp.sum(products, axis=1, keepdims=True) / gain
    total = jnp.sum(squares) + jnp.sum(first_raw * first_raw)
    places = jnp.sum(jnp.where(diagonal, first_raw, 0.0), axis=0, keepdims=True)
    message_ref[...] = jnp.full(message_ref.shape, total, F32)
    for k in range(D // LANES):
        message_ref[k : k + 1, :] = places[:, k * LANES : (k + 1) * LANES]


def expand_column(c):
    right = HALF + SPLIT
    turn = right + HALF
    if c < right:
        return c
    if turn <= c < turn + HALF - SPLIT:
        return c - HALF
    return None


def adam_kernel(message_ref, own_ref, side_ref, other_ref, *refs):
    states, vectors, outputs, vector_outputs, norm_ref = refs[:12], refs[12:20], refs[20:35], refs[35:45], refs[45]
    results, blocks, sem = refs[46:61], refs[61], refs[62]
    wide, narrow = lax.axis_index("wide"), lax.axis_index("narrow")
    norm = jnp.sqrt(message_ref[4:5, :])
    norm_ref[0, 0] = jnp.max(norm)
    clip = CLIP_LIMIT / jnp.maximum(norm, CLIP_LIMIT)
    right = HALF + SPLIT
    turn = right + HALF
    blocks[narrow] = own_ref[...]
    blocks[narrow ^ 1] = other_ref[0]
    blocks[narrow ^ 2] = side_ref[...]
    blocks[narrow ^ 3] = other_ref[1]

    def update(which, gradient, rows, place):
        weight, momentum, variance, average = [ref[rows, place] for ref in states[4 * which : 4 * which + 4]]
        updates = adam_update(
            weight, gradient.astype(F32), momentum, variance, average, clip, RATE_MATRIX, DECAY_MATRIX
        )
        for ref, value in zip(results[5 * which : 5 * which + 5], updates):
            ref[rows, place] = value

    def do_member(member, carry):
        thin = run(member * BLOCK, BLOCK)
        for c in range(0, turn + HALF - SPLIT + ROW, LANES):
            gradient = blocks[member, :, c : c + LANES]
            at = expand_column(c)
            if at is not None:
                update(0, gradient, thin, slice(at, at + LANES))
            elif c < turn:
                k, at = (c - right) // D, (c - right) % D
                update(1, gradient, run(member * 48 + k * BLOCK, BLOCK), slice(at, at + LANES))
            else:
                at = c - turn - (HALF - SPLIT)
                update(2, gradient, thin, slice(at, at + LANES))
        for i in range(15):
            rows = run(member * 48, 48) if 5 <= i < 10 else thin
            pltpu.make_async_copy(results[i].at[rows, :], outputs[i].at[rows, :], sem.at[i]).start()
        return carry

    lax.fori_loop(0, 4, do_member, 0)
    own = blocks[0, :, turn + HALF - SPLIT + ROW :].astype(F32)
    gains = jnp.where(wide == 0, message_ref[0:2, :], jnp.where(wide == 1, message_ref[2:4, :], own[0:2, :]))
    for which, gradient in ((0, gains), (1, own[2:3, :64])):
        weight, momentum, variance, average = [ref[...] for ref in vectors[4 * which : 4 * which + 4]]
        updates = adam_update(
            weight, gradient, momentum, variance, average, clip[:, : gradient.shape[1]], RATE_VECTOR, 0.0
        )
        for ref, value in zip(vector_outputs[5 * which : 5 * which + 5], updates):
            ref[...] = value
    for i in range(15):
        pltpu.make_async_copy(results[i], outputs[i], sem.at[i]).wait()


def call_kernel(kernel, name, args, in_specs, out_types, scratch, flops, limit=VMEM_LIMIT):
    vmem = pl.BlockSpec(memory_space=pltpu.VMEM)
    specs = [kind[1] if isinstance(kind, tuple) else vmem for kind in out_types]
    types = [
        kind[0] if isinstance(kind, tuple) else pltpu.VMEM(kind.shape, kind.dtype) for kind in out_types
    ]
    in_specs = [vmem if spec is None else spec for spec in in_specs]
    args = [
        pltpu.with_memory_space_constraint(value, pltpu.HBM) if spec.memory_space == pltpu.HBM else value
        for value, spec in zip(args, in_specs)
    ]
    results = pl.pallas_call(
        kernel,
        name=name,
        in_specs=in_specs,
        out_specs=specs,
        out_shape=types,
        scratch_shapes=scratch,
        compiler_params=pltpu.CompilerParams(vmem_limit_bytes=limit),
        cost_estimate=pl.CostEstimate(flops=int(flops), bytes_accessed=int(flops / 500), transcendentals=0),
    )(*args)
    return list(results)


def swap_with(value, axis, size, bit):
    return lax.ppermute(value, axis, [(i, i ^ bit) for i in range(size)])


def after(value, *others):
    return lax.optimization_barrier((value,) + others)[0]


def sum_core(keep_far, came):
    return (keep_far.astype(F32) + came[1].astype(F32)).astype(BF16)


def adam_update(weight, gradient, momentum, variance, average, clip_scale, step_rate, decay_rate):
    ema_rate = min(EMA_DECAY, (1.0 + STEP) / (10.0 + STEP))
    clipped = clip_scale * gradient
    moment = BETA_FIRST * momentum + (1.0 - BETA_FIRST) * clipped
    square = BETA_SECOND * variance + (1.0 - BETA_SECOND) * clipped * clipped
    first_hat = moment / (1.0 - BETA_FIRST**STEP)
    second_hat = square / (1.0 - BETA_SECOND**STEP)
    updated = weight - step_rate * (
        first_hat / (jnp.sqrt(second_hat) + ADAM_EPS) + decay_rate * weight
    )
    smoothed = ema_rate * average + (1.0 - ema_rate) * updated
    return (clipped, moment, square, updated, smoothed)


def on_device(
    activations,
    cotangent,
    doc_lengths,
    expand_weight,
    expand_momentum,
    expand_variance,
    expand_average,
    shrink_weight,
    shrink_momentum,
    shrink_variance,
    shrink_average,
    spatial_weight,
    spatial_momentum,
    spatial_variance,
    spatial_average,
    norm_gains,
    gains_momentum,
    gains_variance,
    gains_average,
    spatial_bias,
    bias_momentum,
    bias_variance,
    bias_average,
):
    narrow_size, wide_size = lax.axis_size("narrow"), lax.axis_size("wide")
    wide, narrow = lax.axis_index("wide"), lax.axis_index("narrow")
    group_rows, quarter = activations.shape[0], activations.shape[1]
    rows = group_rows // narrow_size
    tokens = rows * ROW
    tree = (wide_size, narrow_size) == (8, 4)
    smem = pl.BlockSpec(memory_space=pltpu.SMEM)
    anywhere = pl.BlockSpec(memory_space=pl.ANY)
    stored = pl.BlockSpec(memory_space=pltpu.HBM)
    shape = jax.ShapeDtypeStruct
    dma = pltpu.SemaphoreType.DMA
    part = shape((rows, quarter, D), BF16)
    product = 2 * tokens * HALF * D
    cross_x = lambda value: swap_with(value, "wide", wide_size, 1)
    cross_y = lambda value: swap_with(value, "narrow", narrow_size, 2)
    cross_core = lambda value: swap_with(value, "narrow", narrow_size, 1)

    def trade(core_part, pair):
        side = cross_y(pair)
        return [cross_core(core_part), side, cross_core(side)]

    def stack(values):
        kind = shape((len(values), *values[0].shape), values[0].dtype)
        return call_kernel(stack_kernel, "stack", values, [None] * len(values), [kind], [], product // 64)[0]

    def add(*values):
        kind = shape(values[0].shape, values[0].dtype)
        return call_kernel(add_kernel, "add", values, [None] * len(values), [kind], [], product // 64)[0]

    pair = shape((2, *part.shape), BF16)

    def cut(acts, cots):
        return call_kernel(
            cut_kernel,
            "cut",
            [acts, cots],
            [stored] * 2,
            [(pair, stored), (shape((2, *pair.shape), BF16), stored)],
            [dma((6,))],
            product // 64,
        )

    if tree:
        first_own = call_kernel(
            pack_first_kernel,
            "pack_first",
            [expand_weight, spatial_weight, norm_gains.reshape(2, LANES), spatial_bias.reshape(1, 64)],
            [stored] * 4,
            [shape((32, HALF + ROW + VECTOR_LANES), BF16)],
            [pltpu.VMEM((32, HALF), F32), pltpu.VMEM((32, ROW), F32), pltpu.VMEM((2, LANES), F32)]
            + [pltpu.VMEM((1, 64), F32), dma((4,))],
            product // 64,
        )[0]
        over_z = lambda own: [swap_with(own, "wide", wide_size, 2 * s) for s in range(1, 4)]
        came_z = over_z(first_own)
        core_cut, pair_cut = cut(after(activations, first_own), cotangent)
        side_came = cross_y(pair_cut)
        expand_own, shrink_own = call_kernel(
            pack_second_kernel,
            "pack_second",
            [expand_weight, shrink_weight],
            [stored, stored],
            [shape((32, HALF), BF16)] * 2,
            [pltpu.VMEM((32, HALF), F32), pltpu.VMEM((96, D), F32), dma((2,))],
            product // 64,
        )
        *came_z, core_came, _, expand_own = lax.optimization_barrier(
            (*came_z, cross_core(core_cut), pair_cut, expand_own)
        )
        first_near = stack([first_own, *came_z])
        first_across = cross_x(first_near)
        expand_own = after(expand_own, first_near)
        *came_z, side_came = lax.optimization_barrier((*over_z(expand_own), side_came))
        expand_near = stack([expand_own, *came_z])
        expand_across = cross_x(after(expand_near, first_across))
        shrink_own = after(shrink_own, expand_near)
        shrink_came = over_z(shrink_own)
        near_core = cross_core(after(first_near, expand_near))
        across_core = cross_core(after(first_across, expand_near))
        forward_came = cross_core(after(side_came, expand_near))
        first_pieces = [after(first_near, expand_near), first_across, near_core, across_core]
        small_pieces = first_pieces[:2]
        near_other = cross_core(expand_near)
        count = len(PIECES)
    else:
        gather = lambda value: lax.all_gather(value.astype(BF16), "wide", axis=0, tiled=True)
        expand_low = gather(expand_weight)
        gains_low, bias_low = gather(norm_gains), gather(spatial_bias)
        small = jnp.concatenate(
            [
                gains_low.reshape(8, 2, 128),
                jnp.pad(bias_low.reshape(8, 1, 64), ((0, 0), (0, 0), (0, 64))),
                jnp.zeros((8, 13, 128), BF16),
            ],
            axis=1,
        )
        first_pieces = [expand_low[:, HALF:], gather(spatial_weight)]
        small_pieces = [small, small]
        expand_pieces, shrink_pieces = [expand_low[:, :HALF]], [gather(shrink_weight)]
        core_came, side_came, forward_came = trade(*cut(activations, cotangent))
        count = 2

    low_d, low_half = shape((rows, ROW, D), BF16), shape((rows, ROW, HALF), BF16)
    thin = shape((rows, ROW, 128), F32)
    weight_type = shape((D, HALF), BF16)

    normed, xhat, scale, gate_normed, slope, rstd, spatial_low, gains, bias_col, gate_weight = call_kernel(
        functools.partial(gating_kernel, tree, count, narrow_size),
        "gating",
        [activations, core_came, side_came, forward_came] + list(first_pieces) + list(small_pieces),
        [stored] + [anywhere] * (narrow_size - 1 + count + 2),
        [low_d, low_d, thin, low_half, low_half, thin]
        + [shape((ROW, ROW), BF16), shape((8, D + HALF), F32), shape((ROW, 128), F32), weight_type],
        [
            pltpu.VMEM((8, BLOCK, 128), BF16),
            pltpu.VMEM((narrow_size, *part.shape), BF16),
            pltpu.VMEM((ROW, HALF), F32),
            pltpu.VMEM((ROW, 128), F32),
            dma((4,)),
        ],
        product // 64,
    )

    bias_late = bias_col
    if tree:
        *shrink_came, expand_across, _ = lax.optimization_barrier((*shrink_came, expand_across, normed))
        shrink_near = stack([shrink_own, *shrink_came])
        shrink_across = cross_x(shrink_near)
        expand_pieces = [expand_near, expand_across, near_other, cross_core(expand_across)]
        bias_late = after(bias_col, shrink_near)
    mixed = call_kernel(
        mixing_kernel,
        "mixing",
        [doc_lengths, spatial_low, gate_normed, bias_late],
        [smem] + [None] * 3,
        [low_half],
        [],
        product // 64,
    )[0]
    normed_late = normed
    if tree:
        expand_pieces[3], normed_late, _ = lax.optimization_barrier((expand_pieces[3], normed, mixed))
    content, content_slope, content_weight = call_kernel(
        functools.partial(content_up_kernel, tree),
        "content_up",
        [normed_late, *expand_pieces],
        [None] + [anywhere] * len(expand_pieces),
        [low_half, low_half, weight_type],
        [dma(())],
        product // 64,
    )
    if tree:
        shrink_across, _ = lax.optimization_barrier((shrink_across, content))
        shrink_pieces = [shrink_near, shrink_across, cross_core(shrink_near), cross_core(shrink_across)]

    def raw_outputs(column_list, plain):
        if tree:
            return [
                shape(size, BF16)
                for columns in column_list
                for size in ((2, 4, BLOCK, columns), (2, 4, BLOCK, columns), (2, 2, 4, BLOCK, columns))
            ]
        return [shape(size, F32) for size in plain]

    gated, content_grad, grad_mixed, bias_part, shrink_low, *shrink_raws = call_kernel(
        functools.partial(content_down_kernel, tree, len(shrink_pieces), narrow_size),
        "content_down",
        [doc_lengths, content, content_slope, mixed, cotangent, core_came, side_came, forward_came, *shrink_pieces],
        [smem, None, None, None, stored] + [anywhere] * (narrow_size - 1 + len(shrink_pieces)),
        [low_half, low_half, low_half, shape((ROW, 128), F32), shape((HALF, D), BF16)]
        + raw_outputs((HALF,), ((HALF, D),)),
        [
            pltpu.VMEM((tokens, D), BF16),
            pltpu.VMEM((tokens, 128), F32),
            pltpu.VMEM((HALF, D), F32),
            dma((2,)),
        ],
        product // 64,
    )
    if tree:
        came = {"shrink": cross_core(shrink_raws[2])}
    sum_scratch = [pltpu.VMEM((D, tokens), BF16), pltpu.VMEM((D, D), F32)]
    content_raws = call_kernel(
        functools.partial(content_sum_kernel, tree),
        "content_sum",
        [normed, content_grad],
        [None] * 2,
        raw_outputs((HALF,), ((D, HALF),)),
        sum_scratch,
        product // 64,
    )
    mixed_late = grad_mixed
    if tree:
        came["shrink"], content_raws[0] = lax.optimization_barrier((came["shrink"], content_raws[0]))
        came["content"] = cross_core(content_raws[2])
        far = {"shrink": sum_core(shrink_raws[1], came["shrink"])}
        came_far = {"shrink": cross_y(far["shrink"])}
        mixed_late = after(grad_mixed, far["shrink"])
    square_sum = call_kernel(
        spatial_sum_kernel,
        "spatial_sum",
        [doc_lengths, mixed_late, gate_normed],
        [smem, None, None],
        [shape((ROW, ROW), F32)],
        [],
        product // 64,
    )[0]
    if tree:
        came["content"], square_sum = lax.optimization_barrier((came["content"], square_sum))
        far["content"] = sum_core(content_raws[1], came["content"])
        came_far["content"] = cross_x(far["content"])
        mixed_late = after(grad_mixed, far["content"])

    gate_grad, vectors = call_kernel(
        gate_back_kernel,
        "gate_back",
        [doc_lengths, mixed_late, gate_normed, slope, rstd, spatial_low, gains, bias_part],
        [smem] + [None] * 7,
        [low_half, shape((8, BLOCK, 128), F32)],
        [
            pltpu.VMEM((ROW, ROW), BF16),
            pltpu.VMEM((ROW, HALF), BF16),
            pltpu.VMEM((ROW, 128), F32),
            pltpu.VMEM((ROW, 128), F32),
            pltpu.VMEM((8, HALF), F32),
            pltpu.VMEM((8, HALF), F32),
        ],
        product // 64,
    )
    normed_late = normed
    if tree:
        came_far["shrink"], normed_late = lax.optimization_barrier((came_far["shrink"], normed))
    second_raws = call_kernel(
        functools.partial(gate_sum_kernel, tree),
        "gate_sum",
        [normed_late, gate_grad, square_sum, vectors],
        [None] * 4,
        raw_outputs((SPLIT, HALF - SPLIT + ROW + VECTOR_LANES), ((D, HALF), (ROW, ROW), (8, BLOCK, 128))),
        sum_scratch,
        product // 64,
    )
    def side_step(terms, widths):
        kinds = [shape((4, BLOCK, width), BF16) for width in widths]
        return call_kernel(side_kernel, "side", terms, [None] * 6, kinds, [], product // 64)

    gated_late = gated
    if tree:
        second_raws[2], second_raws[5], came_far["content"] = lax.optimization_barrier(
            (second_raws[2], second_raws[5], came_far["content"])
        )
        second_came = [cross_core(second_raws[i]) for i in (2, 5)]
        first_terms = [content_raws[0], came["content"], came_far["content"]]
        first_terms += [shrink_raws[0], came["shrink"], came_far["shrink"]]
        first_sides = side_step(first_terms, (HALF, HALF))
        first_came_side = [cross_y(first_sides[0]), cross_x(first_sides[1])]
        gated_late = after(gated, second_raws[0], *first_sides)
    part_scratch = pltpu.VMEM((narrow_size, *part.shape), BF16)
    layer_own, layer_core, layer_pair = call_kernel(
        layer_kernel,
        "layer",
        [gated_late, shrink_low],
        [None] * 2,
        [part, part, pair],
        [part_scratch],
        product // 64,
    )
    grad_late = gate_grad
    if tree:
        *second_came, layer_own = lax.optimization_barrier((*second_came, layer_own))
        second_far = [sum_core(second_raws[1], second_came[0]), sum_core(second_raws[4], second_came[1])]
        second_came_far = [cross_x(second_far[0]), cross_y(second_far[1])]
        grad_late = after(gate_grad, *second_far)
    grad_own, core_back, pair_back = call_kernel(
        back_kernel,
        "back",
        [grad_late, content_grad, gate_weight, content_weight, xhat, scale, gains, layer_core, layer_pair],
        [None] * 9,
        [part, pair, shape((2, *pair.shape), BF16)],
        [part_scratch],
        product // 64,
    )

    def give(cots_base, acts_base, returned):
        whole = (group_rows, quarter, D)
        return call_kernel(
            give_kernel,
            "give",
            [cots_base, acts_base, grad_own, layer_own, *returned],
            [None] * 7,
            [(shape(whole, F32), stored), (shape(whole, BF16), stored)],
            [
                pltpu.VMEM((narrow_size, *part.shape), F32),
                pltpu.VMEM((narrow_size, *part.shape), BF16),
                dma((2, narrow_size)),
            ],
            product // 64,
        )

    if tree:
        columns = HALF + HALF + SPLIT + (HALF - SPLIT) + ROW + VECTOR_LANES
        tied = lax.optimization_barrier((*second_came_far, *first_came_side, grad_own))
        second_came_far, first_came_side, grad_own = tied[:2], tied[2:4], tied[4]
        second_terms = [second_raws[0], second_came[0], second_came_far[0]]
        second_terms += [second_raws[3], second_came[1], second_came_far[1]]
        second_sides = side_step(second_terms, (SPLIT, HALF - SPLIT + ROW + VECTOR_LANES))
        second_came_side = [cross_y(second_sides[0]), cross_x(second_sides[1])]
        terms = first_terms[:3] + second_terms[:3] + first_terms[3:] + second_terms[3:]
        came_side = [first_came_side[0], second_came_side[0], first_came_side[1], second_came_side[1]]
        mine, *sent = call_kernel(
            fold_kernel,
            "fold",
            terms + came_side,
            [None] * 16,
            [shape((BLOCK, columns), F32)] + [shape((BLOCK, columns), BF16)] * 3,
            [],
            product // 64,
        )
        came_z = [swap_with(sent[s - 1], "wide", wide_size, 2 * s) for s in range(1, 4)]
        matrices = [expand_weight, expand_momentum, expand_variance, expand_average]
        matrices += [shrink_weight, shrink_momentum, shrink_variance, shrink_average]
        matrices += [spatial_weight, spatial_momentum, spatial_variance, spatial_average]
        fetched = [*matrices, cotangent, activations]
        states = call_kernel(
            fetch_kernel,
            "fetch",
            list(lax.optimization_barrier((*fetched, sent[0]))[:14]),
            [stored] * 14,
            [shape(value.shape, value.dtype) for value in fetched],
            [dma((14,))],
            product // 64,
        )
        states, bases = states[:12], states[12:]
        side_back = cross_y(after(pair_back, sent[0]))
        core_back = cross_core(after(core_back, sent[0]))
        *came_z, first_state = lax.optimization_barrier((*came_z, states[0]))
        low, message = call_kernel(
            norm_kernel,
            "norm",
            [mine, *came_z, first_state, gains],
            [None] * 6,
            [shape((BLOCK, columns), BF16), shape((8, LANES), F32)],
            [],
            product // 64,
        )
        side = cross_y(low)
        message = add(message, cross_core(message))
        message = add(message, cross_x(message))
        *arrived, side, side_back = lax.optimization_barrier((*over_z(message), side, side_back))
        message = add(message, *arrived)
        other = cross_core(stack([low, side]))
        returned = [core_back, side_back, cross_core(side_back)]
        input_grad, layer_out = give(*bases, returned)
        arrived, layer_out, input_grad = lax.optimization_barrier((cross_y(message), layer_out, input_grad))
        message = add(message, arrived)
        as_rows = lambda value: value.reshape(-1, min(value.shape[0], LANES))
        vector_states = [norm_gains, gains_momentum, gains_variance, gains_average]
        vector_states += [spatial_bias, bias_momentum, bias_variance, bias_average]
        vector_kinds = [shape((2, LANES), F32)] * 5 + [shape((1, 64), F32)] * 5
        *updates, norm_row = call_kernel(
            adam_kernel,
            "adam",
            [message, low, side, other, *states] + [as_rows(value) for value in vector_states],
            [None] * 24,
            [(shape(value.shape, F32), stored) for value in (matrices[0], matrices[4], matrices[8]) for _ in range(5)]
            + [(kind, pl.BlockSpec(memory_space=pltpu.VMEM)) for kind in vector_kinds]
            + [(shape((1, 1), F32), smem)],
            [pltpu.VMEM(value.shape, F32) for value in (matrices[0], matrices[4], matrices[8]) for _ in range(5)]
            + [pltpu.VMEM((4, BLOCK, columns), BF16), dma((15,))],
            product // 64,
        )
        grad_norm = norm_row[0, 0]
        results = [layer_out, input_grad, grad_norm, *updates[:15]]
        return tuple(results + [value.reshape(-1) for value in updates[15:]])

    returned = trade(core_back, pair_back)
    input_grad, layer_out = give(cotangent, activations, returned)
    gains_size, bias_size = norm_gains.shape[0], spatial_bias.shape[0]
    vectors = lax.psum(second_raws[2], ("narrow", "wide"))
    totals = lax.psum(
        (jnp.concatenate([content_raws[0], second_raws[0]], axis=1), shrink_raws[0], second_raws[1]), "narrow"
    )
    expand_shard, shrink_shard, spatial_shard = [
        lax.psum_scatter(total, "wide", scatter_dimension=0, tiled=True) for total in totals
    ]
    second_shard = lax.dynamic_slice_in_dim(vectors[:, :2].reshape(-1), wide * gains_size, gains_size)
    bias_shard = lax.dynamic_slice_in_dim(vectors[:, 2, :64].reshape(-1), wide * bias_size, bias_size)
    low_weight = expand_weight.astype(BF16).astype(F32)
    height = expand_weight.shape[0]
    first_gain = lax.dynamic_slice_in_dim(gains[0], wide * height, height)
    first_raw = jnp.sum(low_weight * expand_shard, axis=1) / first_gain
    squares = [expand_shard, shrink_shard, spatial_shard, second_shard, bias_shard, first_raw]
    square_total = lax.psum(sum(jnp.sum(value * value) for value in squares), "wide")
    first_all = lax.all_gather(first_raw, "wide", axis=0, tiled=True)
    first_all = jnp.concatenate([first_all, jnp.zeros((HALF,), F32)])
    gains_shard = second_shard + lax.dynamic_slice_in_dim(first_all, wide * gains_size, gains_size)
    grad_norm = jnp.sqrt(square_total)
    clip_scale = CLIP_LIMIT / jnp.maximum(grad_norm, CLIP_LIMIT)
    results = [layer_out, input_grad, grad_norm]
    for weight, shard, momentum, variance, average, rate, decay in (
        (expand_weight, expand_shard, expand_momentum, expand_variance, expand_average, RATE_MATRIX, DECAY_MATRIX),
        (shrink_weight, shrink_shard, shrink_momentum, shrink_variance, shrink_average, RATE_MATRIX, DECAY_MATRIX),
        (spatial_weight, spatial_shard, spatial_momentum, spatial_variance, spatial_average, RATE_MATRIX, DECAY_MATRIX),
        (norm_gains, gains_shard, gains_momentum, gains_variance, gains_average, RATE_VECTOR, 0.0),
        (spatial_bias, bias_shard, bias_momentum, bias_variance, bias_average, RATE_VECTOR, 0.0),
    ):
        results += adam_update(weight, shard, momentum, variance, average, clip_scale, rate, decay)
    return tuple(results)


def solution(mesh):
    tokens, matrix, vector = P("wide", "narrow", None), P("wide", None), P("wide")
    return jax.shard_map(
        on_device,
        mesh=mesh,
        in_specs=(tokens, tokens) + (matrix,) * 13 + (vector,) * 8,
        out_specs=(tokens, tokens, P()) + (matrix,) * 15 + (vector,) * 10,
        check_vma=False,
    )
```

```python
import functools

import jax
import jax.numpy as jnp
from jax import lax
from jax.experimental import pallas as pl
from jax.experimental.pallas import tpu as pltpu
from jax.sharding import PartitionSpec as P

D = 512
FF = 3072
ROW = 512
DOCS = 5
STEP = 10
HALF = 1536

LAYER_EPS = 1e-05
CLIP_LIMIT = 1.0
BETA_FIRST = 0.9
BETA_SECOND = 0.999
ADAM_EPS = 1e-08
RATE_MATRIX = 0.03
RATE_VECTOR = 0.2
DECAY_MATRIX = 0.1
EMA_DECAY = 0.9999

F32 = jnp.float32
BF16 = jnp.bfloat16
GELU_A = 0.7978845608028654
GELU_B = GELU_A * 0.044715
LANES = 128
CHUNK = 64
BLOCK = 16
VMEM_LIMIT = 16 * 1024 * 1024

PIECES = ((0, 0), (1, 0), (0, 1), (1, 1))
WIDTH = 256
SPLIT = 1024
VECTOR_LANES = 128


def gelu_gate(hidden):
    squares = hidden * hidden
    gate = 0.5 * jnp.tanh(hidden * (GELU_A + GELU_B * squares)) + 0.5
    return squares, gate


def gelu_slope(hidden, squares, gate):
    return gate * (1.0 + hidden * (1.0 - gate) * (2.0 * GELU_A + 6.0 * GELU_B * squares))


def doc_ids(places, lens_ref, row):
    bound = jnp.int32(0)
    ids = jnp.zeros(places.shape, jnp.int32)
    for k in range(DOCS - 1):
        bound = bound + lens_ref[row, k]
        ids = ids + (places >= bound).astype(jnp.int32)
    return ids


def doc_mask(start, rows, lens_ref, row):
    across = doc_ids(lax.broadcasted_iota(jnp.int32, (1, ROW), 1), lens_ref, row)
    down = doc_ids(lax.broadcasted_iota(jnp.int32, (rows, 1), 0) + start, lens_ref, row)
    live = down != DOCS - 1
    return jnp.where(live, down, -1) == across, live


def dot(left, right, dims=((1,), (0,))):
    return lax.dot_general(left, right, (dims, ((), ())), preferred_element_type=F32)


def run(start, size):
    return pl.ds(pl.multiple_of(start, size), size)


def fetch_weights(sources, moves, tree):
    if not tree:
        for source, (_, _, _, target, _, _, _, sem) in zip(sources, moves):
            pltpu.make_async_copy(source, target, sem).start()
        return
    wide, core = lax.axis_index("wide"), lax.axis_index("narrow") & 1
    for base, first, count, target, height, unit, shift, sem in moves:
        for i, (x_off, core_off) in enumerate(PIECES):
            for step in range(4):
                start = (wide ^ (2 * step + x_off)) * height + (core ^ core_off) * unit + shift
                pltpu.make_async_copy(
                    sources[base + i].at[step, :, pl.ds(first, count)], target.at[run(start, 32), :], sem
                ).start()


def wait_weights(targets):
    for target, sem in targets:
        pltpu.make_async_copy(target, target, sem).wait()


def cut_kernel(acts_ref, cots_ref, core_out, pair_out, sems):
    rows_here = core_out.shape[1]
    narrow = lax.axis_index("narrow")
    copies = []
    for i, ref in enumerate((acts_ref, cots_ref)):
        for j, target in ((1, core_out.at[i]), (2, pair_out.at[0, i]), (3, pair_out.at[1, i])):
            source = ref.at[pl.ds((narrow ^ j) * rows_here, rows_here)]
            copies.append(pltpu.make_async_copy(source, target, sems.at[len(copies)]))
    for copy in copies:
        copy.start()
    for copy in copies:
        copy.wait()


def pack_first_kernel(expand_ref, spatial_ref, gains_ref, bias_ref, out_ref, expand, spatial, gains, bias, sems):
    rows = run((lax.axis_index("narrow") & 1) * 32, 32)
    copies = [
        pltpu.make_async_copy(expand_ref.at[rows, pl.ds(HALF, HALF)], expand, sems.at[0]),
        pltpu.make_async_copy(spatial_ref.at[rows, :], spatial, sems.at[1]),
        pltpu.make_async_copy(gains_ref, gains, sems.at[2]),
        pltpu.make_async_copy(bias_ref, bias, sems.at[3]),
    ]
    for copy in copies:
        copy.start()
    for copy in copies:
        copy.wait()
    vectors = jnp.concatenate(
        [
            gains[...],
            jnp.concatenate([bias[...], jnp.zeros((1, LANES - 64), F32)], axis=1),
            jnp.zeros((29, LANES), F32),
        ],
        axis=0,
    )
    out_ref[:, HALF + ROW :] = vectors.astype(BF16)
    out_ref[:, :HALF] = expand[...].astype(BF16)
    out_ref[:, HALF : HALF + ROW] = spatial[...].astype(BF16)


def pack_second_kernel(expand_ref, shrink_ref, expand_out, shrink_out, expand, shrink, sems):
    core = lax.axis_index("narrow") & 1
    copies = [
        pltpu.make_async_copy(expand_ref.at[run(core * 32, 32), pl.ds(0, HALF)], expand, sems.at[0]),
        pltpu.make_async_copy(shrink_ref.at[run(core * 96, 32 * 3), :], shrink, sems.at[1]),
    ]
    for copy in copies:
        copy.start()
    for copy in copies:
        copy.wait()
    expand_out[...] = expand[...].astype(BF16)
    for k in range(3):
        shrink_out[:, k * D : (k + 1) * D] = shrink[k * 32 : (k + 1) * 32, :].astype(BF16)


def stack_kernel(*refs):
    for i, ref in enumerate(refs[:-1]):
        refs[-1][i] = ref[...]


def add_kernel(*refs):
    total = refs[0][...] + refs[1][...]
    if len(refs) == 5:
        total = total + (refs[2][...] + refs[3][...])
    refs[-1][...] = total


def fetch_kernel(*refs):
    count = (len(refs) - 1) // 2
    copies = [pltpu.make_async_copy(refs[i], refs[count + i], refs[-1].at[i]) for i in range(count)]
    for copy in copies:
        copy.start()
    for copy in copies:
        copy.wait()


def gating_kernel(tree, count, members, own_ref, core_ref, side_ref, forward_ref, *refs):
    parts = [core_ref.at[0], side_ref.at[0, 0], forward_ref.at[1, 0]]
    sources, small_sources = refs[:count], refs[count : count + 2]
    (
        normed_ref, xhat_ref, scale_ref, gate_ref, slope_ref, rstd_ref, spatial_ref, gains_ref, bias_col, weight,
        small, acts, active, sums, sems,
    ) = refs[count + 2 :]
    wide, narrow = lax.axis_index("wide"), lax.axis_index("narrow")
    rows_here, quarter = acts.shape[1:3]

    pltpu.make_async_copy(own_ref.at[pl.ds(narrow * rows_here, rows_here)], acts.at[narrow], sems.at[3]).start()
    for j, part in enumerate(parts):
        pltpu.make_async_copy(part, acts.at[narrow ^ (j + 1)], sems.at[3]).start()
    fetch_weights(
        sources,
        [
            (0, 0, HALF, weight, 64, 32, 0, sems.at[0]),
            (0, HALF, ROW, spatial_ref, 64, 32, 0, sems.at[1]),
        ],
        tree,
    )
    if tree:
        for x_off in range(2):
            for step in range(4):
                pltpu.make_async_copy(
                    small_sources[x_off].at[step, pl.ds(0, BLOCK), pl.ds(HALF + ROW, 128)],
                    small.at[wide ^ (2 * step + x_off)],
                    sems.at[2],
                ).start()
    else:
        pltpu.make_async_copy(small_sources[0], small, sems.at[2]).start()
    wait_weights([(weight, sems.at[0]), (spatial_ref, sems.at[1]), (small, sems.at[2]), (acts, sems.at[3])])
    diagonal = lax.broadcasted_iota(jnp.int32, (64, 128), 0) == lax.broadcasted_iota(jnp.int32, (64, 128), 1)
    for owner in range(8):
        values = small[owner].astype(F32)
        for k in range(2):
            gains_ref[:, owner * 256 + k * 128 : owner * 256 + (k + 1) * 128] = jnp.broadcast_to(
                values[k : k + 1, :], (8, 128)
            )
        column = jnp.sum(jnp.where(diagonal, values[2:3, :], 0.0), axis=1, keepdims=True)
        bias_col[owner * 64 : (owner + 1) * 64, :] = jnp.broadcast_to(column, (64, 128))

    def do_row(row, carry):
        for member in range(members):
            here = slice(member * quarter, (member + 1) * quarter)
            values = acts[member, row].astype(F32)
            shifted = values - jnp.mean(values, axis=1, keepdims=True)
            scale = lax.rsqrt(jnp.mean(shifted * shifted, axis=1, keepdims=True) + LAYER_EPS)
            xhat = shifted * scale
            scale_ref[row, here, :] = jnp.broadcast_to(scale, (quarter, 128))
            xhat_ref[row, here, :] = xhat.astype(BF16)
            normed_ref[row, here, :] = (xhat * gains_ref[0:1, :D]).astype(BF16)

        normed = normed_ref[row]
        for c in range(0, HALF, WIDTH):
            hidden = dot(normed, weight[:, c : c + WIDTH])
            for p in range(0, ROW, CHUNK):
                here = slice(p, p + CHUNK)
                values = hidden[here]
                squares, gate = gelu_gate(values)
                slope_ref[row, here, c : c + WIDTH] = gelu_slope(values, squares, gate).astype(BF16)
                result = values * gate
                active[here, c : c + WIDTH] = result
                total = result[:, :LANES] + result[:, LANES:]
                sums[here, :] = total if c == 0 else sums[here, :] + total
        for p in range(0, ROW, CHUNK):
            here = slice(p, p + CHUNK)
            centre = jnp.sum(sums[here, :], axis=1, keepdims=True) * (1.0 / HALF)
            total = jnp.zeros((CHUNK, LANES), F32)
            for c in range(0, HALF, LANES):
                shifted = active[here, c : c + LANES] - centre
                total = total + shifted * shifted
            scale = lax.rsqrt(jnp.sum(total, axis=1, keepdims=True) * (1.0 / HALF) + LAYER_EPS)
            rstd_ref[row, here, :] = jnp.broadcast_to(scale, (CHUNK, 128))
            for c in range(0, HALF, LANES):
                vhat = (active[here, c : c + LANES] - centre) * scale
                gate_ref[row, here, c : c + LANES] = (vhat * gains_ref[0:1, D + c : D + c + LANES]).astype(BF16)

        return carry

    lax.fori_loop(0, rows_here, do_row, 0)


def mixing_kernel(lens_ref, spatial_ref, gate_ref, bias_col, mixed_ref):
    rows_here = gate_ref.shape[0]
    narrow = lax.axis_index("narrow")
    for row in range(rows_here):
        same, live = doc_mask(0, ROW, lens_ref, narrow * rows_here + row)
        masked = jnp.where(same, spatial_ref[...], jnp.zeros((), BF16))
        bias = jnp.where(live, bias_col[:, 0:1], 0.0)
        for c in range(0, HALF, D):
            mixed_ref[row, :, c : c + D] = (dot(masked, gate_ref[row, :, c : c + D]) + bias).astype(BF16)


def emit_blocks(order, read, columns, first, keep_near, keep_far, send):
    wide, narrow = lax.axis_index("wide"), lax.axis_index("narrow")
    for core in range(2):
        for one in range(2):
            for two in range(2):
                for step in range(4):
                    x_off, y_off = (one, two) if order == "x" else (two, one)
                    values = read(wide ^ (2 * step + x_off), narrow ^ (2 * y_off + core)).astype(BF16)
                    place = pl.ds(first, columns)
                    if core == 1:
                        send[one, two, step, :, place] = values
                    elif one == 1:
                        keep_far[two, step, :, place] = values
                    else:
                        keep_near[two, step, :, place] = values


def reader(matrix, height, part, shift, columns):
    def read(owner, member):
        return matrix[run(owner * height + member * part + shift, BLOCK), columns]

    return read


def content_up_kernel(tree, normed_ref, *refs):
    sources, (content_ref, slope_ref, weight, sem) = refs[:-4], refs[-4:]
    tokens = normed_ref.shape[0] * normed_ref.shape[1]
    if tree:
        fetch_weights(sources, [(0, 0, HALF, weight, 64, 32, 0, sem)], tree)
    else:
        pltpu.make_async_copy(sources[0], weight, sem).start()
    wait_weights([(weight, sem)])

    def do_channels(k, carry):
        channels = run(k * WIDTH, WIDTH)
        hidden = dot(normed_ref[...].reshape(tokens, D), weight[:, channels])
        for p in range(0, tokens, CHUNK):
            r, here = p // ROW, slice(p % ROW, p % ROW + CHUNK)
            values = hidden[p : p + CHUNK]
            squares, gate = gelu_gate(values)
            content_ref[r, here, channels] = (values * gate).astype(BF16)
            slope_ref[r, here, channels] = gelu_slope(values, squares, gate).astype(BF16)
        return carry

    lax.fori_loop(0, HALF // WIDTH, do_channels, 0)


def content_down_kernel(
    tree, count, members, lens_ref, content_ref, content_slope_ref, mixed_ref, own_ref, core_ref, side_ref, forward_ref, *refs
):
    parts = [core_ref.at[1], side_ref.at[0, 1], forward_ref.at[1, 1]]
    sources = refs[:count]
    gated_ref, grad_ref, grad_mixed_ref, bias_ref, shrink = refs[count : count + 5]
    raws = refs[count + 5 : count + (8 if tree else 6)]
    cots, sums, tall_sum, sems = refs[count + 5 + len(raws) :]
    narrow = lax.axis_index("narrow")
    rows_here, quarter = core_ref.shape[1:3]
    tokens = rows_here * ROW

    if tree:
        fetch_weights(sources, [(0, k * D, D, shrink, 192, 96, k * 32, sems.at[0]) for k in range(3)], tree)
    else:
        pltpu.make_async_copy(sources[0], shrink, sems.at[0]).start()
    for r in range(rows_here):
        for j in range(members):
            source = own_ref.at[narrow * rows_here + r] if j == 0 else parts[j - 1].at[r]
            place = run(r * ROW + (narrow ^ j) * quarter, quarter)
            pltpu.make_async_copy(source, cots.at[place, :], sems.at[1]).start()
    sums[...] = jnp.zeros_like(sums)
    wait_weights([(shrink, sems.at[0]), (cots, sems.at[1])])

    def do_channels(k, carry):
        channels = run(k * WIDTH, WIDTH)
        grad_gated = dot(cots[...], shrink[channels, :], ((1,), (1,)))
        for p in range(0, tokens, CHUNK):
            r, here = p // ROW, slice(p % ROW, p % ROW + CHUNK)
            grads = grad_gated[p : p + CHUNK].astype(BF16)
            content = content_ref[r, here, channels]
            mixed = mixed_ref[r, here, channels]
            gated_ref[r, here, channels] = content * mixed
            grad_ref[r, here, channels] = grads * (mixed * content_slope_ref[r, here, channels])
            grad_mixed = grads * content
            grad_mixed_ref[r, here, channels] = grad_mixed
            total = grad_mixed.astype(F32)
            sums[p : p + CHUNK, :] += total[:, :LANES] + total[:, LANES:]
        tall_sum[channels, :] = dot(gated_ref[:, :, channels].reshape(tokens, WIDTH), cots[...], ((0,), (0,)))
        return carry

    lax.fori_loop(0, HALF // WIDTH, do_channels, 0)
    for r in range(rows_here):
        _, live = doc_mask(0, ROW, lens_ref, narrow * rows_here + r)
        part = jnp.where(live, sums[r * ROW : (r + 1) * ROW, :], 0.0)
        bias_ref[...] = part if r == 0 else bias_ref[...] + part
    if tree:
        for j in range(3):
            emit_blocks("y", reader(tall_sum, 192, 48, j * BLOCK, slice(0, D)), D, j * D, *raws)
    else:
        raws[0][...] = tall_sum[...]


def content_sum_kernel(tree, normed_ref, grad_ref, *refs):
    raws, normed_turned, wide_sum = refs[:-2], refs[-2], refs[-1]
    tokens = normed_ref.shape[0] * normed_ref.shape[1]
    normed_turned[...] = normed_ref[...].reshape(tokens, D).T
    for c in range(0, HALF, D):
        wide_sum[...] = dot(normed_turned[...], grad_ref[:, :, c : c + D].reshape(tokens, D))
        if tree:
            emit_blocks("x", reader(wide_sum, 64, 16, 0, slice(0, D)), D, c, *raws)
        else:
            raws[0][:, c : c + D] = wide_sum[...]


def spatial_sum_kernel(lens_ref, grad_mixed_ref, gate_ref, square_ref):
    rows_here = grad_mixed_ref.shape[0]
    narrow = lax.axis_index("narrow")
    for row in range(rows_here):
        same, _ = doc_mask(0, ROW, lens_ref, narrow * rows_here + row)
        products = jnp.where(same, dot(grad_mixed_ref[row], gate_ref[row], ((1,), (1,))), 0.0)
        square_ref[...] = products if row == 0 else square_ref[...] + products


def gate_back_kernel(
    lens_ref, grad_mixed_ref, gate_ref, slope_ref, rstd_ref, spatial_ref, gains_ref, bias_ref,
    grad_ref, vectors_ref, turned, grad_gate, first_sums, second_sums, second, inverse, gains_low, inverse_low,
):
    rows_here = grad_mixed_ref.shape[0]
    narrow = lax.axis_index("narrow")
    turned[...] = spatial_ref[...].T
    second[...] = jnp.zeros_like(second)
    inverse[...] = 1.0 / gains_ref[:, D:]
    gains_low[...] = jnp.broadcast_to(gains_ref[0:1, D:], (BLOCK, HALF)).astype(BF16)
    inverse_low[...] = jnp.broadcast_to(inverse[0:1, :], (BLOCK, HALF)).astype(BF16)

    def do_row(row, carry):
        same, _ = doc_mask(0, ROW, lens_ref, narrow * rows_here + row)
        masked = jnp.where(same, turned[...], jnp.zeros((), BF16))
        for c in range(0, HALF, WIDTH):
            grads_all = dot(masked, grad_mixed_ref[row, :, c : c + WIDTH])
            vector = jnp.zeros((8, WIDTH), F32)
            for p in range(0, ROW, CHUNK):
                here = slice(p, p + CHUNK)
                low = grads_all[here].astype(BF16)
                grad_gate[here, c : c + WIDTH] = low
                products = (low * gate_ref[row, here, c : c + WIDTH]).astype(F32)
                vector = vector + jnp.sum(products.reshape(CHUNK // 8, 8, WIDTH), axis=0)
                scaled = (low * gains_low[0:1, c : c + WIDTH]).astype(F32)
                first = scaled[:, :LANES] + scaled[:, LANES:]
                other = products[:, :LANES] + products[:, LANES:]
                first_sums[here, :] = first if c == 0 else first_sums[here, :] + first
                second_sums[here, :] = other if c == 0 else second_sums[here, :] + other
            second[:, c : c + WIDTH] += vector
        for p in range(0, ROW, CHUNK):
            here = slice(p, p + CHUNK)
            scale = rstd_ref[row, here, 0:1]
            first_mean = jnp.sum(first_sums[here, :], axis=1, keepdims=True) * (1.0 / HALF) * scale
            second_mean = jnp.sum(second_sums[here, :], axis=1, keepdims=True) * (1.0 / HALF) * scale
            wide_row = lambda value: jnp.broadcast_to(value, (CHUNK, LANES)).astype(BF16)
            scale, first_mean, second_mean = wide_row(scale), wide_row(first_mean), wide_row(second_mean)
            for c in range(0, HALF, LANES):
                place = slice(c, c + LANES)
                scaled = grad_gate[here, place] * gains_low[0:1, place] * scale
                vhat = gate_ref[row, here, place] * inverse_low[0:1, place]
                grad_ref[row, here, place] = (scaled - first_mean - vhat * second_mean) * slope_ref[row, here, place]
        return carry

    lax.fori_loop(0, rows_here, do_row, 0)
    vectors_ref[...] = jnp.zeros_like(vectors_ref)
    diagonal = lax.broadcasted_iota(jnp.int32, (64, 128), 0) == lax.broadcasted_iota(jnp.int32, (64, 128), 1)
    for owner in range(8):
        for k in range(2 if owner >= 2 else 0):
            c = (owner - 2) * 256 + k * 128
            total = jnp.sum(second[:, c : c + 128], axis=0, keepdims=True)
            vectors_ref[owner, k : k + 1, :] = total * inverse[0:1, c : c + 128]
        column = jnp.sum(bias_ref[owner * 64 : (owner + 1) * 64, :], axis=1, keepdims=True)
        vectors_ref[owner, 2:3, :] = jnp.sum(jnp.where(diagonal, column, 0.0), axis=0, keepdims=True)


def gate_sum_kernel(tree, normed_ref, grad_ref, square_ref, vectors_ref, *refs):
    raws, normed_turned, wide_sum = refs[:-2], refs[-2], refs[-1]
    tokens = normed_ref.shape[0] * normed_ref.shape[1]
    rest = HALF - SPLIT
    normed_turned[...] = normed_ref[...].reshape(tokens, D).T
    if tree:
        emit_blocks("y", reader(square_ref, 64, 16, 0, slice(0, ROW)), ROW, rest, *raws[3:])
        emit_blocks("y", lambda owner, member: vectors_ref[owner], VECTOR_LANES, rest + ROW, *raws[3:])
    else:
        raws[1][...] = square_ref[...]
        raws[2][...] = vectors_ref[...]
    for c in range(0, HALF, D):
        wide_sum[...] = dot(normed_turned[...], grad_ref[:, :, c : c + D].reshape(tokens, D))
        if not tree:
            raws[0][:, c : c + D] = wide_sum[...]
        elif c < SPLIT:
            emit_blocks("x", reader(wide_sum, 64, 16, 0, slice(0, D)), D, c, *raws[:3])
        else:
            emit_blocks("y", reader(wide_sum, 64, 16, 0, slice(0, D)), D, c - SPLIT, *raws[3:])


def layer_kernel(gated_ref, shrink, own_ref, core_ref, pair_ref, total):
    members, rows_here, quarter = total.shape[:3]
    narrow = lax.axis_index("narrow")
    for row in range(rows_here):
        added = dot(gated_ref[row], shrink[...])
        for member in range(members):
            total[member ^ narrow, row] = added[member * quarter : (member + 1) * quarter].astype(BF16)
    own_ref[...] = total[0]
    core_ref[...] = total[1]
    pair_ref[0] = total[2]
    pair_ref[1] = total[3]


def back_kernel(
    gate_grad_ref, content_grad_ref, gate_weight, weight, xhat_ref, scale_ref, gains_ref, layer_core, layer_pair,
    own_ref, core_ref, pair_ref, total,
):
    members, rows_here, quarter = total.shape[:3]
    narrow = lax.axis_index("narrow")
    for row in range(rows_here):
        grad_normed = dot(gate_grad_ref[row], gate_weight[...], ((1,), (1,))) + dot(
            content_grad_ref[row], weight[...], ((1,), (1,))
        )
        for member in range(members):
            here = slice(member * quarter, (member + 1) * quarter)
            xhat = xhat_ref[row, here, :].astype(F32)
            scaled = grad_normed[here] * gains_ref[0:1, :D]
            first_mean = jnp.mean(scaled, axis=1, keepdims=True)
            second_mean = jnp.mean(scaled * xhat, axis=1, keepdims=True)
            scale = scale_ref[row, here, 0:1]
            total[member ^ narrow, row] = ((scaled - first_mean - xhat * second_mean) * scale).astype(BF16)
    own_ref[...] = total[0]
    core_ref[0] = total[1]
    core_ref[1] = layer_core[...]
    for j in range(2):
        pair_ref[j, 0] = total[2 + j]
        pair_ref[j, 1] = layer_pair[j]


def give_kernel(
    cots_ref, acts_ref, grad_own, layer_own, core_ref, side_ref, forward_ref, grad_out, layer_out, grads, layers, sems
):
    rows_here = grad_own.shape[0]
    narrow = lax.axis_index("narrow")
    stores = []
    for kind, (base, own, total, out) in enumerate(
        ((cots_ref, grad_own, grads, grad_out), (acts_ref, layer_own, layers, layer_out))
    ):
        parts = [own, core_ref.at[kind], side_ref.at[0, kind], forward_ref.at[1, kind]]
        for j, part in enumerate(parts):
            rows = pl.ds((narrow ^ j) * rows_here, rows_here)
            total[j] = (base[rows].astype(F32) + part[...].astype(F32)).astype(total.dtype)
            stores.append(pltpu.make_async_copy(total.at[j], out.at[rows], sems.at[kind, j]))
            stores[-1].start()
    for store in stores:
        store.wait()


def sum_three(near_ref, came_ref, far_ref, half, columns):
    values = near_ref[half, :, :, columns].astype(F32) + came_ref[0, half, :, :, columns].astype(F32)
    return values + far_ref[half, :, :, columns].astype(F32)


def side_kernel(*refs):
    for i, out_ref in enumerate(refs[6:]):
        near, came, far = refs[3 * i : 3 * i + 3]
        for c in range(0, near.shape[3], LANES):
            out_ref[:, :, c : c + LANES] = sum_three(near, came, far, 1, slice(c, c + LANES)).astype(BF16)


def fold_kernel(*refs):
    sides, outputs = refs[12:16], refs[16:]
    first = 0
    for i in range(4):
        near, came, far = refs[3 * i : 3 * i + 3]
        for c in range(0, near.shape[3], LANES):
            place = slice(c, c + LANES)
            total = sum_three(near, came, far, 0, place) + sides[i][:, :, place].astype(F32)
            there = slice(first + c, first + c + LANES)
            outputs[0][:, there] = total[0]
            for step in range(1, 4):
                outputs[step][:, there] = total[step].astype(BF16)
        first += near.shape[3]


def norm_kernel(mine_ref, one_ref, two_ref, three_ref, weight_ref, gains_ref, low_ref, message_ref):
    wide, narrow = lax.axis_index("wide"), lax.axis_index("narrow")
    columns = mine_ref.shape[1]
    squares = jnp.zeros((BLOCK, LANES), F32)
    products = jnp.zeros((BLOCK, LANES), F32)
    here = run(narrow * BLOCK, BLOCK)
    for c in range(0, columns, LANES):
        place = slice(c, c + LANES)
        total = mine_ref[:, place]
        for ref in (one_ref, two_ref, three_ref):
            total = total + ref[:, place].astype(F32)
        low = total.astype(BF16)
        low_ref[:, place] = low
        value = low.astype(F32)
        square = value * value
        squares = squares + (square if c < columns - LANES else jnp.where(narrow == 0, square, 0.0))
        at = expand_column(c)
        if at is not None:
            weight = weight_ref[here, at : at + LANES].astype(BF16).astype(F32)
            products = products + value * weight
    first = wide * 64 + narrow * BLOCK
    lanes = lax.broadcasted_iota(jnp.int32, (BLOCK, D), 1)
    diagonal = lanes == lax.broadcasted_iota(jnp.int32, (BLOCK, D), 0) + first
    gain = jnp.sum(jnp.where(diagonal, gains_ref[0:1, :D], 0.0), axis=1, keepdims=True)
    first_raw = jnp.sum(products, axis=1, keepdims=True) / gain
    total = jnp.sum(squares) + jnp.sum(first_raw * first_raw)
    places = jnp.sum(jnp.where(diagonal, first_raw, 0.0), axis=0, keepdims=True)
    message_ref[...] = jnp.full(message_ref.shape, total, F32)
    for k in range(D // LANES):
        message_ref[k : k + 1, :] = places[:, k * LANES : (k + 1) * LANES]


def expand_column(c):
    right = HALF + SPLIT
    turn = right + HALF
    if c < right:
        return c
    if turn <= c < turn + HALF - SPLIT:
        return c - HALF
    return None


def adam_kernel(message_ref, own_ref, side_ref, other_ref, *refs):
    states, vectors, outputs, vector_outputs, norm_ref = refs[:12], refs[12:20], refs[20:35], refs[35:45], refs[45]
    results, blocks, sem = refs[46:61], refs[61], refs[62]
    wide, narrow = lax.axis_index("wide"), lax.axis_index("narrow")
    norm = jnp.sqrt(message_ref[4:5, :])
    norm_ref[0, 0] = jnp.max(norm)
    clip = CLIP_LIMIT / jnp.maximum(norm, CLIP_LIMIT)
    right = HALF + SPLIT
    turn = right + HALF
    blocks[narrow] = own_ref[...]
    blocks[narrow ^ 1] = other_ref[0]
    blocks[narrow ^ 2] = side_ref[...]
    blocks[narrow ^ 3] = other_ref[1]

    def update(which, gradient, rows, place):
        weight, momentum, variance, average = [ref[rows, place] for ref in states[4 * which : 4 * which + 4]]
        updates = adam_update(
            weight, gradient.astype(F32), momentum, variance, average, clip, RATE_MATRIX, DECAY_MATRIX
        )
        for ref, value in zip(results[5 * which : 5 * which + 5], updates):
            ref[rows, place] = value

    def do_member(member, carry):
        thin = run(member * BLOCK, BLOCK)
        for c in range(0, turn + HALF - SPLIT + ROW, LANES):
            gradient = blocks[member, :, c : c + LANES]
            at = expand_column(c)
            if at is not None:
                update(0, gradient, thin, slice(at, at + LANES))
            elif c < turn:
                k, at = (c - right) // D, (c - right) % D
                update(1, gradient, run(member * 48 + k * BLOCK, BLOCK), slice(at, at + LANES))
            else:
                at = c - turn - (HALF - SPLIT)
                update(2, gradient, thin, slice(at, at + LANES))
        for i in range(15):
            rows = run(member * 48, 48) if 5 <= i < 10 else thin
            pltpu.make_async_copy(results[i].at[rows, :], outputs[i].at[rows, :], sem.at[i]).start()
        return carry

    lax.fori_loop(0, 4, do_member, 0)
    own = blocks[0, :, turn + HALF - SPLIT + ROW :].astype(F32)
    gains = jnp.where(wide == 0, message_ref[0:2, :], jnp.where(wide == 1, message_ref[2:4, :], own[0:2, :]))
    for which, gradient in ((0, gains), (1, own[2:3, :64])):
        weight, momentum, variance, average = [ref[...] for ref in vectors[4 * which : 4 * which + 4]]
        updates = adam_update(
            weight, gradient, momentum, variance, average, clip[:, : gradient.shape[1]], RATE_VECTOR, 0.0
        )
        for ref, value in zip(vector_outputs[5 * which : 5 * which + 5], updates):
            ref[...] = value
    for i in range(15):
        pltpu.make_async_copy(results[i], outputs[i], sem.at[i]).wait()


def call_kernel(kernel, name, args, in_specs, out_types, scratch, flops, limit=VMEM_LIMIT):
    vmem = pl.BlockSpec(memory_space=pltpu.VMEM)
    specs = [kind[1] if isinstance(kind, tuple) else vmem for kind in out_types]
    types = [
        kind[0] if isinstance(kind, tuple) else pltpu.VMEM(kind.shape, kind.dtype) for kind in out_types
    ]
    in_specs = [vmem if spec is None else spec for spec in in_specs]
    args = [
        pltpu.with_memory_space_constraint(value, pltpu.HBM) if spec.memory_space == pltpu.HBM else value
        for value, spec in zip(args, in_specs)
    ]
    results = pl.pallas_call(
        kernel,
        name=name,
        in_specs=in_specs,
        out_specs=specs,
        out_shape=types,
        scratch_shapes=scratch,
        compiler_params=pltpu.CompilerParams(vmem_limit_bytes=limit),
        cost_estimate=pl.CostEstimate(flops=int(flops), bytes_accessed=int(flops / 500), transcendentals=0),
    )(*args)
    return list(results)


def swap_with(value, axis, size, bit):
    return lax.ppermute(value, axis, [(i, i ^ bit) for i in range(size)])


def after(value, *others):
    return lax.optimization_barrier((value,) + others)[0]


def sum_core(keep_far, came):
    return (keep_far.astype(F32) + came[1].astype(F32)).astype(BF16)


def adam_update(weight, gradient, momentum, variance, average, clip_scale, step_rate, decay_rate):
    ema_rate = min(EMA_DECAY, (1.0 + STEP) / (10.0 + STEP))
    clipped = clip_scale * gradient
    moment = BETA_FIRST * momentum + (1.0 - BETA_FIRST) * clipped
    square = BETA_SECOND * variance + (1.0 - BETA_SECOND) * clipped * clipped
    first_hat = moment * (1.0 / (1.0 - BETA_FIRST**STEP))
    second_hat = square * (1.0 / (1.0 - BETA_SECOND**STEP))
    updated = weight - step_rate * (
        first_hat / (jnp.sqrt(second_hat) + ADAM_EPS) + decay_rate * weight
    )
    smoothed = ema_rate * average + (1.0 - ema_rate) * updated
    return (clipped, moment, square, updated, smoothed)


def on_device(
    activations,
    cotangent,
    doc_lengths,
    expand_weight,
    expand_momentum,
    expand_variance,
    expand_average,
    shrink_weight,
    shrink_momentum,
    shrink_variance,
    shrink_average,
    spatial_weight,
    spatial_momentum,
    spatial_variance,
    spatial_average,
    norm_gains,
    gains_momentum,
    gains_variance,
    gains_average,
    spatial_bias,
    bias_momentum,
    bias_variance,
    bias_average,
):
    narrow_size, wide_size = lax.axis_size("narrow"), lax.axis_size("wide")
    wide, narrow = lax.axis_index("wide"), lax.axis_index("narrow")
    group_rows, quarter = activations.shape[0], activations.shape[1]
    rows = group_rows // narrow_size
    tokens = rows * ROW
    tree = (wide_size, narrow_size) == (8, 4)
    smem = pl.BlockSpec(memory_space=pltpu.SMEM)
    anywhere = pl.BlockSpec(memory_space=pl.ANY)
    stored = pl.BlockSpec(memory_space=pltpu.HBM)
    shape = jax.ShapeDtypeStruct
    dma = pltpu.SemaphoreType.DMA
    part = shape((rows, quarter, D), BF16)
    product = 2 * tokens * HALF * D
    cross_x = lambda value: swap_with(value, "wide", wide_size, 1)
    cross_y = lambda value: swap_with(value, "narrow", narrow_size, 2)
    cross_core = lambda value: swap_with(value, "narrow", narrow_size, 1)

    def trade(core_part, pair):
        side = cross_y(pair)
        return [cross_core(core_part), side, cross_core(side)]

    def stack(values):
        kind = shape((len(values), *values[0].shape), values[0].dtype)
        return call_kernel(stack_kernel, "stack", values, [None] * len(values), [kind], [], product // 64)[0]

    def add(*values):
        kind = shape(values[0].shape, values[0].dtype)
        return call_kernel(add_kernel, "add", values, [None] * len(values), [kind], [], product // 64)[0]

    pair = shape((2, *part.shape), BF16)

    def cut(acts, cots):
        return call_kernel(
            cut_kernel,
            "cut",
            [acts, cots],
            [stored] * 2,
            [(pair, stored), (shape((2, *pair.shape), BF16), stored)],
            [dma((6,))],
            product // 64,
        )

    if tree:
        first_own = call_kernel(
            pack_first_kernel,
            "pack_first",
            [expand_weight, spatial_weight, norm_gains.reshape(2, LANES), spatial_bias.reshape(1, 64)],
            [stored] * 4,
            [shape((32, HALF + ROW + VECTOR_LANES), BF16)],
            [pltpu.VMEM((32, HALF), F32), pltpu.VMEM((32, ROW), F32), pltpu.VMEM((2, LANES), F32)]
            + [pltpu.VMEM((1, 64), F32), dma((4,))],
            product // 64,
        )[0]
        over_z = lambda own: [swap_with(own, "wide", wide_size, 2 * s) for s in range(1, 4)]
        came_z = over_z(first_own)
        core_cut, pair_cut = cut(after(activations, first_own), cotangent)
        side_came = cross_y(pair_cut)
        expand_own, shrink_own = call_kernel(
            pack_second_kernel,
            "pack_second",
            [expand_weight, shrink_weight],
            [stored, stored],
            [shape((32, HALF), BF16)] * 2,
            [pltpu.VMEM((32, HALF), F32), pltpu.VMEM((96, D), F32), dma((2,))],
            product // 64,
        )
        *came_z, core_came, _, expand_own = lax.optimization_barrier(
            (*came_z, cross_core(core_cut), pair_cut, expand_own)
        )
        first_near = stack([first_own, *came_z])
        first_across = cross_x(first_near)
        expand_own = after(expand_own, first_near)
        *came_z, side_came = lax.optimization_barrier((*over_z(expand_own), side_came))
        expand_near = stack([expand_own, *came_z])
        expand_across = cross_x(after(expand_near, first_across))
        shrink_own = after(shrink_own, expand_near)
        shrink_came = over_z(shrink_own)
        near_core = cross_core(after(first_near, expand_near))
        across_core = cross_core(after(first_across, expand_near))
        forward_came = cross_core(after(side_came, expand_near))
        first_pieces = [after(first_near, expand_near), first_across, near_core, across_core]
        small_pieces = first_pieces[:2]
        near_other = cross_core(expand_near)
        count = len(PIECES)
    else:
        gather = lambda value: lax.all_gather(value.astype(BF16), "wide", axis=0, tiled=True)
        expand_low = gather(expand_weight)
        gains_low, bias_low = gather(norm_gains), gather(spatial_bias)
        small = jnp.concatenate(
            [
                gains_low.reshape(8, 2, 128),
                jnp.pad(bias_low.reshape(8, 1, 64), ((0, 0), (0, 0), (0, 64))),
                jnp.zeros((8, 13, 128), BF16),
            ],
            axis=1,
        )
        first_pieces = [expand_low[:, HALF:], gather(spatial_weight)]
        small_pieces = [small, small]
        expand_pieces, shrink_pieces = [expand_low[:, :HALF]], [gather(shrink_weight)]
        core_came, side_came, forward_came = trade(*cut(activations, cotangent))
        count = 2

    low_d, low_half = shape((rows, ROW, D), BF16), shape((rows, ROW, HALF), BF16)
    thin = shape((rows, ROW, 128), F32)
    weight_type = shape((D, HALF), BF16)

    normed, xhat, scale, gate_normed, slope, rstd, spatial_low, gains, bias_col, gate_weight = call_kernel(
        functools.partial(gating_kernel, tree, count, narrow_size),
        "gating",
        [activations, core_came, side_came, forward_came] + list(first_pieces) + list(small_pieces),
        [stored] + [anywhere] * (narrow_size - 1 + count + 2),
        [low_d, low_d, thin, low_half, low_half, thin]
        + [shape((ROW, ROW), BF16), shape((8, D + HALF), F32), shape((ROW, 128), F32), weight_type],
        [
            pltpu.VMEM((8, BLOCK, 128), BF16),
            pltpu.VMEM((narrow_size, *part.shape), BF16),
            pltpu.VMEM((ROW, HALF), F32),
            pltpu.VMEM((ROW, 128), F32),
            dma((4,)),
        ],
        product // 64,
    )

    bias_late = bias_col
    if tree:
        *shrink_came, expand_across, _ = lax.optimization_barrier((*shrink_came, expand_across, normed))
        shrink_near = stack([shrink_own, *shrink_came])
        shrink_across = cross_x(shrink_near)
        expand_pieces = [expand_near, expand_across, near_other, cross_core(expand_across)]
        bias_late = after(bias_col, shrink_near)
    mixed = call_kernel(
        mixing_kernel,
        "mixing",
        [doc_lengths, spatial_low, gate_normed, bias_late],
        [smem] + [None] * 3,
        [low_half],
        [],
        product // 64,
    )[0]
    normed_late = normed
    if tree:
        expand_pieces[3], normed_late, _ = lax.optimization_barrier((expand_pieces[3], normed, mixed))
    content, content_slope, content_weight = call_kernel(
        functools.partial(content_up_kernel, tree),
        "content_up",
        [normed_late, *expand_pieces],
        [None] + [anywhere] * len(expand_pieces),
        [low_half, low_half, weight_type],
        [dma(())],
        product // 64,
    )
    if tree:
        shrink_across, _ = lax.optimization_barrier((shrink_across, content))
        shrink_pieces = [shrink_near, shrink_across, cross_core(shrink_near), cross_core(shrink_across)]

    def raw_outputs(column_list, plain):
        if tree:
            return [
                shape(size, BF16)
                for columns in column_list
                for size in ((2, 4, BLOCK, columns), (2, 4, BLOCK, columns), (2, 2, 4, BLOCK, columns))
            ]
        return [shape(size, F32) for size in plain]

    gated, content_grad, grad_mixed, bias_part, shrink_low, *shrink_raws = call_kernel(
        functools.partial(content_down_kernel, tree, len(shrink_pieces), narrow_size),
        "content_down",
        [doc_lengths, content, content_slope, mixed, cotangent, core_came, side_came, forward_came, *shrink_pieces],
        [smem, None, None, None, stored] + [anywhere] * (narrow_size - 1 + len(shrink_pieces)),
        [low_half, low_half, low_half, shape((ROW, 128), F32), shape((HALF, D), BF16)]
        + raw_outputs((HALF,), ((HALF, D),)),
        [
            pltpu.VMEM((tokens, D), BF16),
            pltpu.VMEM((tokens, 128), F32),
            pltpu.VMEM((HALF, D), F32),
            dma((2,)),
        ],
        product // 64,
    )
    if tree:
        came = {"shrink": cross_core(shrink_raws[2])}
    sum_scratch = [pltpu.VMEM((D, tokens), BF16), pltpu.VMEM((D, D), F32)]
    content_raws = call_kernel(
        functools.partial(content_sum_kernel, tree),
        "content_sum",
        [normed, content_grad],
        [None] * 2,
        raw_outputs((HALF,), ((D, HALF),)),
        sum_scratch,
        product // 64,
    )
    mixed_late = grad_mixed
    if tree:
        came["shrink"], content_raws[0] = lax.optimization_barrier((came["shrink"], content_raws[0]))
        came["content"] = cross_core(content_raws[2])
        far = {"shrink": sum_core(shrink_raws[1], came["shrink"])}
        came_far = {"shrink": cross_y(far["shrink"])}
        mixed_late = after(grad_mixed, far["shrink"])
    square_sum = call_kernel(
        spatial_sum_kernel,
        "spatial_sum",
        [doc_lengths, mixed_late, gate_normed],
        [smem, None, None],
        [shape((ROW, ROW), F32)],
        [],
        product // 64,
    )[0]
    if tree:
        came["content"], square_sum = lax.optimization_barrier((came["content"], square_sum))
        far["content"] = sum_core(content_raws[1], came["content"])
        came_far["content"] = cross_x(far["content"])
        mixed_late = after(grad_mixed, far["content"])

    gate_grad, vectors = call_kernel(
        gate_back_kernel,
        "gate_back",
        [doc_lengths, mixed_late, gate_normed, slope, rstd, spatial_low, gains, bias_part],
        [smem] + [None] * 7,
        [low_half, shape((8, BLOCK, 128), F32)],
        [
            pltpu.VMEM((ROW, ROW), BF16),
            pltpu.VMEM((ROW, HALF), BF16),
            pltpu.VMEM((ROW, 128), F32),
            pltpu.VMEM((ROW, 128), F32),
            pltpu.VMEM((8, HALF), F32),
            pltpu.VMEM((8, HALF), F32),
            pltpu.VMEM((BLOCK, HALF), BF16),
            pltpu.VMEM((BLOCK, HALF), BF16),
        ],
        product // 64,
    )
    normed_late = normed
    if tree:
        came_far["shrink"], normed_late = lax.optimization_barrier((came_far["shrink"], normed))
    second_raws = call_kernel(
        functools.partial(gate_sum_kernel, tree),
        "gate_sum",
        [normed_late, gate_grad, square_sum, vectors],
        [None] * 4,
        raw_outputs((SPLIT, HALF - SPLIT + ROW + VECTOR_LANES), ((D, HALF), (ROW, ROW), (8, BLOCK, 128))),
        sum_scratch,
        product // 64,
    )
    def side_step(terms, widths):
        kinds = [shape((4, BLOCK, width), BF16) for width in widths]
        return call_kernel(side_kernel, "side", terms, [None] * 6, kinds, [], product // 64)

    gated_late = gated
    if tree:
        second_raws[2], second_raws[5], came_far["content"] = lax.optimization_barrier(
            (second_raws[2], second_raws[5], came_far["content"])
        )
        second_came = [cross_core(second_raws[i]) for i in (2, 5)]
        first_terms = [content_raws[0], came["content"], came_far["content"]]
        first_terms += [shrink_raws[0], came["shrink"], came_far["shrink"]]
        first_sides = side_step(first_terms, (HALF, HALF))
        first_came_side = [cross_y(first_sides[0]), cross_x(first_sides[1])]
        gated_late = after(gated, second_raws[0], *first_sides)
    part_scratch = pltpu.VMEM((narrow_size, *part.shape), BF16)
    layer_own, layer_core, layer_pair = call_kernel(
        layer_kernel,
        "layer",
        [gated_late, shrink_low],
        [None] * 2,
        [part, part, pair],
        [part_scratch],
        product // 64,
    )
    grad_late = gate_grad
    if tree:
        *second_came, layer_own = lax.optimization_barrier((*second_came, layer_own))
        second_far = [sum_core(second_raws[1], second_came[0]), sum_core(second_raws[4], second_came[1])]
        second_came_far = [cross_x(second_far[0]), cross_y(second_far[1])]
        grad_late = after(gate_grad, *second_far)
    grad_own, core_back, pair_back = call_kernel(
        back_kernel,
        "back",
        [grad_late, content_grad, gate_weight, content_weight, xhat, scale, gains, layer_core, layer_pair],
        [None] * 9,
        [part, pair, shape((2, *pair.shape), BF16)],
        [part_scratch],
        product // 64,
    )

    def give(cots_base, acts_base, returned):
        whole = (group_rows, quarter, D)
        return call_kernel(
            give_kernel,
            "give",
            [cots_base, acts_base, grad_own, layer_own, *returned],
            [None] * 7,
            [(shape(whole, F32), stored), (shape(whole, BF16), stored)],
            [
                pltpu.VMEM((narrow_size, *part.shape), F32),
                pltpu.VMEM((narrow_size, *part.shape), BF16),
                dma((2, narrow_size)),
            ],
            product // 64,
        )

    if tree:
        columns = HALF + HALF + SPLIT + (HALF - SPLIT) + ROW + VECTOR_LANES
        tied = lax.optimization_barrier((*second_came_far, *first_came_side, grad_own))
        second_came_far, first_came_side, grad_own = tied[:2], tied[2:4], tied[4]
        second_terms = [second_raws[0], second_came[0], second_came_far[0]]
        second_terms += [second_raws[3], second_came[1], second_came_far[1]]
        second_sides = side_step(second_terms, (SPLIT, HALF - SPLIT + ROW + VECTOR_LANES))
        second_came_side = [cross_y(second_sides[0]), cross_x(second_sides[1])]
        terms = first_terms[:3] + second_terms[:3] + first_terms[3:] + second_terms[3:]
        came_side = [first_came_side[0], second_came_side[0], first_came_side[1], second_came_side[1]]
        mine, *sent = call_kernel(
            fold_kernel,
            "fold",
            terms + came_side,
            [None] * 16,
            [shape((BLOCK, columns), F32)] + [shape((BLOCK, columns), BF16)] * 3,
            [],
            product // 64,
        )
        came_z = [swap_with(sent[s - 1], "wide", wide_size, 2 * s) for s in range(1, 4)]
        matrices = [expand_weight, expand_momentum, expand_variance, expand_average]
        matrices += [shrink_weight, shrink_momentum, shrink_variance, shrink_average]
        matrices += [spatial_weight, spatial_momentum, spatial_variance, spatial_average]
        fetched = [*matrices, cotangent, activations]
        states = call_kernel(
            fetch_kernel,
            "fetch",
            list(lax.optimization_barrier((*fetched, sent[0]))[:14]),
            [stored] * 14,
            [shape(value.shape, value.dtype) for value in fetched],
            [dma((14,))],
            product // 64,
        )
        states, bases = states[:12], states[12:]
        side_back = cross_y(after(pair_back, sent[0]))
        core_back = cross_core(after(core_back, sent[0]))
        *came_z, first_state = lax.optimization_barrier((*came_z, states[0]))
        low, message = call_kernel(
            norm_kernel,
            "norm",
            [mine, *came_z, first_state, gains],
            [None] * 6,
            [shape((BLOCK, columns), BF16), shape((8, LANES), F32)],
            [],
            product // 64,
        )
        side = cross_y(low)
        message = add(message, cross_core(message))
        message = add(message, cross_x(message))
        *arrived, side, side_back = lax.optimization_barrier((*over_z(message), side, side_back))
        message = add(message, *arrived)
        other = cross_core(stack([low, side]))
        returned = [core_back, side_back, cross_core(side_back)]
        input_grad, layer_out = give(*bases, returned)
        arrived, layer_out, input_grad = lax.optimization_barrier((cross_y(message), layer_out, input_grad))
        message = add(message, arrived)
        as_rows = lambda value: value.reshape(-1, min(value.shape[0], LANES))
        vector_states = [norm_gains, gains_momentum, gains_variance, gains_average]
        vector_states += [spatial_bias, bias_momentum, bias_variance, bias_average]
        vector_kinds = [shape((2, LANES), F32)] * 5 + [shape((1, 64), F32)] * 5
        *updates, norm_row = call_kernel(
            adam_kernel,
            "adam",
            [message, low, side, other, *states] + [as_rows(value) for value in vector_states],
            [None] * 24,
            [(shape(value.shape, F32), stored) for value in (matrices[0], matrices[4], matrices[8]) for _ in range(5)]
            + [(kind, pl.BlockSpec(memory_space=pltpu.VMEM)) for kind in vector_kinds]
            + [(shape((1, 1), F32), smem)],
            [pltpu.VMEM(value.shape, F32) for value in (matrices[0], matrices[4], matrices[8]) for _ in range(5)]
            + [pltpu.VMEM((4, BLOCK, columns), BF16), dma((15,))],
            product // 64,
        )
        grad_norm = norm_row[0, 0]
        results = [layer_out, input_grad, grad_norm, *updates[:15]]
        return tuple(results + [value.reshape(-1) for value in updates[15:]])

    returned = trade(core_back, pair_back)
    input_grad, layer_out = give(cotangent, activations, returned)
    gains_size, bias_size = norm_gains.shape[0], spatial_bias.shape[0]
    vectors = lax.psum(second_raws[2], ("narrow", "wide"))
    totals = lax.psum(
        (jnp.concatenate([content_raws[0], second_raws[0]], axis=1), shrink_raws[0], second_raws[1]), "narrow"
    )
    expand_shard, shrink_shard, spatial_shard = [
        lax.psum_scatter(total, "wide", scatter_dimension=0, tiled=True) for total in totals
    ]
    second_shard = lax.dynamic_slice_in_dim(vectors[:, :2].reshape(-1), wide * gains_size, gains_size)
    bias_shard = lax.dynamic_slice_in_dim(vectors[:, 2, :64].reshape(-1), wide * bias_size, bias_size)
    low_weight = expand_weight.astype(BF16).astype(F32)
    height = expand_weight.shape[0]
    first_gain = lax.dynamic_slice_in_dim(gains[0], wide * height, height)
    first_raw = jnp.sum(low_weight * expand_shard, axis=1) / first_gain
    squares = [expand_shard, shrink_shard, spatial_shard, second_shard, bias_shard, first_raw]
    square_total = lax.psum(sum(jnp.sum(value * value) for value in squares), "wide")
    first_all = lax.all_gather(first_raw, "wide", axis=0, tiled=True)
    first_all = jnp.concatenate([first_all, jnp.zeros((HALF,), F32)])
    gains_shard = second_shard + lax.dynamic_slice_in_dim(first_all, wide * gains_size, gains_size)
    grad_norm = jnp.sqrt(square_total)
    clip_scale = CLIP_LIMIT / jnp.maximum(grad_norm, CLIP_LIMIT)
    results = [layer_out, input_grad, grad_norm]
    for weight, shard, momentum, variance, average, rate, decay in (
        (expand_weight, expand_shard, expand_momentum, expand_variance, expand_average, RATE_MATRIX, DECAY_MATRIX),
        (shrink_weight, shrink_shard, shrink_momentum, shrink_variance, shrink_average, RATE_MATRIX, DECAY_MATRIX),
        (spatial_weight, spatial_shard, spatial_momentum, spatial_variance, spatial_average, RATE_MATRIX, DECAY_MATRIX),
        (norm_gains, gains_shard, gains_momentum, gains_variance, gains_average, RATE_VECTOR, 0.0),
        (spatial_bias, bias_shard, bias_momentum, bias_variance, bias_average, RATE_VECTOR, 0.0),
    ):
        results += adam_update(weight, shard, momentum, variance, average, clip_scale, rate, decay)
    return tuple(results)


def solution(mesh):
    tokens, matrix, vector = P("wide", "narrow", None), P("wide", None), P("wide")
    return jax.shard_map(
        on_device,
        mesh=mesh,
        in_specs=(tokens, tokens) + (matrix,) * 13 + (vector,) * 8,
        out_specs=(tokens, tokens, P()) + (matrix,) * 15 + (vector,) * 10,
        check_vma=False,
    )
```

```python
import functools

import jax
import jax.numpy as jnp
from jax import lax
from jax.experimental import pallas as pl
from jax.experimental.pallas import tpu as pltpu
from jax.sharding import PartitionSpec as P

D = 512
FF = 3072
ROW = 512
DOCS = 5
STEP = 10
HALF = 1536

LAYER_EPS = 1e-05
CLIP_LIMIT = 1.0
BETA_FIRST = 0.9
BETA_SECOND = 0.999
ADAM_EPS = 1e-08
RATE_MATRIX = 0.03
RATE_VECTOR = 0.2
DECAY_MATRIX = 0.1
EMA_DECAY = 0.9999

F32 = jnp.float32
BF16 = jnp.bfloat16
GELU_A = 0.7978845608028654
GELU_B = GELU_A * 0.044715
LANES = 128
CHUNK = 64
PIECE = 32
BLOCK = 16
VMEM_LIMIT = 16 * 1024 * 1024

PIECES = ((0, 0), (1, 0), (0, 1), (1, 1))
WIDTH = 256
SPLIT = 1024
VECTOR_LANES = 128


def gelu_gate(hidden):
    squares = hidden * hidden
    gate = 0.5 * jnp.tanh(hidden * (GELU_A + GELU_B * squares)) + 0.5
    return squares, gate


def gelu_slope(hidden, squares, gate):
    return gate * (1.0 + hidden * (1.0 - gate) * (2.0 * GELU_A + 6.0 * GELU_B * squares))


def doc_ids(places, lens_ref, row):
    bound = jnp.int32(0)
    ids = jnp.zeros(places.shape, jnp.int32)
    for k in range(DOCS - 1):
        bound = bound + lens_ref[row, k]
        ids = ids + (places >= bound).astype(jnp.int32)
    return ids


def doc_mask(start, rows, lens_ref, row):
    across = doc_ids(lax.broadcasted_iota(jnp.int32, (1, ROW), 1), lens_ref, row)
    down = doc_ids(lax.broadcasted_iota(jnp.int32, (rows, 1), 0) + start, lens_ref, row)
    live = down != DOCS - 1
    return jnp.where(live, down, -1) == across, live


def dot(left, right, dims=((1,), (0,))):
    return lax.dot_general(left, right, (dims, ((), ())), preferred_element_type=F32)


def run(start, size):
    return pl.ds(pl.multiple_of(start, size), size)


def fetch_weights(sources, moves, tree):
    if not tree:
        for source, (_, _, _, target, _, _, _, sem) in zip(sources, moves):
            pltpu.make_async_copy(source, target, sem).start()
        return
    wide, core = lax.axis_index("wide"), lax.axis_index("narrow") & 1
    for base, first, count, target, height, unit, shift, sem in moves:
        for i, (x_off, core_off) in enumerate(PIECES):
            for step in range(4):
                start = (wide ^ (2 * step + x_off)) * height + (core ^ core_off) * unit + shift
                pltpu.make_async_copy(
                    sources[base + i].at[step, :, pl.ds(first, count)], target.at[run(start, 32), :], sem
                ).start()


def wait_weights(targets):
    for target, sem in targets:
        pltpu.make_async_copy(target, target, sem).wait()


def cut_kernel(acts_ref, cots_ref, core_out, pair_out, sems):
    rows_here = core_out.shape[1]
    narrow = lax.axis_index("narrow")
    copies = []
    for i, ref in enumerate((acts_ref, cots_ref)):
        for j, target in ((1, core_out.at[i]), (2, pair_out.at[0, i]), (3, pair_out.at[1, i])):
            source = ref.at[pl.ds((narrow ^ j) * rows_here, rows_here)]
            copies.append(pltpu.make_async_copy(source, target, sems.at[len(copies)]))
    for copy in copies:
        copy.start()
    for copy in copies:
        copy.wait()


def pack_first_kernel(expand_ref, spatial_ref, gains_ref, bias_ref, out_ref, expand, spatial, gains, bias, sems):
    rows = run((lax.axis_index("narrow") & 1) * 32, 32)
    copies = [
        pltpu.make_async_copy(expand_ref.at[rows, pl.ds(HALF, HALF)], expand, sems.at[0]),
        pltpu.make_async_copy(spatial_ref.at[rows, :], spatial, sems.at[1]),
        pltpu.make_async_copy(gains_ref, gains, sems.at[2]),
        pltpu.make_async_copy(bias_ref, bias, sems.at[3]),
    ]
    for copy in copies:
        copy.start()
    for copy in copies:
        copy.wait()
    vectors = jnp.concatenate(
        [
            gains[...],
            jnp.concatenate([bias[...], jnp.zeros((1, LANES - 64), F32)], axis=1),
            jnp.zeros((29, LANES), F32),
        ],
        axis=0,
    )
    out_ref[:, HALF + ROW :] = vectors.astype(BF16)
    out_ref[:, :HALF] = expand[...].astype(BF16)
    out_ref[:, HALF : HALF + ROW] = spatial[...].astype(BF16)


def pack_second_kernel(expand_ref, shrink_ref, expand_out, shrink_out, expand, shrink, sems):
    core = lax.axis_index("narrow") & 1
    copies = [
        pltpu.make_async_copy(expand_ref.at[run(core * 32, 32), pl.ds(0, HALF)], expand, sems.at[0]),
        pltpu.make_async_copy(shrink_ref.at[run(core * 96, 32 * 3), :], shrink, sems.at[1]),
    ]
    for copy in copies:
        copy.start()
    for copy in copies:
        copy.wait()
    expand_out[...] = expand[...].astype(BF16)
    for k in range(3):
        shrink_out[:, k * D : (k + 1) * D] = shrink[k * 32 : (k + 1) * 32, :].astype(BF16)


def stack_kernel(*refs):
    for i, ref in enumerate(refs[:-1]):
        refs[-1][i] = ref[...]


def add_kernel(*refs):
    total = refs[0][...] + refs[1][...]
    if len(refs) == 5:
        total = total + (refs[2][...] + refs[3][...])
    refs[-1][...] = total


def fetch_kernel(*refs):
    count = (len(refs) - 1) // 2
    copies = [pltpu.make_async_copy(refs[i], refs[count + i], refs[-1].at[i]) for i in range(count)]
    for copy in copies:
        copy.start()
    for copy in copies:
        copy.wait()


def gating_kernel(tree, count, members, own_ref, core_ref, side_ref, forward_ref, *refs):
    parts = [core_ref.at[0], side_ref.at[0, 0], forward_ref.at[1, 0]]
    sources, small_sources = refs[:count], refs[count : count + 2]
    (
        normed_ref, xhat_ref, scale_ref, gate_ref, slope_ref, rstd_ref, spatial_ref, gains_ref, bias_col, weight,
        small, acts, active, sums, sems,
    ) = refs[count + 2 :]
    wide, narrow = lax.axis_index("wide"), lax.axis_index("narrow")
    rows_here, quarter = acts.shape[1:3]

    pltpu.make_async_copy(own_ref.at[pl.ds(narrow * rows_here, rows_here)], acts.at[narrow], sems.at[3]).start()
    for j, part in enumerate(parts):
        pltpu.make_async_copy(part, acts.at[narrow ^ (j + 1)], sems.at[3]).start()
    fetch_weights(
        sources,
        [
            (0, 0, HALF, weight, 64, 32, 0, sems.at[0]),
            (0, HALF, ROW, spatial_ref, 64, 32, 0, sems.at[1]),
        ],
        tree,
    )
    if tree:
        for x_off in range(2):
            for step in range(4):
                pltpu.make_async_copy(
                    small_sources[x_off].at[step, pl.ds(0, BLOCK), pl.ds(HALF + ROW, 128)],
                    small.at[wide ^ (2 * step + x_off)],
                    sems.at[2],
                ).start()
    else:
        pltpu.make_async_copy(small_sources[0], small, sems.at[2]).start()
    wait_weights([(weight, sems.at[0]), (spatial_ref, sems.at[1]), (small, sems.at[2]), (acts, sems.at[3])])
    diagonal = lax.broadcasted_iota(jnp.int32, (64, 128), 0) == lax.broadcasted_iota(jnp.int32, (64, 128), 1)
    for owner in range(8):
        values = small[owner].astype(F32)
        for k in range(2):
            gains_ref[:, owner * 256 + k * 128 : owner * 256 + (k + 1) * 128] = jnp.broadcast_to(
                values[k : k + 1, :], (8, 128)
            )
        column = jnp.sum(jnp.where(diagonal, values[2:3, :], 0.0), axis=1, keepdims=True)
        bias_col[owner * 64 : (owner + 1) * 64, :] = jnp.broadcast_to(column, (64, 128))

    def do_row(row, carry):
        for member in range(members):
            here = slice(member * quarter, (member + 1) * quarter)
            values = acts[member, row].astype(F32)
            shifted = values - jnp.mean(values, axis=1, keepdims=True)
            scale = lax.rsqrt(jnp.mean(shifted * shifted, axis=1, keepdims=True) + LAYER_EPS)
            xhat = shifted * scale
            scale_ref[row, here, :] = jnp.broadcast_to(scale, (quarter, 128))
            xhat_ref[row, here, :] = xhat.astype(BF16)
            normed_ref[row, here, :] = (xhat * gains_ref[0:1, :D]).astype(BF16)

        normed = normed_ref[row]
        for c in range(0, HALF, WIDTH):
            hidden = dot(normed, weight[:, c : c + WIDTH])
            for p in range(0, ROW, PIECE):
                here = slice(p, p + PIECE)
                values = hidden[here]
                squares, gate = gelu_gate(values)
                slope_ref[row, here, c : c + WIDTH] = gelu_slope(values, squares, gate).astype(BF16)
                result = values * gate
                active[here, c : c + WIDTH] = result
                total = result[:, :LANES] + result[:, LANES:]
                sums[here, :] = total if c == 0 else sums[here, :] + total
        for p in range(0, ROW, CHUNK):
            here = slice(p, p + CHUNK)
            centre = jnp.sum(sums[here, :], axis=1, keepdims=True) * (1.0 / HALF)
            total = jnp.zeros((CHUNK, LANES), F32)
            for c in range(0, HALF, LANES):
                shifted = active[here, c : c + LANES] - centre
                total = total + shifted * shifted
            scale = lax.rsqrt(jnp.sum(total, axis=1, keepdims=True) * (1.0 / HALF) + LAYER_EPS)
            rstd_ref[row, here, :] = jnp.broadcast_to(scale, (CHUNK, 128))
            for c in range(0, HALF, LANES):
                vhat = (active[here, c : c + LANES] - centre) * scale
                gate_ref[row, here, c : c + LANES] = (vhat * gains_ref[0:1, D + c : D + c + LANES]).astype(BF16)

        return carry

    lax.fori_loop(0, rows_here, do_row, 0)


def mixing_kernel(lens_ref, spatial_ref, gate_ref, bias_col, mixed_ref):
    rows_here = gate_ref.shape[0]
    narrow = lax.axis_index("narrow")
    for row in range(rows_here):
        same, live = doc_mask(0, ROW, lens_ref, narrow * rows_here + row)
        masked = jnp.where(same, spatial_ref[...], jnp.zeros((), BF16))
        bias = jnp.where(live, bias_col[:, 0:1], 0.0)
        for c in range(0, HALF, D):
            mixed_ref[row, :, c : c + D] = (dot(masked, gate_ref[row, :, c : c + D]) + bias).astype(BF16)


def emit_blocks(order, read, columns, first, keep_near, keep_far, send):
    wide, narrow = lax.axis_index("wide"), lax.axis_index("narrow")
    for core in range(2):
        for one in range(2):
            for two in range(2):
                for step in range(4):
                    x_off, y_off = (one, two) if order == "x" else (two, one)
                    values = read(wide ^ (2 * step + x_off), narrow ^ (2 * y_off + core)).astype(BF16)
                    place = pl.ds(first, columns)
                    if core == 1:
                        send[one, two, step, :, place] = values
                    elif one == 1:
                        keep_far[two, step, :, place] = values
                    else:
                        keep_near[two, step, :, place] = values


def reader(matrix, height, part, shift, columns):
    def read(owner, member):
        return matrix[run(owner * height + member * part + shift, BLOCK), columns]

    return read


def content_up_kernel(tree, normed_ref, *refs):
    sources, (content_ref, slope_ref, weight, sem) = refs[:-4], refs[-4:]
    tokens = normed_ref.shape[0] * normed_ref.shape[1]
    if tree:
        fetch_weights(sources, [(0, 0, HALF, weight, 64, 32, 0, sem)], tree)
    else:
        pltpu.make_async_copy(sources[0], weight, sem).start()
    wait_weights([(weight, sem)])

    def do_channels(k, carry):
        channels = run(k * WIDTH, WIDTH)
        hidden = dot(normed_ref[...].reshape(tokens, D), weight[:, channels])
        for p in range(0, tokens, PIECE):
            r, here = p // ROW, slice(p % ROW, p % ROW + PIECE)
            values = hidden[p : p + PIECE]
            squares, gate = gelu_gate(values)
            content_ref[r, here, channels] = (values * gate).astype(BF16)
            slope_ref[r, here, channels] = gelu_slope(values, squares, gate).astype(BF16)
        return carry

    lax.fori_loop(0, HALF // WIDTH, do_channels, 0)


def content_down_kernel(
    tree, count, members, lens_ref, content_ref, slope_ref, mixed_ref, own_ref, core_ref, side_ref, forward_ref, *refs
):
    parts = [core_ref.at[1], side_ref.at[0, 1], forward_ref.at[1, 1]]
    sources = refs[:count]
    gated_ref, grad_ref, grad_mixed_ref, bias_ref, shrink = refs[count : count + 5]
    raws = refs[count + 5 : count + (8 if tree else 6)]
    cots, sums, tall_sum, sems = refs[count + 5 + len(raws) :]
    narrow = lax.axis_index("narrow")
    rows_here, quarter = core_ref.shape[1:3]
    tokens = rows_here * ROW

    if tree:
        fetch_weights(sources, [(0, k * D, D, shrink, 192, 96, k * 32, sems.at[0]) for k in range(3)], tree)
    else:
        pltpu.make_async_copy(sources[0], shrink, sems.at[0]).start()
    for r in range(rows_here):
        for j in range(members):
            source = own_ref.at[narrow * rows_here + r] if j == 0 else parts[j - 1].at[r]
            place = run(r * ROW + (narrow ^ j) * quarter, quarter)
            pltpu.make_async_copy(source, cots.at[place, :], sems.at[1]).start()
    sums[...] = jnp.zeros_like(sums)
    wait_weights([(shrink, sems.at[0]), (cots, sems.at[1])])

    def do_channels(k, carry):
        channels = run(k * WIDTH, WIDTH)
        grad_gated = dot(cots[...], shrink[channels, :], ((1,), (1,)))
        for p in range(0, tokens, PIECE):
            r, here = p // ROW, slice(p % ROW, p % ROW + PIECE)
            grads = grad_gated[p : p + PIECE]
            content = content_ref[r, here, channels].astype(F32)
            mixed = mixed_ref[r, here, channels].astype(F32)
            slope = slope_ref[r, here, channels].astype(F32)
            gated_ref[r, here, channels] = (content * mixed).astype(BF16)
            grad_ref[r, here, channels] = (grads * mixed * slope).astype(BF16)
            grad_mixed = (grads * content).astype(BF16)
            grad_mixed_ref[r, here, channels] = grad_mixed
            total = grad_mixed.astype(F32)
            sums[p : p + PIECE, :] += total[:, :LANES] + total[:, LANES:]
        tall_sum[channels, :] = dot(gated_ref[:, :, channels].reshape(tokens, WIDTH), cots[...], ((0,), (0,)))
        return carry

    lax.fori_loop(0, HALF // WIDTH, do_channels, 0)
    for r in range(rows_here):
        _, live = doc_mask(0, ROW, lens_ref, narrow * rows_here + r)
        part = jnp.where(live, sums[r * ROW : (r + 1) * ROW, :], 0.0)
        bias_ref[...] = part if r == 0 else bias_ref[...] + part
    if tree:
        for j in range(3):
            emit_blocks("y", reader(tall_sum, 192, 48, j * BLOCK, slice(0, D)), D, j * D, *raws)
    else:
        raws[0][...] = tall_sum[...]


def content_sum_kernel(tree, normed_ref, grad_ref, *refs):
    raws, normed_turned, wide_sum = refs[:-2], refs[-2], refs[-1]
    tokens = normed_ref.shape[0] * normed_ref.shape[1]
    normed_turned[...] = normed_ref[...].reshape(tokens, D).T
    for c in range(0, HALF, D):
        wide_sum[...] = dot(normed_turned[...], grad_ref[:, :, c : c + D].reshape(tokens, D))
        if tree:
            emit_blocks("x", reader(wide_sum, 64, 16, 0, slice(0, D)), D, c, *raws)
        else:
            raws[0][:, c : c + D] = wide_sum[...]


def spatial_sum_kernel(lens_ref, grad_mixed_ref, gate_ref, square_ref):
    rows_here = grad_mixed_ref.shape[0]
    narrow = lax.axis_index("narrow")
    for row in range(rows_here):
        same, _ = doc_mask(0, ROW, lens_ref, narrow * rows_here + row)
        products = jnp.where(same, dot(grad_mixed_ref[row], gate_ref[row], ((1,), (1,))), 0.0)
        square_ref[...] = products if row == 0 else square_ref[...] + products


def gate_back_kernel(
    lens_ref, grad_mixed_ref, gate_ref, slope_ref, rstd_ref, spatial_ref, gains_ref, bias_ref,
    grad_ref, vectors_ref, turned, grad_gate, first_sums, second_sums, second, inverse,
):
    rows_here = grad_mixed_ref.shape[0]
    narrow = lax.axis_index("narrow")
    turned[...] = spatial_ref[...].T
    second[...] = jnp.zeros_like(second)
    inverse[...] = 1.0 / gains_ref[:, D:]

    def do_row(row, carry):
        same, _ = doc_mask(0, ROW, lens_ref, narrow * rows_here + row)
        masked = jnp.where(same, turned[...], jnp.zeros((), BF16))
        for c in range(0, HALF, WIDTH):
            grads_all = dot(masked, grad_mixed_ref[row, :, c : c + WIDTH])
            vector = jnp.zeros((8, WIDTH), F32)
            for p in range(0, ROW, PIECE):
                here = slice(p, p + PIECE)
                low = grads_all[here].astype(BF16)
                grad_gate[here, c : c + WIDTH] = low
                grads = low.astype(F32)
                products = grads * gate_ref[row, here, c : c + WIDTH].astype(F32)
                vector = vector + jnp.sum(products.reshape(PIECE // 8, 8, WIDTH), axis=0)
                scaled = grads * gains_ref[0:1, D + c : D + c + WIDTH]
                first = scaled[:, :LANES] + scaled[:, LANES:]
                other = products[:, :LANES] + products[:, LANES:]
                first_sums[here, :] = first if c == 0 else first_sums[here, :] + first
                second_sums[here, :] = other if c == 0 else second_sums[here, :] + other
            second[:, c : c + WIDTH] += vector
        for p in range(0, ROW, CHUNK):
            here = slice(p, p + CHUNK)
            scale = rstd_ref[row, here, 0:1]
            first_mean = jnp.sum(first_sums[here, :], axis=1, keepdims=True) * (1.0 / HALF) * scale
            second_mean = jnp.sum(second_sums[here, :], axis=1, keepdims=True) * (1.0 / HALF) * scale
            for c in range(0, HALF, LANES):
                place = slice(c, c + LANES)
                scaled = grad_gate[here, place].astype(F32) * gains_ref[0:1, D + c : D + c + LANES] * scale
                vhat = gate_ref[row, here, place].astype(F32) * inverse[0:1, place]
                slope = slope_ref[row, here, place].astype(F32)
                grad_ref[row, here, place] = ((scaled - first_mean - vhat * second_mean) * slope).astype(BF16)
        return carry

    lax.fori_loop(0, rows_here, do_row, 0)
    vectors_ref[...] = jnp.zeros_like(vectors_ref)
    diagonal = lax.broadcasted_iota(jnp.int32, (64, 128), 0) == lax.broadcasted_iota(jnp.int32, (64, 128), 1)
    for owner in range(8):
        for k in range(2 if owner >= 2 else 0):
            c = (owner - 2) * 256 + k * 128
            total = jnp.sum(second[:, c : c + 128], axis=0, keepdims=True)
            vectors_ref[owner, k : k + 1, :] = total * inverse[0:1, c : c + 128]
        column = jnp.sum(bias_ref[owner * 64 : (owner + 1) * 64, :], axis=1, keepdims=True)
        vectors_ref[owner, 2:3, :] = jnp.sum(jnp.where(diagonal, column, 0.0), axis=0, keepdims=True)


def gate_sum_kernel(tree, normed_ref, grad_ref, square_ref, vectors_ref, *refs):
    raws, normed_turned, wide_sum = refs[:-2], refs[-2], refs[-1]
    tokens = normed_ref.shape[0] * normed_ref.shape[1]
    rest = HALF - SPLIT
    normed_turned[...] = normed_ref[...].reshape(tokens, D).T
    if tree:
        emit_blocks("y", reader(square_ref, 64, 16, 0, slice(0, ROW)), ROW, rest, *raws[3:])
        emit_blocks("y", lambda owner, member: vectors_ref[owner], VECTOR_LANES, rest + ROW, *raws[3:])
    else:
        raws[1][...] = square_ref[...]
        raws[2][...] = vectors_ref[...]
    for c in range(0, HALF, D):
        wide_sum[...] = dot(normed_turned[...], grad_ref[:, :, c : c + D].reshape(tokens, D))
        if not tree:
            raws[0][:, c : c + D] = wide_sum[...]
        elif c < SPLIT:
            emit_blocks("x", reader(wide_sum, 64, 16, 0, slice(0, D)), D, c, *raws[:3])
        else:
            emit_blocks("y", reader(wide_sum, 64, 16, 0, slice(0, D)), D, c - SPLIT, *raws[3:])


def layer_kernel(gated_ref, shrink, own_ref, core_ref, pair_ref, total):
    members, rows_here, quarter = total.shape[:3]
    narrow = lax.axis_index("narrow")
    for row in range(rows_here):
        added = dot(gated_ref[row], shrink[...])
        for member in range(members):
            total[member ^ narrow, row] = added[member * quarter : (member + 1) * quarter].astype(BF16)
    own_ref[...] = total[0]
    core_ref[...] = total[1]
    pair_ref[0] = total[2]
    pair_ref[1] = total[3]


def back_kernel(
    gate_grad_ref, content_grad_ref, gate_weight, weight, xhat_ref, scale_ref, gains_ref, layer_core, layer_pair,
    own_ref, core_ref, pair_ref, total,
):
    members, rows_here, quarter = total.shape[:3]
    narrow = lax.axis_index("narrow")
    for row in range(rows_here):
        grad_normed = dot(gate_grad_ref[row], gate_weight[...], ((1,), (1,))) + dot(
            content_grad_ref[row], weight[...], ((1,), (1,))
        )
        for member in range(members):
            here = slice(member * quarter, (member + 1) * quarter)
            xhat = xhat_ref[row, here, :].astype(F32)
            scaled = grad_normed[here] * gains_ref[0:1, :D]
            first_mean = jnp.mean(scaled, axis=1, keepdims=True)
            second_mean = jnp.mean(scaled * xhat, axis=1, keepdims=True)
            scale = scale_ref[row, here, 0:1]
            total[member ^ narrow, row] = ((scaled - first_mean - xhat * second_mean) * scale).astype(BF16)
    own_ref[...] = total[0]
    core_ref[0] = total[1]
    core_ref[1] = layer_core[...]
    for j in range(2):
        pair_ref[j, 0] = total[2 + j]
        pair_ref[j, 1] = layer_pair[j]


def give_kernel(
    cots_ref, acts_ref, grad_own, layer_own, core_ref, side_ref, forward_ref, grad_out, layer_out, grads, layers, sems
):
    rows_here = grad_own.shape[0]
    narrow = lax.axis_index("narrow")
    stores = []
    for kind, (base, own, total, out) in enumerate(
        ((cots_ref, grad_own, grads, grad_out), (acts_ref, layer_own, layers, layer_out))
    ):
        parts = [own, core_ref.at[kind], side_ref.at[0, kind], forward_ref.at[1, kind]]
        for j, part in enumerate(parts):
            rows = pl.ds((narrow ^ j) * rows_here, rows_here)
            total[j] = (base[rows].astype(F32) + part[...].astype(F32)).astype(total.dtype)
            stores.append(pltpu.make_async_copy(total.at[j], out.at[rows], sems.at[kind, j]))
            stores[-1].start()
    for store in stores:
        store.wait()


def sum_three(near_ref, came_ref, far_ref, half, columns):
    values = near_ref[half, :, :, columns].astype(F32) + came_ref[0, half, :, :, columns].astype(F32)
    return values + far_ref[half, :, :, columns].astype(F32)


def side_kernel(*refs):
    for i, out_ref in enumerate(refs[6:]):
        near, came, far = refs[3 * i : 3 * i + 3]
        for c in range(0, near.shape[3], LANES):
            out_ref[:, :, c : c + LANES] = sum_three(near, came, far, 1, slice(c, c + LANES)).astype(BF16)


def fold_kernel(*refs):
    sides, outputs = refs[12:16], refs[16:]
    first = 0
    for i in range(4):
        near, came, far = refs[3 * i : 3 * i + 3]
        for c in range(0, near.shape[3], LANES):
            place = slice(c, c + LANES)
            total = sum_three(near, came, far, 0, place) + sides[i][:, :, place].astype(F32)
            there = slice(first + c, first + c + LANES)
            outputs[0][:, there] = total[0]
            for step in range(1, 4):
                outputs[step][:, there] = total[step].astype(BF16)
        first += near.shape[3]


def norm_kernel(mine_ref, one_ref, two_ref, three_ref, weight_ref, gains_ref, low_ref, message_ref):
    wide, narrow = lax.axis_index("wide"), lax.axis_index("narrow")
    columns = mine_ref.shape[1]
    squares = jnp.zeros((BLOCK, LANES), F32)
    products = jnp.zeros((BLOCK, LANES), F32)
    here = run(narrow * BLOCK, BLOCK)
    for c in range(0, columns, LANES):
        place = slice(c, c + LANES)
        total = mine_ref[:, place]
        for ref in (one_ref, two_ref, three_ref):
            total = total + ref[:, place].astype(F32)
        low = total.astype(BF16)
        low_ref[:, place] = low
        value = low.astype(F32)
        square = value * value
        squares = squares + (square if c < columns - LANES else jnp.where(narrow == 0, square, 0.0))
        at = expand_column(c)
        if at is not None:
            weight = weight_ref[here, at : at + LANES].astype(BF16).astype(F32)
            products = products + value * weight
    first = wide * 64 + narrow * BLOCK
    lanes = lax.broadcasted_iota(jnp.int32, (BLOCK, D), 1)
    diagonal = lanes == lax.broadcasted_iota(jnp.int32, (BLOCK, D), 0) + first
    gain = jnp.sum(jnp.where(diagonal, gains_ref[0:1, :D], 0.0), axis=1, keepdims=True)
    first_raw = jnp.sum(products, axis=1, keepdims=True) / gain
    total = jnp.sum(squares) + jnp.sum(first_raw * first_raw)
    places = jnp.sum(jnp.where(diagonal, first_raw, 0.0), axis=0, keepdims=True)
    message_ref[...] = jnp.full(message_ref.shape, total, F32)
    for k in range(D // LANES):
        message_ref[k : k + 1, :] = places[:, k * LANES : (k + 1) * LANES]


def expand_column(c):
    right = HALF + SPLIT
    turn = right + HALF
    if c < right:
        return c
    if turn <= c < turn + HALF - SPLIT:
        return c - HALF
    return None


def adam_kernel(message_ref, own_ref, side_ref, other_ref, *refs):
    states, vectors, outputs, vector_outputs, norm_ref = refs[:12], refs[12:20], refs[20:35], refs[35:45], refs[45]
    results, blocks, sem = refs[46:61], refs[61], refs[62]
    wide, narrow = lax.axis_index("wide"), lax.axis_index("narrow")
    norm = jnp.sqrt(message_ref[4:5, :])
    norm_ref[0, 0] = jnp.max(norm)
    clip = CLIP_LIMIT / jnp.maximum(norm, CLIP_LIMIT)
    right = HALF + SPLIT
    turn = right + HALF
    blocks[narrow] = own_ref[...]
    blocks[narrow ^ 1] = other_ref[0]
    blocks[narrow ^ 2] = side_ref[...]
    blocks[narrow ^ 3] = other_ref[1]

    def update(which, gradient, rows, place):
        weight, momentum, variance, average = [ref[rows, place] for ref in states[4 * which : 4 * which + 4]]
        updates = adam_update(
            weight, gradient.astype(F32), momentum, variance, average, clip, RATE_MATRIX, DECAY_MATRIX
        )
        for ref, value in zip(results[5 * which : 5 * which + 5], updates):
            ref[rows, place] = value

    def do_member(member, carry):
        thin = run(member * BLOCK, BLOCK)
        for c in range(0, turn + HALF - SPLIT + ROW, LANES):
            gradient = blocks[member, :, c : c + LANES]
            at = expand_column(c)
            if at is not None:
                update(0, gradient, thin, slice(at, at + LANES))
            elif c < turn:
                k, at = (c - right) // D, (c - right) % D
                update(1, gradient, run(member * 48 + k * BLOCK, BLOCK), slice(at, at + LANES))
            else:
                at = c - turn - (HALF - SPLIT)
                update(2, gradient, thin, slice(at, at + LANES))
        for i in range(15):
            rows = run(member * 48, 48) if 5 <= i < 10 else thin
            pltpu.make_async_copy(results[i].at[rows, :], outputs[i].at[rows, :], sem.at[i]).start()
        return carry

    lax.fori_loop(0, 4, do_member, 0)
    own = blocks[0, :, turn + HALF - SPLIT + ROW :].astype(F32)
    gains = jnp.where(wide == 0, message_ref[0:2, :], jnp.where(wide == 1, message_ref[2:4, :], own[0:2, :]))
    for which, gradient in ((0, gains), (1, own[2:3, :64])):
        weight, momentum, variance, average = [ref[...] for ref in vectors[4 * which : 4 * which + 4]]
        updates = adam_update(
            weight, gradient, momentum, variance, average, clip[:, : gradient.shape[1]], RATE_VECTOR, 0.0
        )
        for ref, value in zip(vector_outputs[5 * which : 5 * which + 5], updates):
            ref[...] = value
    for i in range(15):
        pltpu.make_async_copy(results[i], outputs[i], sem.at[i]).wait()


def call_kernel(kernel, name, args, in_specs, out_types, scratch, flops, limit=VMEM_LIMIT):
    vmem = pl.BlockSpec(memory_space=pltpu.VMEM)
    specs = [kind[1] if isinstance(kind, tuple) else vmem for kind in out_types]
    types = [
        kind[0] if isinstance(kind, tuple) else pltpu.VMEM(kind.shape, kind.dtype) for kind in out_types
    ]
    in_specs = [vmem if spec is None else spec for spec in in_specs]
    args = [
        pltpu.with_memory_space_constraint(value, pltpu.HBM) if spec.memory_space == pltpu.HBM else value
        for value, spec in zip(args, in_specs)
    ]
    results = pl.pallas_call(
        kernel,
        name=name,
        in_specs=in_specs,
        out_specs=specs,
        out_shape=types,
        scratch_shapes=scratch,
        compiler_params=pltpu.CompilerParams(vmem_limit_bytes=limit),
        cost_estimate=pl.CostEstimate(flops=int(flops), bytes_accessed=int(flops / 500), transcendentals=0),
    )(*args)
    return list(results)


def swap_with(value, axis, size, bit):
    return lax.ppermute(value, axis, [(i, i ^ bit) for i in range(size)])


def after(value, *others):
    return lax.optimization_barrier((value,) + others)[0]


def sum_core(keep_far, came):
    return (keep_far.astype(F32) + came[1].astype(F32)).astype(BF16)


def adam_update(weight, gradient, momentum, variance, average, clip_scale, step_rate, decay_rate):
    ema_rate = min(EMA_DECAY, (1.0 + STEP) / (10.0 + STEP))
    clipped = clip_scale * gradient
    moment = BETA_FIRST * momentum + (1.0 - BETA_FIRST) * clipped
    square = BETA_SECOND * variance + (1.0 - BETA_SECOND) * clipped * clipped
    first_hat = moment * (1.0 / (1.0 - BETA_FIRST**STEP))
    second_hat = square * (1.0 / (1.0 - BETA_SECOND**STEP))
    updated = weight - step_rate * (
        first_hat / (jnp.sqrt(second_hat) + ADAM_EPS) + decay_rate * weight
    )
    smoothed = ema_rate * average + (1.0 - ema_rate) * updated
    return (clipped, moment, square, updated, smoothed)


def on_device(
    activations,
    cotangent,
    doc_lengths,
    expand_weight,
    expand_momentum,
    expand_variance,
    expand_average,
    shrink_weight,
    shrink_momentum,
    shrink_variance,
    shrink_average,
    spatial_weight,
    spatial_momentum,
    spatial_variance,
    spatial_average,
    norm_gains,
    gains_momentum,
    gains_variance,
    gains_average,
    spatial_bias,
    bias_momentum,
    bias_variance,
    bias_average,
):
    narrow_size, wide_size = lax.axis_size("narrow"), lax.axis_size("wide")
    wide, narrow = lax.axis_index("wide"), lax.axis_index("narrow")
    group_rows, quarter = activations.shape[0], activations.shape[1]
    rows = group_rows // narrow_size
    tokens = rows * ROW
    tree = (wide_size, narrow_size) == (8, 4)
    smem = pl.BlockSpec(memory_space=pltpu.SMEM)
    anywhere = pl.BlockSpec(memory_space=pl.ANY)
    stored = pl.BlockSpec(memory_space=pltpu.HBM)
    shape = jax.ShapeDtypeStruct
    dma = pltpu.SemaphoreType.DMA
    part = shape((rows, quarter, D), BF16)
    product = 2 * tokens * HALF * D
    cross_x = lambda value: swap_with(value, "wide", wide_size, 1)
    cross_y = lambda value: swap_with(value, "narrow", narrow_size, 2)
    cross_core = lambda value: swap_with(value, "narrow", narrow_size, 1)

    def trade(core_part, pair):
        side = cross_y(pair)
        return [cross_core(core_part), side, cross_core(side)]

    def stack(values):
        kind = shape((len(values), *values[0].shape), values[0].dtype)
        return call_kernel(stack_kernel, "stack", values, [None] * len(values), [kind], [], product // 64)[0]

    def add(*values):
        kind = shape(values[0].shape, values[0].dtype)
        return call_kernel(add_kernel, "add", values, [None] * len(values), [kind], [], product // 64)[0]

    pair = shape((2, *part.shape), BF16)

    def cut(acts, cots):
        return call_kernel(
            cut_kernel,
            "cut",
            [acts, cots],
            [stored] * 2,
            [(pair, stored), (shape((2, *pair.shape), BF16), stored)],
            [dma((6,))],
            product // 64,
        )

    if tree:
        first_own = call_kernel(
            pack_first_kernel,
            "pack_first",
            [expand_weight, spatial_weight, norm_gains.reshape(2, LANES), spatial_bias.reshape(1, 64)],
            [stored] * 4,
            [shape((32, HALF + ROW + VECTOR_LANES), BF16)],
            [pltpu.VMEM((32, HALF), F32), pltpu.VMEM((32, ROW), F32), pltpu.VMEM((2, LANES), F32)]
            + [pltpu.VMEM((1, 64), F32), dma((4,))],
            product // 64,
        )[0]
        over_z = lambda own: [swap_with(own, "wide", wide_size, 2 * s) for s in range(1, 4)]
        came_z = over_z(first_own)
        core_cut, pair_cut = cut(after(activations, first_own), cotangent)
        side_came = cross_y(pair_cut)
        expand_own, shrink_own = call_kernel(
            pack_second_kernel,
            "pack_second",
            [expand_weight, shrink_weight],
            [stored, stored],
            [shape((32, HALF), BF16)] * 2,
            [pltpu.VMEM((32, HALF), F32), pltpu.VMEM((96, D), F32), dma((2,))],
            product // 64,
        )
        *came_z, core_came, _, expand_own = lax.optimization_barrier(
            (*came_z, cross_core(core_cut), pair_cut, expand_own)
        )
        first_near = stack([first_own, *came_z])
        first_across = cross_x(first_near)
        expand_own = after(expand_own, first_near)
        *came_z, side_came = lax.optimization_barrier((*over_z(expand_own), side_came))
        expand_near = stack([expand_own, *came_z])
        expand_across = cross_x(after(expand_near, first_across))
        shrink_own = after(shrink_own, expand_near)
        shrink_came = over_z(shrink_own)
        near_core = cross_core(after(first_near, expand_near))
        across_core = cross_core(after(first_across, expand_near))
        forward_came = cross_core(after(side_came, expand_near))
        first_pieces = [after(first_near, expand_near), first_across, near_core, across_core]
        small_pieces = first_pieces[:2]
        near_other = cross_core(expand_near)
        count = len(PIECES)
    else:
        gather = lambda value: lax.all_gather(value.astype(BF16), "wide", axis=0, tiled=True)
        expand_low = gather(expand_weight)
        gains_low, bias_low = gather(norm_gains), gather(spatial_bias)
        small = jnp.concatenate(
            [
                gains_low.reshape(8, 2, 128),
                jnp.pad(bias_low.reshape(8, 1, 64), ((0, 0), (0, 0), (0, 64))),
                jnp.zeros((8, 13, 128), BF16),
            ],
            axis=1,
        )
        first_pieces = [expand_low[:, HALF:], gather(spatial_weight)]
        small_pieces = [small, small]
        expand_pieces, shrink_pieces = [expand_low[:, :HALF]], [gather(shrink_weight)]
        core_came, side_came, forward_came = trade(*cut(activations, cotangent))
        count = 2

    low_d, low_half = shape((rows, ROW, D), BF16), shape((rows, ROW, HALF), BF16)
    thin = shape((rows, ROW, 128), F32)
    weight_type = shape((D, HALF), BF16)

    normed, xhat, scale, gate_normed, slope, rstd, spatial_low, gains, bias_col, gate_weight = call_kernel(
        functools.partial(gating_kernel, tree, count, narrow_size),
        "gating",
        [activations, core_came, side_came, forward_came] + list(first_pieces) + list(small_pieces),
        [stored] + [anywhere] * (narrow_size - 1 + count + 2),
        [low_d, low_d, thin, low_half, low_half, thin]
        + [shape((ROW, ROW), BF16), shape((8, D + HALF), F32), shape((ROW, 128), F32), weight_type],
        [
            pltpu.VMEM((8, BLOCK, 128), BF16),
            pltpu.VMEM((narrow_size, *part.shape), BF16),
            pltpu.VMEM((ROW, HALF), F32),
            pltpu.VMEM((ROW, 128), F32),
            dma((4,)),
        ],
        product // 64,
    )

    bias_late = bias_col
    if tree:
        *shrink_came, expand_across, _ = lax.optimization_barrier((*shrink_came, expand_across, normed))
        shrink_near = stack([shrink_own, *shrink_came])
        shrink_across = cross_x(shrink_near)
        expand_pieces = [expand_near, expand_across, near_other, cross_core(expand_across)]
        bias_late = after(bias_col, shrink_near)
    mixed = call_kernel(
        mixing_kernel,
        "mixing",
        [doc_lengths, spatial_low, gate_normed, bias_late],
        [smem] + [None] * 3,
        [low_half],
        [],
        product // 64,
    )[0]
    normed_late = normed
    if tree:
        expand_pieces[3], normed_late, _ = lax.optimization_barrier((expand_pieces[3], normed, mixed))
    content, content_slope, content_weight = call_kernel(
        functools.partial(content_up_kernel, tree),
        "content_up",
        [normed_late, *expand_pieces],
        [None] + [anywhere] * len(expand_pieces),
        [low_half, low_half, weight_type],
        [dma(())],
        product // 64,
    )
    if tree:
        shrink_across, _ = lax.optimization_barrier((shrink_across, content))
        shrink_pieces = [shrink_near, shrink_across, cross_core(shrink_near), cross_core(shrink_across)]

    def raw_outputs(column_list, plain):
        if tree:
            return [
                shape(size, BF16)
                for columns in column_list
                for size in ((2, 4, BLOCK, columns), (2, 4, BLOCK, columns), (2, 2, 4, BLOCK, columns))
            ]
        return [shape(size, F32) for size in plain]

    gated, content_grad, grad_mixed, bias_part, shrink_low, *shrink_raws = call_kernel(
        functools.partial(content_down_kernel, tree, len(shrink_pieces), narrow_size),
        "content_down",
        [doc_lengths, content, content_slope, mixed, cotangent, core_came, side_came, forward_came, *shrink_pieces],
        [smem, None, None, None, stored] + [anywhere] * (narrow_size - 1 + len(shrink_pieces)),
        [low_half, low_half, low_half, shape((ROW, 128), F32), shape((HALF, D), BF16)]
        + raw_outputs((HALF,), ((HALF, D),)),
        [
            pltpu.VMEM((tokens, D), BF16),
            pltpu.VMEM((tokens, 128), F32),
            pltpu.VMEM((HALF, D), F32),
            dma((2,)),
        ],
        product // 64,
    )
    if tree:
        came = {"shrink": cross_core(shrink_raws[2])}
    sum_scratch = [pltpu.VMEM((D, tokens), BF16), pltpu.VMEM((D, D), F32)]
    content_raws = call_kernel(
        functools.partial(content_sum_kernel, tree),
        "content_sum",
        [normed, content_grad],
        [None] * 2,
        raw_outputs((HALF,), ((D, HALF),)),
        sum_scratch,
        product // 64,
    )
    mixed_late = grad_mixed
    if tree:
        came["shrink"], content_raws[0] = lax.optimization_barrier((came["shrink"], content_raws[0]))
        came["content"] = cross_core(content_raws[2])
        far = {"shrink": sum_core(shrink_raws[1], came["shrink"])}
        came_far = {"shrink": cross_y(far["shrink"])}
        mixed_late = after(grad_mixed, far["shrink"])
    square_sum = call_kernel(
        spatial_sum_kernel,
        "spatial_sum",
        [doc_lengths, mixed_late, gate_normed],
        [smem, None, None],
        [shape((ROW, ROW), F32)],
        [],
        product // 64,
    )[0]
    if tree:
        came["content"], square_sum = lax.optimization_barrier((came["content"], square_sum))
        far["content"] = sum_core(content_raws[1], came["content"])
        came_far["content"] = cross_x(far["content"])
        mixed_late = after(grad_mixed, far["content"])

    gate_grad, vectors = call_kernel(
        gate_back_kernel,
        "gate_back",
        [doc_lengths, mixed_late, gate_normed, slope, rstd, spatial_low, gains, bias_part],
        [smem] + [None] * 7,
        [low_half, shape((8, BLOCK, 128), F32)],
        [
            pltpu.VMEM((ROW, ROW), BF16),
            pltpu.VMEM((ROW, HALF), BF16),
            pltpu.VMEM((ROW, 128), F32),
            pltpu.VMEM((ROW, 128), F32),
            pltpu.VMEM((8, HALF), F32),
            pltpu.VMEM((8, HALF), F32),
        ],
        product // 64,
    )
    normed_late = normed
    if tree:
        came_far["shrink"], normed_late = lax.optimization_barrier((came_far["shrink"], normed))
    second_raws = call_kernel(
        functools.partial(gate_sum_kernel, tree),
        "gate_sum",
        [normed_late, gate_grad, square_sum, vectors],
        [None] * 4,
        raw_outputs((SPLIT, HALF - SPLIT + ROW + VECTOR_LANES), ((D, HALF), (ROW, ROW), (8, BLOCK, 128))),
        sum_scratch,
        product // 64,
    )
    def side_step(terms, widths):
        kinds = [shape((4, BLOCK, width), BF16) for width in widths]
        return call_kernel(side_kernel, "side", terms, [None] * 6, kinds, [], product // 64)

    gated_late = gated
    if tree:
        second_raws[2], second_raws[5], came_far["content"] = lax.optimization_barrier(
            (second_raws[2], second_raws[5], came_far["content"])
        )
        second_came = [cross_core(second_raws[i]) for i in (2, 5)]
        first_terms = [content_raws[0], came["content"], came_far["content"]]
        first_terms += [shrink_raws[0], came["shrink"], came_far["shrink"]]
        first_sides = side_step(first_terms, (HALF, HALF))
        first_came_side = [cross_y(first_sides[0]), cross_x(first_sides[1])]
        gated_late = after(gated, second_raws[0], *first_sides)
    part_scratch = pltpu.VMEM((narrow_size, *part.shape), BF16)
    layer_own, layer_core, layer_pair = call_kernel(
        layer_kernel,
        "layer",
        [gated_late, shrink_low],
        [None] * 2,
        [part, part, pair],
        [part_scratch],
        product // 64,
    )
    grad_late = gate_grad
    if tree:
        *second_came, layer_own = lax.optimization_barrier((*second_came, layer_own))
        second_far = [sum_core(second_raws[1], second_came[0]), sum_core(second_raws[4], second_came[1])]
        second_came_far = [cross_x(second_far[0]), cross_y(second_far[1])]
        grad_late = after(gate_grad, *second_far)
    grad_own, core_back, pair_back = call_kernel(
        back_kernel,
        "back",
        [grad_late, content_grad, gate_weight, content_weight, xhat, scale, gains, layer_core, layer_pair],
        [None] * 9,
        [part, pair, shape((2, *pair.shape), BF16)],
        [part_scratch],
        product // 64,
    )

    def give(cots_base, acts_base, returned):
        whole = (group_rows, quarter, D)
        return call_kernel(
            give_kernel,
            "give",
            [cots_base, acts_base, grad_own, layer_own, *returned],
            [None] * 7,
            [(shape(whole, F32), stored), (shape(whole, BF16), stored)],
            [
                pltpu.VMEM((narrow_size, *part.shape), F32),
                pltpu.VMEM((narrow_size, *part.shape), BF16),
                dma((2, narrow_size)),
            ],
            product // 64,
        )

    if tree:
        columns = HALF + HALF + SPLIT + (HALF - SPLIT) + ROW + VECTOR_LANES
        tied = lax.optimization_barrier((*second_came_far, *first_came_side, grad_own))
        second_came_far, first_came_side, grad_own = tied[:2], tied[2:4], tied[4]
        second_terms = [second_raws[0], second_came[0], second_came_far[0]]
        second_terms += [second_raws[3], second_came[1], second_came_far[1]]
        second_sides = side_step(second_terms, (SPLIT, HALF - SPLIT + ROW + VECTOR_LANES))
        second_came_side = [cross_y(second_sides[0]), cross_x(second_sides[1])]
        terms = first_terms[:3] + second_terms[:3] + first_terms[3:] + second_terms[3:]
        came_side = [first_came_side[0], second_came_side[0], first_came_side[1], second_came_side[1]]
        mine, *sent = call_kernel(
            fold_kernel,
            "fold",
            terms + came_side,
            [None] * 16,
            [shape((BLOCK, columns), F32)] + [shape((BLOCK, columns), BF16)] * 3,
            [],
            product // 64,
        )
        came_z = [swap_with(sent[s - 1], "wide", wide_size, 2 * s) for s in range(1, 4)]
        matrices = [expand_weight, expand_momentum, expand_variance, expand_average]
        matrices += [shrink_weight, shrink_momentum, shrink_variance, shrink_average]
        matrices += [spatial_weight, spatial_momentum, spatial_variance, spatial_average]
        fetched = [*matrices, cotangent, activations]
        states = call_kernel(
            fetch_kernel,
            "fetch",
            list(lax.optimization_barrier((*fetched, sent[0]))[:14]),
            [stored] * 14,
            [shape(value.shape, value.dtype) for value in fetched],
            [dma((14,))],
            product // 64,
        )
        states, bases = states[:12], states[12:]
        side_back = cross_y(after(pair_back, sent[0]))
        core_back = cross_core(after(core_back, sent[0]))
        *came_z, first_state = lax.optimization_barrier((*came_z, states[0]))
        low, message = call_kernel(
            norm_kernel,
            "norm",
            [mine, *came_z, first_state, gains],
            [None] * 6,
            [shape((BLOCK, columns), BF16), shape((8, LANES), F32)],
            [],
            product // 64,
        )
        side = cross_y(low)
        message = add(message, cross_core(message))
        message = add(message, cross_x(message))
        *arrived, side, side_back = lax.optimization_barrier((*over_z(message), side, side_back))
        message = add(message, *arrived)
        other = cross_core(stack([low, side]))
        returned = [core_back, side_back, cross_core(side_back)]
        input_grad, layer_out = give(*bases, returned)
        arrived, layer_out, input_grad = lax.optimization_barrier((cross_y(message), layer_out, input_grad))
        message = add(message, arrived)
        as_rows = lambda value: value.reshape(-1, min(value.shape[0], LANES))
        vector_states = [norm_gains, gains_momentum, gains_variance, gains_average]
        vector_states += [spatial_bias, bias_momentum, bias_variance, bias_average]
        vector_kinds = [shape((2, LANES), F32)] * 5 + [shape((1, 64), F32)] * 5
        *updates, norm_row = call_kernel(
            adam_kernel,
            "adam",
            [message, low, side, other, *states] + [as_rows(value) for value in vector_states],
            [None] * 24,
            [(shape(value.shape, F32), stored) for value in (matrices[0], matrices[4], matrices[8]) for _ in range(5)]
            + [(kind, pl.BlockSpec(memory_space=pltpu.VMEM)) for kind in vector_kinds]
            + [(shape((1, 1), F32), smem)],
            [pltpu.VMEM(value.shape, F32) for value in (matrices[0], matrices[4], matrices[8]) for _ in range(5)]
            + [pltpu.VMEM((4, BLOCK, columns), BF16), dma((15,))],
            product // 64,
        )
        grad_norm = norm_row[0, 0]
        results = [layer_out, input_grad, grad_norm, *updates[:15]]
        return tuple(results + [value.reshape(-1) for value in updates[15:]])

    returned = trade(core_back, pair_back)
    input_grad, layer_out = give(cotangent, activations, returned)
    gains_size, bias_size = norm_gains.shape[0], spatial_bias.shape[0]
    vectors = lax.psum(second_raws[2], ("narrow", "wide"))
    totals = lax.psum(
        (jnp.concatenate([content_raws[0], second_raws[0]], axis=1), shrink_raws[0], second_raws[1]), "narrow"
    )
    expand_shard, shrink_shard, spatial_shard = [
        lax.psum_scatter(total, "wide", scatter_dimension=0, tiled=True) for total in totals
    ]
    second_shard = lax.dynamic_slice_in_dim(vectors[:, :2].reshape(-1), wide * gains_size, gains_size)
    bias_shard = lax.dynamic_slice_in_dim(vectors[:, 2, :64].reshape(-1), wide * bias_size, bias_size)
    low_weight = expand_weight.astype(BF16).astype(F32)
    height = expand_weight.shape[0]
    first_gain = lax.dynamic_slice_in_dim(gains[0], wide * height, height)
    first_raw = jnp.sum(low_weight * expand_shard, axis=1) / first_gain
    squares = [expand_shard, shrink_shard, spatial_shard, second_shard, bias_shard, first_raw]
    square_total = lax.psum(sum(jnp.sum(value * value) for value in squares), "wide")
    first_all = lax.all_gather(first_raw, "wide", axis=0, tiled=True)
    first_all = jnp.concatenate([first_all, jnp.zeros((HALF,), F32)])
    gains_shard = second_shard + lax.dynamic_slice_in_dim(first_all, wide * gains_size, gains_size)
    grad_norm = jnp.sqrt(square_total)
    clip_scale = CLIP_LIMIT / jnp.maximum(grad_norm, CLIP_LIMIT)
    results = [layer_out, input_grad, grad_norm]
    for weight, shard, momentum, variance, average, rate, decay in (
        (expand_weight, expand_shard, expand_momentum, expand_variance, expand_average, RATE_MATRIX, DECAY_MATRIX),
        (shrink_weight, shrink_shard, shrink_momentum, shrink_variance, shrink_average, RATE_MATRIX, DECAY_MATRIX),
        (spatial_weight, spatial_shard, spatial_momentum, spatial_variance, spatial_average, RATE_MATRIX, DECAY_MATRIX),
        (norm_gains, gains_shard, gains_momentum, gains_variance, gains_average, RATE_VECTOR, 0.0),
        (spatial_bias, bias_shard, bias_momentum, bias_variance, bias_average, RATE_VECTOR, 0.0),
    ):
        results += adam_update(weight, shard, momentum, variance, average, clip_scale, rate, decay)
    return tuple(results)


def solution(mesh):
    tokens, matrix, vector = P("wide", "narrow", None), P("wide", None), P("wide")
    return jax.shard_map(
        on_device,
        mesh=mesh,
        in_specs=(tokens, tokens) + (matrix,) * 13 + (vector,) * 8,
        out_specs=(tokens, tokens, P()) + (matrix,) * 15 + (vector,) * 10,
        check_vma=False,
    )
```

```python
import functools

import jax
import jax.numpy as jnp
from jax import lax
from jax.experimental import pallas as pl
from jax.experimental.pallas import tpu as pltpu
from jax.sharding import PartitionSpec as P

D = 512
FF = 3072
ROW = 512
DOCS = 5
STEP = 10
HALF = 1536

LAYER_EPS = 1e-05
CLIP_LIMIT = 1.0
BETA_FIRST = 0.9
BETA_SECOND = 0.999
ADAM_EPS = 1e-08
RATE_MATRIX = 0.03
RATE_VECTOR = 0.2
DECAY_MATRIX = 0.1
EMA_DECAY = 0.9999

F32 = jnp.float32
BF16 = jnp.bfloat16
GELU_A = 0.7978845608028654
GELU_B = GELU_A * 0.044715
LANES = 128
CHUNK = 64
PIECE = 32
BLOCK = 16
VMEM_LIMIT = 16 * 1024 * 1024

PIECES = ((0, 0), (1, 0), (0, 1), (1, 1))
WIDTH = 256
SPLIT = 1024
VECTOR_LANES = 128


def gelu_gate(hidden):
    squares = hidden * hidden
    gate = 0.5 * jnp.tanh(hidden * (GELU_A + GELU_B * squares)) + 0.5
    return squares, gate


def gelu_slope(hidden, squares, gate):
    return gate * (1.0 + hidden * (1.0 - gate) * (2.0 * GELU_A + 6.0 * GELU_B * squares))


def doc_ids(places, lens_ref, row):
    bound = jnp.int32(0)
    ids = jnp.zeros(places.shape, jnp.int32)
    for k in range(DOCS - 1):
        bound = bound + lens_ref[row, k]
        ids = ids + (places >= bound).astype(jnp.int32)
    return ids


def doc_mask(start, rows, lens_ref, row):
    across = doc_ids(lax.broadcasted_iota(jnp.int32, (1, ROW), 1), lens_ref, row)
    down = doc_ids(lax.broadcasted_iota(jnp.int32, (rows, 1), 0) + start, lens_ref, row)
    live = down != DOCS - 1
    return jnp.where(live, down, -1) == across, live


def dot(left, right, dims=((1,), (0,))):
    return lax.dot_general(left, right, (dims, ((), ())), preferred_element_type=F32)


def run(start, size):
    return pl.ds(pl.multiple_of(start, size), size)


def fetch_weights(sources, moves, tree):
    if not tree:
        for source, (_, _, _, target, _, _, _, sem) in zip(sources, moves):
            pltpu.make_async_copy(source, target, sem).start()
        return
    wide, core = lax.axis_index("wide"), lax.axis_index("narrow") & 1
    for base, first, count, target, height, unit, shift, sem in moves:
        for i, (x_off, core_off) in enumerate(PIECES):
            for step in range(4):
                start = (wide ^ (2 * step + x_off)) * height + (core ^ core_off) * unit + shift
                pltpu.make_async_copy(
                    sources[base + i].at[step, :, pl.ds(first, count)], target.at[run(start, 32), :], sem
                ).start()


def wait_weights(targets):
    for target, sem in targets:
        pltpu.make_async_copy(target, target, sem).wait()


def cut_kernel(acts_ref, cots_ref, core_out, pair_out, sems):
    rows_here = core_out.shape[1]
    narrow = lax.axis_index("narrow")
    copies = []
    for i, ref in enumerate((acts_ref, cots_ref)):
        for j, target in ((1, core_out.at[i]), (2, pair_out.at[0, i]), (3, pair_out.at[1, i])):
            source = ref.at[pl.ds((narrow ^ j) * rows_here, rows_here)]
            copies.append(pltpu.make_async_copy(source, target, sems.at[len(copies)]))
    for copy in copies:
        copy.start()
    for copy in copies:
        copy.wait()


def pack_first_kernel(expand_ref, spatial_ref, gains_ref, bias_ref, out_ref, expand, spatial, gains, bias, sems):
    rows = run((lax.axis_index("narrow") & 1) * 32, 32)
    copies = [
        pltpu.make_async_copy(expand_ref.at[rows, pl.ds(HALF, HALF)], expand, sems.at[0]),
        pltpu.make_async_copy(spatial_ref.at[rows, :], spatial, sems.at[1]),
        pltpu.make_async_copy(gains_ref, gains, sems.at[2]),
        pltpu.make_async_copy(bias_ref, bias, sems.at[3]),
    ]
    for copy in copies:
        copy.start()
    for copy in copies:
        copy.wait()
    vectors = jnp.concatenate(
        [
            gains[...],
            jnp.concatenate([bias[...], jnp.zeros((1, LANES - 64), F32)], axis=1),
            jnp.zeros((29, LANES), F32),
        ],
        axis=0,
    )
    out_ref[:, HALF + ROW :] = vectors.astype(BF16)
    out_ref[:, :HALF] = expand[...].astype(BF16)
    out_ref[:, HALF : HALF + ROW] = spatial[...].astype(BF16)


def pack_second_kernel(expand_ref, shrink_ref, expand_out, shrink_out, expand, shrink, sems):
    core = lax.axis_index("narrow") & 1
    copies = [
        pltpu.make_async_copy(expand_ref.at[run(core * 32, 32), pl.ds(0, HALF)], expand, sems.at[0]),
        pltpu.make_async_copy(shrink_ref.at[run(core * 96, 32 * 3), :], shrink, sems.at[1]),
    ]
    for copy in copies:
        copy.start()
    for copy in copies:
        copy.wait()
    expand_out[...] = expand[...].astype(BF16)
    for k in range(3):
        shrink_out[:, k * D : (k + 1) * D] = shrink[k * 32 : (k + 1) * 32, :].astype(BF16)


def stack_kernel(*refs):
    for i, ref in enumerate(refs[:-1]):
        refs[-1][i] = ref[...]


def add_kernel(*refs):
    total = refs[0][...] + refs[1][...]
    if len(refs) == 5:
        total = total + (refs[2][...] + refs[3][...])
    refs[-1][...] = total


def fetch_kernel(*refs):
    count = (len(refs) - 1) // 2
    copies = [pltpu.make_async_copy(refs[i], refs[count + i], refs[-1].at[i]) for i in range(count)]
    for copy in copies:
        copy.start()
    for copy in copies:
        copy.wait()


def gating_kernel(tree, count, members, own_ref, core_ref, side_ref, forward_ref, *refs):
    parts = [core_ref.at[0], side_ref.at[0, 0], forward_ref.at[1, 0]]
    sources, small_sources = refs[:count], refs[count : count + 2]
    (
        normed_ref, xhat_ref, scale_ref, gate_ref, slope_ref, rstd_ref, spatial_ref, gains_ref, bias_col, weight,
        small, acts, active, sums, sems,
    ) = refs[count + 2 :]
    wide, narrow = lax.axis_index("wide"), lax.axis_index("narrow")
    rows_here, quarter = acts.shape[1:3]

    pltpu.make_async_copy(own_ref.at[pl.ds(narrow * rows_here, rows_here)], acts.at[narrow], sems.at[3]).start()
    for j, part in enumerate(parts):
        pltpu.make_async_copy(part, acts.at[narrow ^ (j + 1)], sems.at[3]).start()
    fetch_weights(
        sources,
        [
            (0, 0, HALF, weight, 64, 32, 0, sems.at[0]),
            (0, HALF, ROW, spatial_ref, 64, 32, 0, sems.at[1]),
        ],
        tree,
    )
    if tree:
        for x_off in range(2):
            for step in range(4):
                pltpu.make_async_copy(
                    small_sources[x_off].at[step, pl.ds(0, BLOCK), pl.ds(HALF + ROW, 128)],
                    small.at[wide ^ (2 * step + x_off)],
                    sems.at[2],
                ).start()
    else:
        pltpu.make_async_copy(small_sources[0], small, sems.at[2]).start()
    wait_weights([(weight, sems.at[0]), (spatial_ref, sems.at[1]), (small, sems.at[2]), (acts, sems.at[3])])
    diagonal = lax.broadcasted_iota(jnp.int32, (64, 128), 0) == lax.broadcasted_iota(jnp.int32, (64, 128), 1)
    for owner in range(8):
        values = small[owner].astype(F32)
        for k in range(2):
            gains_ref[:, owner * 256 + k * 128 : owner * 256 + (k + 1) * 128] = jnp.broadcast_to(
                values[k : k + 1, :], (8, 128)
            )
        column = jnp.sum(jnp.where(diagonal, values[2:3, :], 0.0), axis=1, keepdims=True)
        bias_col[owner * 64 : (owner + 1) * 64, :] = jnp.broadcast_to(column, (64, 128))

    def do_row(row, carry):
        for member in range(members):
            here = slice(member * quarter, (member + 1) * quarter)
            values = acts[member, row].astype(F32)
            shifted = values - jnp.mean(values, axis=1, keepdims=True)
            scale = lax.rsqrt(jnp.mean(shifted * shifted, axis=1, keepdims=True) + LAYER_EPS)
            xhat = shifted * scale
            scale_ref[row, here, :] = jnp.broadcast_to(scale, (quarter, 128))
            xhat_ref[row, here, :] = xhat.astype(BF16)
            normed_ref[row, here, :] = (xhat * gains_ref[0:1, :D]).astype(BF16)

        normed = normed_ref[row]
        for c in range(0, HALF, WIDTH):
            hidden = dot(normed, weight[:, c : c + WIDTH])
            for p in range(0, ROW, PIECE):
                here = slice(p, p + PIECE)
                values = hidden[here]
                squares, gate = gelu_gate(values)
                slope_ref[row, here, c : c + WIDTH] = gelu_slope(values, squares, gate).astype(BF16)
                result = values * gate
                active[here, c : c + WIDTH] = result
                total = result[:, :LANES] + result[:, LANES:]
                sums[here, :] = total if c == 0 else sums[here, :] + total
        for p in range(0, ROW, CHUNK):
            here = slice(p, p + CHUNK)
            centre = jnp.sum(sums[here, :], axis=1, keepdims=True) * (1.0 / HALF)
            total = jnp.zeros((CHUNK, LANES), F32)
            for c in range(0, HALF, LANES):
                shifted = active[here, c : c + LANES] - centre
                total = total + shifted * shifted
            scale = lax.rsqrt(jnp.sum(total, axis=1, keepdims=True) * (1.0 / HALF) + LAYER_EPS)
            rstd_ref[row, here, :] = jnp.broadcast_to(scale, (CHUNK, 128))
            for c in range(0, HALF, LANES):
                vhat = (active[here, c : c + LANES] - centre) * scale
                gate_ref[row, here, c : c + LANES] = (vhat * gains_ref[0:1, D + c : D + c + LANES]).astype(BF16)

        return carry

    lax.fori_loop(0, rows_here, do_row, 0)


def mixing_kernel(lens_ref, spatial_ref, gate_ref, bias_col, mixed_ref):
    rows_here = gate_ref.shape[0]
    narrow = lax.axis_index("narrow")
    for row in range(rows_here):
        same, live = doc_mask(0, ROW, lens_ref, narrow * rows_here + row)
        masked = jnp.where(same, spatial_ref[...], jnp.zeros((), BF16))
        bias = jnp.where(live, bias_col[:, 0:1], 0.0)
        for c in range(0, HALF, D):
            mixed_ref[row, :, c : c + D] = (dot(masked, gate_ref[row, :, c : c + D]) + bias).astype(BF16)


def emit_blocks(order, read, columns, first, keep_near, keep_far, send):
    wide, narrow = lax.axis_index("wide"), lax.axis_index("narrow")
    for core in range(2):
        for one in range(2):
            for two in range(2):
                for step in range(4):
                    x_off, y_off = (one, two) if order == "x" else (two, one)
                    values = read(wide ^ (2 * step + x_off), narrow ^ (2 * y_off + core)).astype(BF16)
                    place = pl.ds(first, columns)
                    if core == 1:
                        send[one, two, step, :, place] = values
                    elif one == 1:
                        keep_far[two, step, :, place] = values
                    else:
                        keep_near[two, step, :, place] = values


def reader(matrix, height, part, shift, columns):
    def read(owner, member):
        return matrix[run(owner * height + member * part + shift, BLOCK), columns]

    return read


def content_up_kernel(tree, members, normed_ref, own_ref, core_ref, side_ref, forward_ref, *refs):
    parts = [core_ref.at[1], side_ref.at[0, 1], forward_ref.at[1, 1]]
    sources, (content_ref, slope_ref, weight, cots_turned, cots, sems) = refs[:-6], refs[-6:]
    narrow = lax.axis_index("narrow")
    rows_here, quarter = core_ref.shape[1:3]
    tokens = rows_here * ROW
    if tree:
        fetch_weights(sources, [(0, 0, HALF, weight, 64, 32, 0, sems.at[0])], tree)
    else:
        pltpu.make_async_copy(sources[0], weight, sems.at[0]).start()
    for r in range(rows_here):
        for j in range(members):
            source = own_ref.at[narrow * rows_here + r] if j == 0 else parts[j - 1].at[r]
            place = run(r * ROW + (narrow ^ j) * quarter, quarter)
            pltpu.make_async_copy(source, cots.at[place, :], sems.at[1]).start()
    wait_weights([(weight, sems.at[0])])

    def do_channels(k, carry):
        channels = run(k * WIDTH, WIDTH)
        hidden = dot(normed_ref[...].reshape(tokens, D), weight[:, channels])
        for p in range(0, tokens, PIECE):
            r, here = p // ROW, slice(p % ROW, p % ROW + PIECE)
            values = hidden[p : p + PIECE]
            squares, gate = gelu_gate(values)
            content_ref[r, here, channels] = (values * gate).astype(BF16)
            slope_ref[r, here, channels] = gelu_slope(values, squares, gate).astype(BF16)
        return carry

    lax.fori_loop(0, HALF // WIDTH, do_channels, 0)
    wait_weights([(cots, sems.at[1])])
    cots_turned[...] = cots[...].T


def content_down_kernel(tree, count, lens_ref, content_ref, slope_ref, mixed_ref, cots, cots_turned, *refs):
    sources = refs[:count]
    gated_ref, grad_ref, grad_mixed_ref, bias_ref, shrink = refs[count : count + 5]
    raws = refs[count + 5 : count + (8 if tree else 6)]
    sums, tall_sum, sem = refs[count + 5 + len(raws) :]
    narrow = lax.axis_index("narrow")
    rows_here = content_ref.shape[0]
    tokens = rows_here * ROW

    if tree:
        fetch_weights(sources, [(0, k * D, D, shrink, 192, 96, k * 32, sem) for k in range(3)], tree)
    else:
        pltpu.make_async_copy(sources[0], shrink, sem).start()
    sums[...] = jnp.zeros_like(sums)
    wait_weights([(shrink, sem)])

    def do_channels(k, carry):
        channels = run(k * WIDTH, WIDTH)
        grad_gated = dot(cots[...], shrink[channels, :], ((1,), (1,)))
        for p in range(0, tokens, PIECE):
            r, here = p // ROW, slice(p % ROW, p % ROW + PIECE)
            grads = grad_gated[p : p + PIECE]
            content = content_ref[r, here, channels].astype(F32)
            mixed = mixed_ref[r, here, channels].astype(F32)
            slope = slope_ref[r, here, channels].astype(F32)
            gated_ref[r, here, channels] = (content * mixed).astype(BF16)
            grad_ref[r, here, channels] = (grads * mixed * slope).astype(BF16)
            grad_mixed = (grads * content).astype(BF16)
            grad_mixed_ref[r, here, channels] = grad_mixed
            total = grad_mixed.astype(F32)
            sums[p : p + PIECE, :] += total[:, :LANES] + total[:, LANES:]
        product = dot(cots_turned[...], gated_ref[:, :, channels].reshape(tokens, WIDTH))
        if tree:
            tall_sum[channels, :] = product.astype(BF16).T
        else:
            raws[0][channels, :] = product.T
        return carry

    lax.fori_loop(0, HALF // WIDTH, do_channels, 0)
    for r in range(rows_here):
        _, live = doc_mask(0, ROW, lens_ref, narrow * rows_here + r)
        part = jnp.where(live, sums[r * ROW : (r + 1) * ROW, :], 0.0)
        bias_ref[...] = part if r == 0 else bias_ref[...] + part
    if tree:
        for j in range(3):
            emit_blocks("y", reader(tall_sum, 192, 48, j * BLOCK, slice(0, D)), D, j * D, *raws)


def content_sum_kernel(tree, normed_ref, grad_ref, *refs):
    raws, normed_turned, wide_sum = refs[:-2], refs[-2], refs[-1]
    tokens = normed_ref.shape[0] * normed_ref.shape[1]
    normed_turned[...] = normed_ref[...].reshape(tokens, D).T
    for c in range(0, HALF, D):
        wide_sum[...] = dot(normed_turned[...], grad_ref[:, :, c : c + D].reshape(tokens, D))
        if tree:
            emit_blocks("x", reader(wide_sum, 64, 16, 0, slice(0, D)), D, c, *raws)
        else:
            raws[0][:, c : c + D] = wide_sum[...]


def spatial_sum_kernel(lens_ref, grad_mixed_ref, gate_ref, square_ref):
    rows_here = grad_mixed_ref.shape[0]
    narrow = lax.axis_index("narrow")
    for row in range(rows_here):
        same, _ = doc_mask(0, ROW, lens_ref, narrow * rows_here + row)
        products = jnp.where(same, dot(grad_mixed_ref[row], gate_ref[row], ((1,), (1,))), 0.0)
        square_ref[...] = products if row == 0 else square_ref[...] + products


def gate_back_kernel(
    lens_ref, grad_mixed_ref, gate_ref, slope_ref, rstd_ref, spatial_ref, gains_ref, bias_ref,
    grad_ref, vectors_ref, turned, grad_gate, first_sums, second_sums, second, inverse,
):
    rows_here = grad_mixed_ref.shape[0]
    narrow = lax.axis_index("narrow")
    turned[...] = spatial_ref[...].T
    second[...] = jnp.zeros_like(second)
    inverse[...] = 1.0 / gains_ref[:, D:]

    def do_row(row, carry):
        same, _ = doc_mask(0, ROW, lens_ref, narrow * rows_here + row)
        masked = jnp.where(same, turned[...], jnp.zeros((), BF16))
        for c in range(0, HALF, WIDTH):
            grads_all = dot(masked, grad_mixed_ref[row, :, c : c + WIDTH])
            vector = jnp.zeros((8, WIDTH), F32)
            for p in range(0, ROW, PIECE):
                here = slice(p, p + PIECE)
                low = grads_all[here].astype(BF16)
                grad_gate[here, c : c + WIDTH] = low
                grads = low.astype(F32)
                products = grads * gate_ref[row, here, c : c + WIDTH].astype(F32)
                vector = vector + jnp.sum(products.reshape(PIECE // 8, 8, WIDTH), axis=0)
                scaled = grads * gains_ref[0:1, D + c : D + c + WIDTH]
                first = scaled[:, :LANES] + scaled[:, LANES:]
                other = products[:, :LANES] + products[:, LANES:]
                first_sums[here, :] = first if c == 0 else first_sums[here, :] + first
                second_sums[here, :] = other if c == 0 else second_sums[here, :] + other
            second[:, c : c + WIDTH] += vector
        for p in range(0, ROW, CHUNK):
            here = slice(p, p + CHUNK)
            scale = rstd_ref[row, here, 0:1]
            first_mean = jnp.sum(first_sums[here, :], axis=1, keepdims=True) * (1.0 / HALF) * scale
            second_mean = jnp.sum(second_sums[here, :], axis=1, keepdims=True) * (1.0 / HALF) * scale
            for c in range(0, HALF, LANES):
                place = slice(c, c + LANES)
                scaled = grad_gate[here, place].astype(F32) * gains_ref[0:1, D + c : D + c + LANES] * scale
                vhat = gate_ref[row, here, place].astype(F32) * inverse[0:1, place]
                slope = slope_ref[row, here, place].astype(F32)
                grad_ref[row, here, place] = ((scaled - first_mean - vhat * second_mean) * slope).astype(BF16)
        return carry

    lax.fori_loop(0, rows_here, do_row, 0)
    vectors_ref[...] = jnp.zeros_like(vectors_ref)
    diagonal = lax.broadcasted_iota(jnp.int32, (64, 128), 0) == lax.broadcasted_iota(jnp.int32, (64, 128), 1)
    for owner in range(8):
        for k in range(2 if owner >= 2 else 0):
            c = (owner - 2) * 256 + k * 128
            total = jnp.sum(second[:, c : c + 128], axis=0, keepdims=True)
            vectors_ref[owner, k : k + 1, :] = total * inverse[0:1, c : c + 128]
        column = jnp.sum(bias_ref[owner * 64 : (owner + 1) * 64, :], axis=1, keepdims=True)
        vectors_ref[owner, 2:3, :] = jnp.sum(jnp.where(diagonal, column, 0.0), axis=0, keepdims=True)


def gate_sum_kernel(tree, normed_ref, grad_ref, square_ref, vectors_ref, *refs):
    raws, normed_turned, wide_sum = refs[:-2], refs[-2], refs[-1]
    tokens = normed_ref.shape[0] * normed_ref.shape[1]
    rest = HALF - SPLIT
    normed_turned[...] = normed_ref[...].reshape(tokens, D).T
    if tree:
        emit_blocks("y", reader(square_ref, 64, 16, 0, slice(0, ROW)), ROW, rest, *raws[3:])
        emit_blocks("y", lambda owner, member: vectors_ref[owner], VECTOR_LANES, rest + ROW, *raws[3:])
    else:
        raws[1][...] = square_ref[...]
        raws[2][...] = vectors_ref[...]
    for c in range(0, HALF, D):
        wide_sum[...] = dot(normed_turned[...], grad_ref[:, :, c : c + D].reshape(tokens, D))
        if not tree:
            raws[0][:, c : c + D] = wide_sum[...]
        elif c < SPLIT:
            emit_blocks("x", reader(wide_sum, 64, 16, 0, slice(0, D)), D, c, *raws[:3])
        else:
            emit_blocks("y", reader(wide_sum, 64, 16, 0, slice(0, D)), D, c - SPLIT, *raws[3:])


def layer_kernel(gated_ref, shrink, own_ref, core_ref, pair_ref, total):
    members, rows_here, quarter = total.shape[:3]
    narrow = lax.axis_index("narrow")
    for row in range(rows_here):
        added = dot(gated_ref[row], shrink[...])
        for member in range(members):
            total[member ^ narrow, row] = added[member * quarter : (member + 1) * quarter].astype(BF16)
    own_ref[...] = total[0]
    core_ref[...] = total[1]
    pair_ref[0] = total[2]
    pair_ref[1] = total[3]


def back_kernel(
    gate_grad_ref, content_grad_ref, gate_weight, weight, xhat_ref, scale_ref, gains_ref, layer_core, layer_pair,
    own_ref, core_ref, pair_ref, total,
):
    members, rows_here, quarter = total.shape[:3]
    narrow = lax.axis_index("narrow")
    for row in range(rows_here):
        grad_normed = dot(gate_grad_ref[row], gate_weight[...], ((1,), (1,))) + dot(
            content_grad_ref[row], weight[...], ((1,), (1,))
        )
        for member in range(members):
            here = slice(member * quarter, (member + 1) * quarter)
            xhat = xhat_ref[row, here, :].astype(F32)
            scaled = grad_normed[here] * gains_ref[0:1, :D]
            first_mean = jnp.mean(scaled, axis=1, keepdims=True)
            second_mean = jnp.mean(scaled * xhat, axis=1, keepdims=True)
            scale = scale_ref[row, here, 0:1]
            total[member ^ narrow, row] = ((scaled - first_mean - xhat * second_mean) * scale).astype(BF16)
    own_ref[...] = total[0]
    core_ref[0] = total[1]
    core_ref[1] = layer_core[...]
    for j in range(2):
        pair_ref[j, 0] = total[2 + j]
        pair_ref[j, 1] = layer_pair[j]


def give_kernel(
    cots_ref, acts_ref, grad_own, layer_own, core_ref, side_ref, forward_ref, grad_out, layer_out, grads, layers, sems
):
    rows_here = grad_own.shape[0]
    narrow = lax.axis_index("narrow")
    stores = []
    for kind, (base, own, total, out) in enumerate(
        ((cots_ref, grad_own, grads, grad_out), (acts_ref, layer_own, layers, layer_out))
    ):
        parts = [own, core_ref.at[kind], side_ref.at[0, kind], forward_ref.at[1, kind]]
        for j, part in enumerate(parts):
            rows = pl.ds((narrow ^ j) * rows_here, rows_here)
            total[j] = (base[rows].astype(F32) + part[...].astype(F32)).astype(total.dtype)
            stores.append(pltpu.make_async_copy(total.at[j], out.at[rows], sems.at[kind, j]))
            stores[-1].start()
    for store in stores:
        store.wait()


def sum_three(near_ref, came_ref, far_ref, half, columns):
    values = near_ref[half, :, :, columns].astype(F32) + came_ref[0, half, :, :, columns].astype(F32)
    return values + far_ref[half, :, :, columns].astype(F32)


def side_kernel(*refs):
    for i, out_ref in enumerate(refs[6:]):
        near, came, far = refs[3 * i : 3 * i + 3]
        for c in range(0, near.shape[3], LANES):
            out_ref[:, :, c : c + LANES] = sum_three(near, came, far, 1, slice(c, c + LANES)).astype(BF16)


def fold_kernel(*refs):
    sides, outputs = refs[12:16], refs[16:]
    first = 0
    for i in range(4):
        near, came, far = refs[3 * i : 3 * i + 3]
        for c in range(0, near.shape[3], LANES):
            place = slice(c, c + LANES)
            total = sum_three(near, came, far, 0, place) + sides[i][:, :, place].astype(F32)
            there = slice(first + c, first + c + LANES)
            outputs[0][:, there] = total[0]
            for step in range(1, 4):
                outputs[step][:, there] = total[step].astype(BF16)
        first += near.shape[3]


def norm_kernel(mine_ref, one_ref, two_ref, three_ref, weight_ref, gains_ref, low_ref, message_ref):
    wide, narrow = lax.axis_index("wide"), lax.axis_index("narrow")
    columns = mine_ref.shape[1]
    squares = jnp.zeros((BLOCK, LANES), F32)
    products = jnp.zeros((BLOCK, LANES), F32)
    here = run(narrow * BLOCK, BLOCK)
    for c in range(0, columns, LANES):
        place = slice(c, c + LANES)
        total = mine_ref[:, place]
        for ref in (one_ref, two_ref, three_ref):
            total = total + ref[:, place].astype(F32)
        low = total.astype(BF16)
        low_ref[:, place] = low
        value = low.astype(F32)
        square = value * value
        squares = squares + (square if c < columns - LANES else jnp.where(narrow == 0, square, 0.0))
        at = expand_column(c)
        if at is not None:
            weight = weight_ref[here, at : at + LANES].astype(BF16).astype(F32)
            products = products + value * weight
    first = wide * 64 + narrow * BLOCK
    lanes = lax.broadcasted_iota(jnp.int32, (BLOCK, D), 1)
    diagonal = lanes == lax.broadcasted_iota(jnp.int32, (BLOCK, D), 0) + first
    gain = jnp.sum(jnp.where(diagonal, gains_ref[0:1, :D], 0.0), axis=1, keepdims=True)
    first_raw = jnp.sum(products, axis=1, keepdims=True) / gain
    total = jnp.sum(squares) + jnp.sum(first_raw * first_raw)
    places = jnp.sum(jnp.where(diagonal, first_raw, 0.0), axis=0, keepdims=True)
    message_ref[...] = jnp.full(message_ref.shape, total, F32)
    for k in range(D // LANES):
        message_ref[k : k + 1, :] = places[:, k * LANES : (k + 1) * LANES]


def expand_column(c):
    right = HALF + SPLIT
    turn = right + HALF
    if c < right:
        return c
    if turn <= c < turn + HALF - SPLIT:
        return c - HALF
    return None


def adam_kernel(message_ref, own_ref, side_ref, other_ref, *refs):
    states, vectors, outputs, vector_outputs, norm_ref = refs[:12], refs[12:20], refs[20:35], refs[35:45], refs[45]
    results, blocks, sem = refs[46:61], refs[61], refs[62]
    wide, narrow = lax.axis_index("wide"), lax.axis_index("narrow")
    norm = jnp.sqrt(message_ref[4:5, :])
    norm_ref[0, 0] = jnp.max(norm)
    clip = CLIP_LIMIT / jnp.maximum(norm, CLIP_LIMIT)
    right = HALF + SPLIT
    turn = right + HALF
    blocks[narrow] = own_ref[...]
    blocks[narrow ^ 1] = other_ref[0]
    blocks[narrow ^ 2] = side_ref[...]
    blocks[narrow ^ 3] = other_ref[1]

    def update(which, gradient, rows, place):
        weight, momentum, variance, average = [ref[rows, place] for ref in states[4 * which : 4 * which + 4]]
        updates = adam_update(
            weight, gradient.astype(F32), momentum, variance, average, clip, RATE_MATRIX, DECAY_MATRIX
        )
        for ref, value in zip(results[5 * which : 5 * which + 5], updates):
            ref[rows, place] = value

    def do_member(member, carry):
        thin = run(member * BLOCK, BLOCK)
        for c in range(0, turn + HALF - SPLIT + ROW, LANES):
            gradient = blocks[member, :, c : c + LANES]
            at = expand_column(c)
            if at is not None:
                update(0, gradient, thin, slice(at, at + LANES))
            elif c < turn:
                k, at = (c - right) // D, (c - right) % D
                update(1, gradient, run(member * 48 + k * BLOCK, BLOCK), slice(at, at + LANES))
            else:
                at = c - turn - (HALF - SPLIT)
                update(2, gradient, thin, slice(at, at + LANES))
        for i in range(15):
            rows = run(member * 48, 48) if 5 <= i < 10 else thin
            pltpu.make_async_copy(results[i].at[rows, :], outputs[i].at[rows, :], sem.at[i]).start()
        return carry

    lax.fori_loop(0, 4, do_member, 0)
    own = blocks[0, :, turn + HALF - SPLIT + ROW :].astype(F32)
    gains = jnp.where(wide == 0, message_ref[0:2, :], jnp.where(wide == 1, message_ref[2:4, :], own[0:2, :]))
    for which, gradient in ((0, gains), (1, own[2:3, :64])):
        weight, momentum, variance, average = [ref[...] for ref in vectors[4 * which : 4 * which + 4]]
        updates = adam_update(
            weight, gradient, momentum, variance, average, clip[:, : gradient.shape[1]], RATE_VECTOR, 0.0
        )
        for ref, value in zip(vector_outputs[5 * which : 5 * which + 5], updates):
            ref[...] = value
    for i in range(15):
        pltpu.make_async_copy(results[i], outputs[i], sem.at[i]).wait()


def call_kernel(kernel, name, args, in_specs, out_types, scratch, flops, limit=VMEM_LIMIT):
    vmem = pl.BlockSpec(memory_space=pltpu.VMEM)
    specs = [kind[1] if isinstance(kind, tuple) else vmem for kind in out_types]
    types = [
        kind[0] if isinstance(kind, tuple) else pltpu.VMEM(kind.shape, kind.dtype) for kind in out_types
    ]
    in_specs = [vmem if spec is None else spec for spec in in_specs]
    args = [
        pltpu.with_memory_space_constraint(value, pltpu.HBM) if spec.memory_space == pltpu.HBM else value
        for value, spec in zip(args, in_specs)
    ]
    results = pl.pallas_call(
        kernel,
        name=name,
        in_specs=in_specs,
        out_specs=specs,
        out_shape=types,
        scratch_shapes=scratch,
        compiler_params=pltpu.CompilerParams(vmem_limit_bytes=limit),
        cost_estimate=pl.CostEstimate(flops=int(flops), bytes_accessed=int(flops / 500), transcendentals=0),
    )(*args)
    return list(results)


def swap_with(value, axis, size, bit):
    return lax.ppermute(value, axis, [(i, i ^ bit) for i in range(size)])


def after(value, *others):
    return lax.optimization_barrier((value,) + others)[0]


def sum_core(keep_far, came):
    return (keep_far.astype(F32) + came[1].astype(F32)).astype(BF16)


def adam_update(weight, gradient, momentum, variance, average, clip_scale, step_rate, decay_rate):
    ema_rate = min(EMA_DECAY, (1.0 + STEP) / (10.0 + STEP))
    clipped = clip_scale * gradient
    moment = BETA_FIRST * momentum + (1.0 - BETA_FIRST) * clipped
    square = BETA_SECOND * variance + (1.0 - BETA_SECOND) * clipped * clipped
    first_hat = moment * (1.0 / (1.0 - BETA_FIRST**STEP))
    second_hat = square * (1.0 / (1.0 - BETA_SECOND**STEP))
    updated = weight - step_rate * (
        first_hat / (jnp.sqrt(second_hat) + ADAM_EPS) + decay_rate * weight
    )
    smoothed = ema_rate * average + (1.0 - ema_rate) * updated
    return (clipped, moment, square, updated, smoothed)


def on_device(
    activations,
    cotangent,
    doc_lengths,
    expand_weight,
    expand_momentum,
    expand_variance,
    expand_average,
    shrink_weight,
    shrink_momentum,
    shrink_variance,
    shrink_average,
    spatial_weight,
    spatial_momentum,
    spatial_variance,
    spatial_average,
    norm_gains,
    gains_momentum,
    gains_variance,
    gains_average,
    spatial_bias,
    bias_momentum,
    bias_variance,
    bias_average,
):
    narrow_size, wide_size = lax.axis_size("narrow"), lax.axis_size("wide")
    wide, narrow = lax.axis_index("wide"), lax.axis_index("narrow")
    group_rows, quarter = activations.shape[0], activations.shape[1]
    rows = group_rows // narrow_size
    tokens = rows * ROW
    tree = (wide_size, narrow_size) == (8, 4)
    smem = pl.BlockSpec(memory_space=pltpu.SMEM)
    anywhere = pl.BlockSpec(memory_space=pl.ANY)
    stored = pl.BlockSpec(memory_space=pltpu.HBM)
    shape = jax.ShapeDtypeStruct
    dma = pltpu.SemaphoreType.DMA
    part = shape((rows, quarter, D), BF16)
    product = 2 * tokens * HALF * D
    cross_x = lambda value: swap_with(value, "wide", wide_size, 1)
    cross_y = lambda value: swap_with(value, "narrow", narrow_size, 2)
    cross_core = lambda value: swap_with(value, "narrow", narrow_size, 1)

    def trade(core_part, pair):
        side = cross_y(pair)
        return [cross_core(core_part), side, cross_core(side)]

    def stack(values):
        kind = shape((len(values), *values[0].shape), values[0].dtype)
        return call_kernel(stack_kernel, "stack", values, [None] * len(values), [kind], [], product // 64)[0]

    def add(*values):
        kind = shape(values[0].shape, values[0].dtype)
        return call_kernel(add_kernel, "add", values, [None] * len(values), [kind], [], product // 64)[0]

    pair = shape((2, *part.shape), BF16)

    def cut(acts, cots):
        return call_kernel(
            cut_kernel,
            "cut",
            [acts, cots],
            [stored] * 2,
            [(pair, stored), (shape((2, *pair.shape), BF16), stored)],
            [dma((6,))],
            product // 64,
        )

    if tree:
        first_own = call_kernel(
            pack_first_kernel,
            "pack_first",
            [expand_weight, spatial_weight, norm_gains.reshape(2, LANES), spatial_bias.reshape(1, 64)],
            [stored] * 4,
            [shape((32, HALF + ROW + VECTOR_LANES), BF16)],
            [pltpu.VMEM((32, HALF), F32), pltpu.VMEM((32, ROW), F32), pltpu.VMEM((2, LANES), F32)]
            + [pltpu.VMEM((1, 64), F32), dma((4,))],
            product // 64,
        )[0]
        over_z = lambda own: [swap_with(own, "wide", wide_size, 2 * s) for s in range(1, 4)]
        came_z = over_z(first_own)
        core_cut, pair_cut = cut(after(activations, first_own), cotangent)
        side_came = cross_y(pair_cut)
        expand_own, shrink_own = call_kernel(
            pack_second_kernel,
            "pack_second",
            [expand_weight, shrink_weight],
            [stored, stored],
            [shape((32, HALF), BF16)] * 2,
            [pltpu.VMEM((32, HALF), F32), pltpu.VMEM((96, D), F32), dma((2,))],
            product // 64,
        )
        *came_z, core_came, _, expand_own = lax.optimization_barrier(
            (*came_z, cross_core(core_cut), pair_cut, expand_own)
        )
        first_near = stack([first_own, *came_z])
        first_across = cross_x(first_near)
        expand_own = after(expand_own, first_near)
        *came_z, side_came = lax.optimization_barrier((*over_z(expand_own), side_came))
        expand_near = stack([expand_own, *came_z])
        expand_across = cross_x(after(expand_near, first_across))
        shrink_own = after(shrink_own, expand_near)
        shrink_came = over_z(shrink_own)
        near_core = cross_core(after(first_near, expand_near))
        across_core = cross_core(after(first_across, expand_near))
        forward_came = cross_core(after(side_came, expand_near))
        first_pieces = [after(first_near, expand_near), first_across, near_core, across_core]
        small_pieces = first_pieces[:2]
        near_other = cross_core(expand_near)
        count = len(PIECES)
    else:
        gather = lambda value: lax.all_gather(value.astype(BF16), "wide", axis=0, tiled=True)
        expand_low = gather(expand_weight)
        gains_low, bias_low = gather(norm_gains), gather(spatial_bias)
        small = jnp.concatenate(
            [
                gains_low.reshape(8, 2, 128),
                jnp.pad(bias_low.reshape(8, 1, 64), ((0, 0), (0, 0), (0, 64))),
                jnp.zeros((8, 13, 128), BF16),
            ],
            axis=1,
        )
        first_pieces = [expand_low[:, HALF:], gather(spatial_weight)]
        small_pieces = [small, small]
        expand_pieces, shrink_pieces = [expand_low[:, :HALF]], [gather(shrink_weight)]
        core_came, side_came, forward_came = trade(*cut(activations, cotangent))
        count = 2

    low_d, low_half = shape((rows, ROW, D), BF16), shape((rows, ROW, HALF), BF16)
    thin = shape((rows, ROW, 128), F32)
    weight_type = shape((D, HALF), BF16)

    normed, xhat, scale, gate_normed, slope, rstd, spatial_low, gains, bias_col, gate_weight = call_kernel(
        functools.partial(gating_kernel, tree, count, narrow_size),
        "gating",
        [activations, core_came, side_came, forward_came] + list(first_pieces) + list(small_pieces),
        [stored] + [anywhere] * (narrow_size - 1 + count + 2),
        [low_d, low_d, thin, low_half, low_half, thin]
        + [shape((ROW, ROW), BF16), shape((8, D + HALF), F32), shape((ROW, 128), F32), weight_type],
        [
            pltpu.VMEM((8, BLOCK, 128), BF16),
            pltpu.VMEM((narrow_size, *part.shape), BF16),
            pltpu.VMEM((ROW, HALF), F32),
            pltpu.VMEM((ROW, 128), F32),
            dma((4,)),
        ],
        product // 64,
    )

    bias_late = bias_col
    if tree:
        *shrink_came, expand_across, _ = lax.optimization_barrier((*shrink_came, expand_across, normed))
        shrink_near = stack([shrink_own, *shrink_came])
        shrink_across = cross_x(shrink_near)
        expand_pieces = [expand_near, expand_across, near_other, cross_core(expand_across)]
        bias_late = after(bias_col, shrink_near)
    mixed = call_kernel(
        mixing_kernel,
        "mixing",
        [doc_lengths, spatial_low, gate_normed, bias_late],
        [smem] + [None] * 3,
        [low_half],
        [],
        product // 64,
    )[0]
    normed_late = normed
    if tree:
        expand_pieces[3], normed_late, _ = lax.optimization_barrier((expand_pieces[3], normed, mixed))
    content, content_slope, content_weight, cots_turned, cots = call_kernel(
        functools.partial(content_up_kernel, tree, narrow_size),
        "content_up",
        [normed_late, cotangent, core_came, side_came, forward_came, *expand_pieces],
        [None, stored] + [anywhere] * (narrow_size - 1 + len(expand_pieces)),
        [low_half, low_half, weight_type, shape((D, tokens), BF16), shape((tokens, D), BF16)],
        [dma((2,))],
        product // 64,
    )
    if tree:
        shrink_across, _ = lax.optimization_barrier((shrink_across, content))
        shrink_pieces = [shrink_near, shrink_across, cross_core(shrink_near), cross_core(shrink_across)]

    def raw_outputs(column_list, plain):
        if tree:
            return [
                shape(size, BF16)
                for columns in column_list
                for size in ((2, 4, BLOCK, columns), (2, 4, BLOCK, columns), (2, 2, 4, BLOCK, columns))
            ]
        return [shape(size, F32) for size in plain]

    gated, content_grad, grad_mixed, bias_part, shrink_low, *shrink_raws = call_kernel(
        functools.partial(content_down_kernel, tree, len(shrink_pieces)),
        "content_down",
        [doc_lengths, content, content_slope, mixed, cots, cots_turned, *shrink_pieces],
        [smem] + [None] * 5 + [anywhere] * len(shrink_pieces),
        [low_half, low_half, low_half, shape((ROW, 128), F32), shape((HALF, D), BF16)]
        + raw_outputs((HALF,), ((HALF, D),)),
        [pltpu.VMEM((tokens, 128), F32), pltpu.VMEM((HALF, D), BF16), dma(())],
        product // 64,
    )
    if tree:
        came = {"shrink": cross_core(shrink_raws[2])}
    sum_scratch = [pltpu.VMEM((D, tokens), BF16), pltpu.VMEM((D, D), F32)]
    content_raws = call_kernel(
        functools.partial(content_sum_kernel, tree),
        "content_sum",
        [normed, content_grad],
        [None] * 2,
        raw_outputs((HALF,), ((D, HALF),)),
        sum_scratch,
        product // 64,
    )
    mixed_late = grad_mixed
    if tree:
        came["shrink"], content_raws[0] = lax.optimization_barrier((came["shrink"], content_raws[0]))
        came["content"] = cross_core(content_raws[2])
        far = {"shrink": sum_core(shrink_raws[1], came["shrink"])}
        came_far = {"shrink": cross_y(far["shrink"])}
        mixed_late = after(grad_mixed, far["shrink"])
    square_sum = call_kernel(
        spatial_sum_kernel,
        "spatial_sum",
        [doc_lengths, mixed_late, gate_normed],
        [smem, None, None],
        [shape((ROW, ROW), F32)],
        [],
        product // 64,
    )[0]
    if tree:
        came["content"], square_sum = lax.optimization_barrier((came["content"], square_sum))
        far["content"] = sum_core(content_raws[1], came["content"])
        came_far["content"] = cross_x(far["content"])
        mixed_late = after(grad_mixed, far["content"])

    gate_grad, vectors = call_kernel(
        gate_back_kernel,
        "gate_back",
        [doc_lengths, mixed_late, gate_normed, slope, rstd, spatial_low, gains, bias_part],
        [smem] + [None] * 7,
        [low_half, shape((8, BLOCK, 128), F32)],
        [
            pltpu.VMEM((ROW, ROW), BF16),
            pltpu.VMEM((ROW, HALF), BF16),
            pltpu.VMEM((ROW, 128), F32),
            pltpu.VMEM((ROW, 128), F32),
            pltpu.VMEM((8, HALF), F32),
            pltpu.VMEM((8, HALF), F32),
        ],
        product // 64,
    )
    normed_late = normed
    if tree:
        came_far["shrink"], normed_late = lax.optimization_barrier((came_far["shrink"], normed))
    second_raws = call_kernel(
        functools.partial(gate_sum_kernel, tree),
        "gate_sum",
        [normed_late, gate_grad, square_sum, vectors],
        [None] * 4,
        raw_outputs((SPLIT, HALF - SPLIT + ROW + VECTOR_LANES), ((D, HALF), (ROW, ROW), (8, BLOCK, 128))),
        sum_scratch,
        product // 64,
    )
    def side_step(terms, widths):
        kinds = [shape((4, BLOCK, width), BF16) for width in widths]
        return call_kernel(side_kernel, "side", terms, [None] * 6, kinds, [], product // 64)

    gated_late = gated
    if tree:
        second_raws[2], second_raws[5], came_far["content"] = lax.optimization_barrier(
            (second_raws[2], second_raws[5], came_far["content"])
        )
        second_came = [cross_core(second_raws[i]) for i in (2, 5)]
        first_terms = [content_raws[0], came["content"], came_far["content"]]
        first_terms += [shrink_raws[0], came["shrink"], came_far["shrink"]]
        first_sides = side_step(first_terms, (HALF, HALF))
        first_came_side = [cross_y(first_sides[0]), cross_x(first_sides[1])]
        gated_late = after(gated, second_raws[0], *first_sides)
    part_scratch = pltpu.VMEM((narrow_size, *part.shape), BF16)
    layer_own, layer_core, layer_pair = call_kernel(
        layer_kernel,
        "layer",
        [gated_late, shrink_low],
        [None] * 2,
        [part, part, pair],
        [part_scratch],
        product // 64,
    )
    grad_late = gate_grad
    if tree:
        *second_came, layer_own = lax.optimization_barrier((*second_came, layer_own))
        second_far = [sum_core(second_raws[1], second_came[0]), sum_core(second_raws[4], second_came[1])]
        second_came_far = [cross_x(second_far[0]), cross_y(second_far[1])]
        grad_late = after(gate_grad, *second_far)
    grad_own, core_back, pair_back = call_kernel(
        back_kernel,
        "back",
        [grad_late, content_grad, gate_weight, content_weight, xhat, scale, gains, layer_core, layer_pair],
        [None] * 9,
        [part, pair, shape((2, *pair.shape), BF16)],
        [part_scratch],
        product // 64,
    )

    def give(cots_base, acts_base, returned):
        whole = (group_rows, quarter, D)
        return call_kernel(
            give_kernel,
            "give",
            [cots_base, acts_base, grad_own, layer_own, *returned],
            [None] * 7,
            [(shape(whole, F32), stored), (shape(whole, BF16), stored)],
            [
                pltpu.VMEM((narrow_size, *part.shape), F32),
                pltpu.VMEM((narrow_size, *part.shape), BF16),
                dma((2, narrow_size)),
            ],
            product // 64,
        )

    if tree:
        columns = HALF + HALF + SPLIT + (HALF - SPLIT) + ROW + VECTOR_LANES
        tied = lax.optimization_barrier((*second_came_far, *first_came_side, grad_own))
        second_came_far, first_came_side, grad_own = tied[:2], tied[2:4], tied[4]
        second_terms = [second_raws[0], second_came[0], second_came_far[0]]
        second_terms += [second_raws[3], second_came[1], second_came_far[1]]
        second_sides = side_step(second_terms, (SPLIT, HALF - SPLIT + ROW + VECTOR_LANES))
        second_came_side = [cross_y(second_sides[0]), cross_x(second_sides[1])]
        terms = first_terms[:3] + second_terms[:3] + first_terms[3:] + second_terms[3:]
        came_side = [first_came_side[0], second_came_side[0], first_came_side[1], second_came_side[1]]
        mine, *sent = call_kernel(
            fold_kernel,
            "fold",
            terms + came_side,
            [None] * 16,
            [shape((BLOCK, columns), F32)] + [shape((BLOCK, columns), BF16)] * 3,
            [],
            product // 64,
        )
        came_z = [swap_with(sent[s - 1], "wide", wide_size, 2 * s) for s in range(1, 4)]
        matrices = [expand_weight, expand_momentum, expand_variance, expand_average]
        matrices += [shrink_weight, shrink_momentum, shrink_variance, shrink_average]
        matrices += [spatial_weight, spatial_momentum, spatial_variance, spatial_average]
        fetched = [*matrices, cotangent, activations]
        states = call_kernel(
            fetch_kernel,
            "fetch",
            list(lax.optimization_barrier((*fetched, sent[0]))[:14]),
            [stored] * 14,
            [shape(value.shape, value.dtype) for value in fetched],
            [dma((14,))],
            product // 64,
        )
        states, bases = states[:12], states[12:]
        side_back = cross_y(after(pair_back, sent[0]))
        core_back = cross_core(after(core_back, sent[0]))
        *came_z, first_state = lax.optimization_barrier((*came_z, states[0]))
        low, message = call_kernel(
            norm_kernel,
            "norm",
            [mine, *came_z, first_state, gains],
            [None] * 6,
            [shape((BLOCK, columns), BF16), shape((8, LANES), F32)],
            [],
            product // 64,
        )
        side = cross_y(low)
        message = add(message, cross_core(message))
        message = add(message, cross_x(message))
        *arrived, side, side_back = lax.optimization_barrier((*over_z(message), side, side_back))
        message = add(message, *arrived)
        other = cross_core(stack([low, side]))
        returned = [core_back, side_back, cross_core(side_back)]
        input_grad, layer_out = give(*bases, returned)
        arrived, layer_out, input_grad = lax.optimization_barrier((cross_y(message), layer_out, input_grad))
        message = add(message, arrived)
        as_rows = lambda value: value.reshape(-1, min(value.shape[0], LANES))
        vector_states = [norm_gains, gains_momentum, gains_variance, gains_average]
        vector_states += [spatial_bias, bias_momentum, bias_variance, bias_average]
        vector_kinds = [shape((2, LANES), F32)] * 5 + [shape((1, 64), F32)] * 5
        *updates, norm_row = call_kernel(
            adam_kernel,
            "adam",
            [message, low, side, other, *states] + [as_rows(value) for value in vector_states],
            [None] * 24,
            [(shape(value.shape, F32), stored) for value in (matrices[0], matrices[4], matrices[8]) for _ in range(5)]
            + [(kind, pl.BlockSpec(memory_space=pltpu.VMEM)) for kind in vector_kinds]
            + [(shape((1, 1), F32), smem)],
            [pltpu.VMEM(value.shape, F32) for value in (matrices[0], matrices[4], matrices[8]) for _ in range(5)]
            + [pltpu.VMEM((4, BLOCK, columns), BF16), dma((15,))],
            product // 64,
        )
        grad_norm = norm_row[0, 0]
        results = [layer_out, input_grad, grad_norm, *updates[:15]]
        return tuple(results + [value.reshape(-1) for value in updates[15:]])

    returned = trade(core_back, pair_back)
    input_grad, layer_out = give(cotangent, activations, returned)
    gains_size, bias_size = norm_gains.shape[0], spatial_bias.shape[0]
    vectors = lax.psum(second_raws[2], ("narrow", "wide"))
    totals = lax.psum(
        (jnp.concatenate([content_raws[0], second_raws[0]], axis=1), shrink_raws[0], second_raws[1]), "narrow"
    )
    expand_shard, shrink_shard, spatial_shard = [
        lax.psum_scatter(total, "wide", scatter_dimension=0, tiled=True) for total in totals
    ]
    second_shard = lax.dynamic_slice_in_dim(vectors[:, :2].reshape(-1), wide * gains_size, gains_size)
    bias_shard = lax.dynamic_slice_in_dim(vectors[:, 2, :64].reshape(-1), wide * bias_size, bias_size)
    low_weight = expand_weight.astype(BF16).astype(F32)
    height = expand_weight.shape[0]
    first_gain = lax.dynamic_slice_in_dim(gains[0], wide * height, height)
    first_raw = jnp.sum(low_weight * expand_shard, axis=1) / first_gain
    squares = [expand_shard, shrink_shard, spatial_shard, second_shard, bias_shard, first_raw]
    square_total = lax.psum(sum(jnp.sum(value * value) for value in squares), "wide")
    first_all = lax.all_gather(first_raw, "wide", axis=0, tiled=True)
    first_all = jnp.concatenate([first_all, jnp.zeros((HALF,), F32)])
    gains_shard = second_shard + lax.dynamic_slice_in_dim(first_all, wide * gains_size, gains_size)
    grad_norm = jnp.sqrt(square_total)
    clip_scale = CLIP_LIMIT / jnp.maximum(grad_norm, CLIP_LIMIT)
    results = [layer_out, input_grad, grad_norm]
    for weight, shard, momentum, variance, average, rate, decay in (
        (expand_weight, expand_shard, expand_momentum, expand_variance, expand_average, RATE_MATRIX, DECAY_MATRIX),
        (shrink_weight, shrink_shard, shrink_momentum, shrink_variance, shrink_average, RATE_MATRIX, DECAY_MATRIX),
        (spatial_weight, spatial_shard, spatial_momentum, spatial_variance, spatial_average, RATE_MATRIX, DECAY_MATRIX),
        (norm_gains, gains_shard, gains_momentum, gains_variance, gains_average, RATE_VECTOR, 0.0),
        (spatial_bias, bias_shard, bias_momentum, bias_variance, bias_average, RATE_VECTOR, 0.0),
    ):
        results += adam_update(weight, shard, momentum, variance, average, clip_scale, rate, decay)
    return tuple(results)


def solution(mesh):
    tokens, matrix, vector = P("wide", "narrow", None), P("wide", None), P("wide")
    return jax.shard_map(
        on_device,
        mesh=mesh,
        in_specs=(tokens, tokens) + (matrix,) * 13 + (vector,) * 8,
        out_specs=(tokens, tokens, P()) + (matrix,) * 15 + (vector,) * 10,
        check_vma=False,
    )
```

```python
import functools

import jax
import jax.numpy as jnp
from jax import lax
from jax.experimental import pallas as pl
from jax.experimental.pallas import tpu as pltpu
from jax.sharding import PartitionSpec as P

D = 512
FF = 3072
ROW = 512
DOCS = 5
STEP = 10
HALF = 1536

LAYER_EPS = 1e-05
CLIP_LIMIT = 1.0
BETA_FIRST = 0.9
BETA_SECOND = 0.999
ADAM_EPS = 1e-08
RATE_MATRIX = 0.03
RATE_VECTOR = 0.2
DECAY_MATRIX = 0.1
EMA_DECAY = 0.9999

F32 = jnp.float32
BF16 = jnp.bfloat16
GELU_A = 0.7978845608028654
GELU_B = GELU_A * 0.044715
LANES = 128
CHUNK = 64
PIECE = 32
BLOCK = 16
VMEM_LIMIT = 16 * 1024 * 1024

PIECES = ((0, 0), (1, 0), (0, 1), (1, 1))
WIDTH = 256
SPLIT = 1024
VECTOR_LANES = 128


def gelu_gate(hidden):
    squares = hidden * hidden
    gate = 0.5 * jnp.tanh(hidden * (GELU_A + GELU_B * squares)) + 0.5
    return squares, gate


def gelu_slope(hidden, squares, gate):
    return gate * (1.0 + hidden * (1.0 - gate) * (2.0 * GELU_A + 6.0 * GELU_B * squares))


def doc_ids(places, lens_ref, row):
    bound = jnp.int32(0)
    ids = jnp.zeros(places.shape, jnp.int32)
    for k in range(DOCS - 1):
        bound = bound + lens_ref[row, k]
        ids = ids + (places >= bound).astype(jnp.int32)
    return ids


def doc_mask(start, rows, lens_ref, row):
    across = doc_ids(lax.broadcasted_iota(jnp.int32, (1, ROW), 1), lens_ref, row)
    down = doc_ids(lax.broadcasted_iota(jnp.int32, (rows, 1), 0) + start, lens_ref, row)
    live = down != DOCS - 1
    return jnp.where(live, down, -1) == across, live


def dot(left, right, dims=((1,), (0,))):
    return lax.dot_general(left, right, (dims, ((), ())), preferred_element_type=F32)


def run(start, size):
    return pl.ds(pl.multiple_of(start, size), size)


def fetch_weights(sources, moves, tree):
    if not tree:
        for source, (_, _, _, target, _, _, _, sem) in zip(sources, moves):
            pltpu.make_async_copy(source, target, sem).start()
        return
    wide, core = lax.axis_index("wide"), lax.axis_index("narrow") & 1
    for base, first, count, target, height, unit, shift, sem in moves:
        for i, (x_off, core_off) in enumerate(PIECES):
            for step in range(4):
                start = (wide ^ (2 * step + x_off)) * height + (core ^ core_off) * unit + shift
                pltpu.make_async_copy(
                    sources[base + i].at[step, :, pl.ds(first, count)], target.at[run(start, 32), :], sem
                ).start()


def wait_weights(targets):
    for target, sem in targets:
        pltpu.make_async_copy(target, target, sem).wait()


def cut_copies(acts_ref, cots_ref, core_out, pair_out, sems):
    rows_here = core_out.shape[1]
    narrow = lax.axis_index("narrow")
    copies = []
    for i, ref in enumerate((acts_ref, cots_ref)):
        for j, target in ((1, core_out.at[i]), (2, pair_out.at[0, i]), (3, pair_out.at[1, i])):
            source = ref.at[pl.ds((narrow ^ j) * rows_here, rows_here)]
            copies.append(pltpu.make_async_copy(source, target, sems.at[len(copies)]))
    return copies


def cut_kernel(acts_ref, cots_ref, core_out, pair_out, sems):
    copies = cut_copies(acts_ref, cots_ref, core_out, pair_out, sems)
    for copy in copies:
        copy.start()
    for copy in copies:
        copy.wait()


def open_kernel(
    acts_ref, cots_ref, expand_ref, spatial_ref, gains_ref, bias_ref, core_out, pair_out, out_ref,
    expand, spatial, gains, bias, sems, cut_sems,
):
    rows = run((lax.axis_index("narrow") & 1) * 32, 32)
    copies = [
        pltpu.make_async_copy(expand_ref.at[rows, pl.ds(HALF, HALF)], expand, sems.at[0]),
        pltpu.make_async_copy(spatial_ref.at[rows, :], spatial, sems.at[1]),
        pltpu.make_async_copy(gains_ref, gains, sems.at[2]),
        pltpu.make_async_copy(bias_ref, bias, sems.at[3]),
    ]
    cuts = cut_copies(acts_ref, cots_ref, core_out, pair_out, cut_sems)
    for copy in copies + cuts:
        copy.start()
    for copy in copies:
        copy.wait()
    vectors = jnp.concatenate(
        [
            gains[...],
            jnp.concatenate([bias[...], jnp.zeros((1, LANES - 64), F32)], axis=1),
            jnp.zeros((29, LANES), F32),
        ],
        axis=0,
    )
    out_ref[:, HALF + ROW :] = vectors.astype(BF16)
    out_ref[:, :HALF] = expand[...].astype(BF16)
    out_ref[:, HALF : HALF + ROW] = spatial[...].astype(BF16)
    for copy in cuts:
        copy.wait()


def pack_second_kernel(expand_ref, shrink_ref, expand_out, shrink_out, expand, shrink, sems):
    core = lax.axis_index("narrow") & 1
    copies = [
        pltpu.make_async_copy(expand_ref.at[run(core * 32, 32), pl.ds(0, HALF)], expand, sems.at[0]),
        pltpu.make_async_copy(shrink_ref.at[run(core * 96, 32 * 3), :], shrink, sems.at[1]),
    ]
    for copy in copies:
        copy.start()
    for copy in copies:
        copy.wait()
    expand_out[...] = expand[...].astype(BF16)
    for k in range(3):
        shrink_out[:, k * D : (k + 1) * D] = shrink[k * 32 : (k + 1) * 32, :].astype(BF16)


def stack_kernel(*refs):
    for i, ref in enumerate(refs[:-1]):
        refs[-1][i] = ref[...]


def add_kernel(*refs):
    total = refs[0][...] + refs[1][...]
    if len(refs) == 5:
        total = total + (refs[2][...] + refs[3][...])
    refs[-1][...] = total


def fetch_kernel(*refs):
    count = (len(refs) - 1) // 2
    copies = [pltpu.make_async_copy(refs[i], refs[count + i], refs[-1].at[i]) for i in range(count)]
    for copy in copies:
        copy.start()
    for copy in copies:
        copy.wait()


def gating_kernel(tree, count, members, own_ref, core_ref, side_ref, forward_ref, *refs):
    parts = [core_ref.at[0], side_ref.at[0, 0], forward_ref.at[1, 0]]
    sources, small_sources = refs[:count], refs[count : count + 2]
    (
        normed_ref, xhat_ref, scale_ref, gate_ref, slope_ref, rstd_ref, spatial_ref, gains_ref, bias_col, weight,
        small, acts, active, sums, sems,
    ) = refs[count + 2 :]
    wide, narrow = lax.axis_index("wide"), lax.axis_index("narrow")
    rows_here, quarter = acts.shape[1:3]

    pltpu.make_async_copy(own_ref.at[pl.ds(narrow * rows_here, rows_here)], acts.at[narrow], sems.at[3]).start()
    for j, part in enumerate(parts):
        pltpu.make_async_copy(part, acts.at[narrow ^ (j + 1)], sems.at[3]).start()
    fetch_weights(
        sources,
        [
            (0, 0, HALF, weight, 64, 32, 0, sems.at[0]),
            (0, HALF, ROW, spatial_ref, 64, 32, 0, sems.at[1]),
        ],
        tree,
    )
    if tree:
        for x_off in range(2):
            for step in range(4):
                pltpu.make_async_copy(
                    small_sources[x_off].at[step, pl.ds(0, BLOCK), pl.ds(HALF + ROW, 128)],
                    small.at[wide ^ (2 * step + x_off)],
                    sems.at[2],
                ).start()
    else:
        pltpu.make_async_copy(small_sources[0], small, sems.at[2]).start()
    wait_weights([(weight, sems.at[0]), (spatial_ref, sems.at[1]), (small, sems.at[2]), (acts, sems.at[3])])
    diagonal = lax.broadcasted_iota(jnp.int32, (64, 128), 0) == lax.broadcasted_iota(jnp.int32, (64, 128), 1)
    for owner in range(8):
        values = small[owner].astype(F32)
        for k in range(2):
            gains_ref[:, owner * 256 + k * 128 : owner * 256 + (k + 1) * 128] = jnp.broadcast_to(
                values[k : k + 1, :], (8, 128)
            )
        column = jnp.sum(jnp.where(diagonal, values[2:3, :], 0.0), axis=1, keepdims=True)
        bias_col[owner * 64 : (owner + 1) * 64, :] = jnp.broadcast_to(column, (64, 128))

    def do_row(row, carry):
        for member in range(members):
            here = slice(member * quarter, (member + 1) * quarter)
            values = acts[member, row].astype(F32)
            shifted = values - jnp.mean(values, axis=1, keepdims=True)
            scale = lax.rsqrt(jnp.mean(shifted * shifted, axis=1, keepdims=True) + LAYER_EPS)
            xhat = shifted * scale
            scale_ref[row, here, :] = jnp.broadcast_to(scale, (quarter, 128))
            xhat_ref[row, here, :] = xhat.astype(BF16)
            normed_ref[row, here, :] = (xhat * gains_ref[0:1, :D]).astype(BF16)

        normed = normed_ref[row]
        for c in range(0, HALF, WIDTH):
            hidden = dot(normed, weight[:, c : c + WIDTH])
            for p in range(0, ROW, PIECE):
                here = slice(p, p + PIECE)
                values = hidden[here]
                squares, gate = gelu_gate(values)
                slope_ref[row, here, c : c + WIDTH] = gelu_slope(values, squares, gate).astype(BF16)
                result = values * gate
                active[here, c : c + WIDTH] = result
                total = result[:, :LANES] + result[:, LANES:]
                sums[here, :] = total if c == 0 else sums[here, :] + total
        for p in range(0, ROW, CHUNK):
            here = slice(p, p + CHUNK)
            centre = jnp.sum(sums[here, :], axis=1, keepdims=True) * (1.0 / HALF)
            total = jnp.zeros((CHUNK, LANES), F32)
            for c in range(0, HALF, LANES):
                shifted = active[here, c : c + LANES] - centre
                total = total + shifted * shifted
            scale = lax.rsqrt(jnp.sum(total, axis=1, keepdims=True) * (1.0 / HALF) + LAYER_EPS)
            rstd_ref[row, here, :] = jnp.broadcast_to(scale, (CHUNK, 128))
            for c in range(0, HALF, LANES):
                vhat = (active[here, c : c + LANES] - centre) * scale
                gate_ref[row, here, c : c + LANES] = (vhat * gains_ref[0:1, D + c : D + c + LANES]).astype(BF16)

        return carry

    lax.fori_loop(0, rows_here, do_row, 0)


def mixing_kernel(lens_ref, spatial_ref, gate_ref, bias_col, mixed_ref):
    rows_here = gate_ref.shape[0]
    narrow = lax.axis_index("narrow")
    for row in range(rows_here):
        same, live = doc_mask(0, ROW, lens_ref, narrow * rows_here + row)
        masked = jnp.where(same, spatial_ref[...], jnp.zeros((), BF16))
        bias = jnp.where(live, bias_col[:, 0:1], 0.0)
        for c in range(0, HALF, D):
            mixed_ref[row, :, c : c + D] = (dot(masked, gate_ref[row, :, c : c + D]) + bias).astype(BF16)


def emit_blocks(order, read, columns, first, keep_near, keep_far, send):
    wide, narrow = lax.axis_index("wide"), lax.axis_index("narrow")
    for core in range(2):
        for one in range(2):
            for two in range(2):
                for step in range(4):
                    x_off, y_off = (one, two) if order == "x" else (two, one)
                    values = read(wide ^ (2 * step + x_off), narrow ^ (2 * y_off + core)).astype(BF16)
                    place = pl.ds(first, columns)
                    if core == 1:
                        send[one, two, step, :, place] = values
                    elif one == 1:
                        keep_far[two, step, :, place] = values
                    else:
                        keep_near[two, step, :, place] = values


def reader(matrix, height, part, shift, columns):
    def read(owner, member):
        return matrix[run(owner * height + member * part + shift, BLOCK), columns]

    return read


def content_up_kernel(tree, members, normed_ref, own_ref, core_ref, side_ref, forward_ref, *refs):
    parts = [core_ref.at[1], side_ref.at[0, 1], forward_ref.at[1, 1]]
    sources, (content_ref, slope_ref, weight, cots_turned, cots, sems) = refs[:-6], refs[-6:]
    narrow = lax.axis_index("narrow")
    rows_here, quarter = core_ref.shape[1:3]
    tokens = rows_here * ROW
    if tree:
        fetch_weights(sources, [(0, 0, HALF, weight, 64, 32, 0, sems.at[0])], tree)
    else:
        pltpu.make_async_copy(sources[0], weight, sems.at[0]).start()
    for r in range(rows_here):
        for j in range(members):
            source = own_ref.at[narrow * rows_here + r] if j == 0 else parts[j - 1].at[r]
            place = run(r * ROW + (narrow ^ j) * quarter, quarter)
            pltpu.make_async_copy(source, cots.at[place, :], sems.at[1]).start()
    wait_weights([(weight, sems.at[0])])

    def do_channels(k, carry):
        channels = run(k * WIDTH, WIDTH)
        hidden = dot(normed_ref[...].reshape(tokens, D), weight[:, channels])
        for p in range(0, tokens, PIECE):
            r, here = p // ROW, slice(p % ROW, p % ROW + PIECE)
            values = hidden[p : p + PIECE]
            squares, gate = gelu_gate(values)
            content_ref[r, here, channels] = (values * gate).astype(BF16)
            slope_ref[r, here, channels] = gelu_slope(values, squares, gate).astype(BF16)
        return carry

    lax.fori_loop(0, HALF // WIDTH, do_channels, 0)
    wait_weights([(cots, sems.at[1])])
    cots_turned[...] = cots[...].T


def content_down_kernel(tree, count, lens_ref, content_ref, slope_ref, mixed_ref, cots, cots_turned, *refs):
    sources = refs[:count]
    gated_ref, grad_ref, grad_mixed_ref, bias_ref, shrink = refs[count : count + 5]
    raws = refs[count + 5 : count + (8 if tree else 6)]
    sums, tall_sum, sem = refs[count + 5 + len(raws) :]
    narrow = lax.axis_index("narrow")
    rows_here = content_ref.shape[0]
    tokens = rows_here * ROW

    if tree:
        fetch_weights(sources, [(0, k * D, D, shrink, 192, 96, k * 32, sem) for k in range(3)], tree)
    else:
        pltpu.make_async_copy(sources[0], shrink, sem).start()
    sums[...] = jnp.zeros_like(sums)
    wait_weights([(shrink, sem)])

    def do_channels(k, carry):
        channels = run(k * WIDTH, WIDTH)
        grad_gated = dot(cots[...], shrink[channels, :], ((1,), (1,)))
        for p in range(0, tokens, PIECE):
            r, here = p // ROW, slice(p % ROW, p % ROW + PIECE)
            grads = grad_gated[p : p + PIECE]
            content = content_ref[r, here, channels].astype(F32)
            mixed = mixed_ref[r, here, channels].astype(F32)
            slope = slope_ref[r, here, channels].astype(F32)
            gated_ref[r, here, channels] = (content * mixed).astype(BF16)
            grad_ref[r, here, channels] = (grads * mixed * slope).astype(BF16)
            grad_mixed = (grads * content).astype(BF16)
            grad_mixed_ref[r, here, channels] = grad_mixed
            total = grad_mixed.astype(F32)
            sums[p : p + PIECE, :] += total[:, :LANES] + total[:, LANES:]
        product = dot(cots_turned[...], gated_ref[:, :, channels].reshape(tokens, WIDTH))
        if tree:
            tall_sum[channels, :] = product.astype(BF16).T
        else:
            raws[0][channels, :] = product.T
        return carry

    lax.fori_loop(0, HALF // WIDTH, do_channels, 0)
    for r in range(rows_here):
        _, live = doc_mask(0, ROW, lens_ref, narrow * rows_here + r)
        part = jnp.where(live, sums[r * ROW : (r + 1) * ROW, :], 0.0)
        bias_ref[...] = part if r == 0 else bias_ref[...] + part
    if tree:
        for j in range(3):
            emit_blocks("y", reader(tall_sum, 192, 48, j * BLOCK, slice(0, D)), D, j * D, *raws)


def content_sum_kernel(tree, normed_ref, grad_ref, *refs):
    raws, normed_turned, wide_sum = refs[:-2], refs[-2], refs[-1]
    tokens = normed_ref.shape[0] * normed_ref.shape[1]
    normed_turned[...] = normed_ref[...].reshape(tokens, D).T
    for c in range(0, HALF, D):
        wide_sum[...] = dot(normed_turned[...], grad_ref[:, :, c : c + D].reshape(tokens, D))
        if tree:
            emit_blocks("x", reader(wide_sum, 64, 16, 0, slice(0, D)), D, c, *raws)
        else:
            raws[0][:, c : c + D] = wide_sum[...]


def spatial_sum_kernel(lens_ref, grad_mixed_ref, gate_ref, square_ref):
    rows_here = grad_mixed_ref.shape[0]
    narrow = lax.axis_index("narrow")
    for row in range(rows_here):
        same, _ = doc_mask(0, ROW, lens_ref, narrow * rows_here + row)
        products = jnp.where(same, dot(grad_mixed_ref[row], gate_ref[row], ((1,), (1,))), 0.0)
        square_ref[...] = products if row == 0 else square_ref[...] + products


def gate_back_kernel(
    lens_ref, grad_mixed_ref, gate_ref, slope_ref, rstd_ref, spatial_ref, gains_ref, bias_ref,
    grad_ref, vectors_ref, turned, grad_gate, first_sums, second_sums, second, inverse,
):
    rows_here = grad_mixed_ref.shape[0]
    narrow = lax.axis_index("narrow")
    turned[...] = spatial_ref[...].T
    second[...] = jnp.zeros_like(second)
    inverse[...] = 1.0 / gains_ref[:, D:]

    def do_row(row, carry):
        same, _ = doc_mask(0, ROW, lens_ref, narrow * rows_here + row)
        masked = jnp.where(same, turned[...], jnp.zeros((), BF16))
        for c in range(0, HALF, WIDTH):
            grads_all = dot(masked, grad_mixed_ref[row, :, c : c + WIDTH])
            vector = jnp.zeros((8, WIDTH), F32)
            for p in range(0, ROW, PIECE):
                here = slice(p, p + PIECE)
                low = grads_all[here].astype(BF16)
                grad_gate[here, c : c + WIDTH] = low
                grads = low.astype(F32)
                products = grads * gate_ref[row, here, c : c + WIDTH].astype(F32)
                vector = vector + jnp.sum(products.reshape(PIECE // 8, 8, WIDTH), axis=0)
                scaled = grads * gains_ref[0:1, D + c : D + c + WIDTH]
                first = scaled[:, :LANES] + scaled[:, LANES:]
                other = products[:, :LANES] + products[:, LANES:]
                first_sums[here, :] = first if c == 0 else first_sums[here, :] + first
                second_sums[here, :] = other if c == 0 else second_sums[here, :] + other
            second[:, c : c + WIDTH] += vector
        for p in range(0, ROW, CHUNK):
            here = slice(p, p + CHUNK)
            scale = rstd_ref[row, here, 0:1]
            first_mean = jnp.sum(first_sums[here, :], axis=1, keepdims=True) * (1.0 / HALF) * scale
            second_mean = jnp.sum(second_sums[here, :], axis=1, keepdims=True) * (1.0 / HALF) * scale
            for c in range(0, HALF, LANES):
                place = slice(c, c + LANES)
                scaled = grad_gate[here, place].astype(F32) * gains_ref[0:1, D + c : D + c + LANES] * scale
                vhat = gate_ref[row, here, place].astype(F32) * inverse[0:1, place]
                slope = slope_ref[row, here, place].astype(F32)
                grad_ref[row, here, place] = ((scaled - first_mean - vhat * second_mean) * slope).astype(BF16)
        return carry

    lax.fori_loop(0, rows_here, do_row, 0)
    vectors_ref[...] = jnp.zeros_like(vectors_ref)
    diagonal = lax.broadcasted_iota(jnp.int32, (64, 128), 0) == lax.broadcasted_iota(jnp.int32, (64, 128), 1)
    for owner in range(8):
        for k in range(2 if owner >= 2 else 0):
            c = (owner - 2) * 256 + k * 128
            total = jnp.sum(second[:, c : c + 128], axis=0, keepdims=True)
            vectors_ref[owner, k : k + 1, :] = total * inverse[0:1, c : c + 128]
        column = jnp.sum(bias_ref[owner * 64 : (owner + 1) * 64, :], axis=1, keepdims=True)
        vectors_ref[owner, 2:3, :] = jnp.sum(jnp.where(diagonal, column, 0.0), axis=0, keepdims=True)


def gate_sum_kernel(tree, normed_ref, grad_ref, square_ref, vectors_ref, *refs):
    raws, normed_turned, wide_sum = refs[:-2], refs[-2], refs[-1]
    tokens = normed_ref.shape[0] * normed_ref.shape[1]
    rest = HALF - SPLIT
    normed_turned[...] = normed_ref[...].reshape(tokens, D).T
    if tree:
        emit_blocks("y", reader(square_ref, 64, 16, 0, slice(0, ROW)), ROW, rest, *raws[3:])
        emit_blocks("y", lambda owner, member: vectors_ref[owner], VECTOR_LANES, rest + ROW, *raws[3:])
    else:
        raws[1][...] = square_ref[...]
        raws[2][...] = vectors_ref[...]
    for c in range(0, HALF, D):
        wide_sum[...] = dot(normed_turned[...], grad_ref[:, :, c : c + D].reshape(tokens, D))
        if not tree:
            raws[0][:, c : c + D] = wide_sum[...]
        elif c < SPLIT:
            emit_blocks("x", reader(wide_sum, 64, 16, 0, slice(0, D)), D, c, *raws[:3])
        else:
            emit_blocks("y", reader(wide_sum, 64, 16, 0, slice(0, D)), D, c - SPLIT, *raws[3:])


def layer_kernel(gated_ref, shrink, own_ref, core_ref, pair_ref, total):
    members, rows_here, quarter = total.shape[:3]
    narrow = lax.axis_index("narrow")
    for row in range(rows_here):
        added = dot(gated_ref[row], shrink[...])
        for member in range(members):
            total[member ^ narrow, row] = added[member * quarter : (member + 1) * quarter].astype(BF16)
    own_ref[...] = total[0]
    core_ref[...] = total[1]
    pair_ref[0] = total[2]
    pair_ref[1] = total[3]


def back_kernel(
    gate_grad_ref, content_grad_ref, gate_weight, weight, xhat_ref, scale_ref, gains_ref, layer_core, layer_pair,
    own_ref, core_ref, pair_ref, total,
):
    members, rows_here, quarter = total.shape[:3]
    narrow = lax.axis_index("narrow")
    for row in range(rows_here):
        grad_normed = dot(gate_grad_ref[row], gate_weight[...], ((1,), (1,))) + dot(
            content_grad_ref[row], weight[...], ((1,), (1,))
        )
        for member in range(members):
            here = slice(member * quarter, (member + 1) * quarter)
            xhat = xhat_ref[row, here, :].astype(F32)
            scaled = grad_normed[here] * gains_ref[0:1, :D]
            first_mean = jnp.mean(scaled, axis=1, keepdims=True)
            second_mean = jnp.mean(scaled * xhat, axis=1, keepdims=True)
            scale = scale_ref[row, here, 0:1]
            total[member ^ narrow, row] = ((scaled - first_mean - xhat * second_mean) * scale).astype(BF16)
    own_ref[...] = total[0]
    core_ref[0] = total[1]
    core_ref[1] = layer_core[...]
    for j in range(2):
        pair_ref[j, 0] = total[2 + j]
        pair_ref[j, 1] = layer_pair[j]


def give_kernel(
    cots_ref, acts_ref, grad_own, layer_own, core_ref, side_ref, forward_ref, grad_out, layer_out, grads, layers, sems
):
    rows_here = grad_own.shape[0]
    narrow = lax.axis_index("narrow")
    stores = []
    for kind, (base, own, total, out) in enumerate(
        ((cots_ref, grad_own, grads, grad_out), (acts_ref, layer_own, layers, layer_out))
    ):
        parts = [own, core_ref.at[kind], side_ref.at[0, kind], forward_ref.at[1, kind]]
        for j, part in enumerate(parts):
            rows = pl.ds((narrow ^ j) * rows_here, rows_here)
            total[j] = (base[rows].astype(F32) + part[...].astype(F32)).astype(total.dtype)
            stores.append(pltpu.make_async_copy(total.at[j], out.at[rows], sems.at[kind, j]))
            stores[-1].start()
    for store in stores:
        store.wait()


def sum_three(near_ref, came_ref, far_ref, half, columns):
    values = near_ref[half, :, :, columns].astype(F32) + came_ref[0, half, :, :, columns].astype(F32)
    return values + far_ref[half, :, :, columns].astype(F32)


def side_kernel(*refs):
    for i, out_ref in enumerate(refs[6:]):
        near, came, far = refs[3 * i : 3 * i + 3]
        for c in range(0, near.shape[3], LANES):
            out_ref[:, :, c : c + LANES] = sum_three(near, came, far, 1, slice(c, c + LANES)).astype(BF16)


def fold_kernel(*refs):
    sides, outputs = refs[12:16], refs[16:]
    first = 0
    for i in range(4):
        near, came, far = refs[3 * i : 3 * i + 3]
        for c in range(0, near.shape[3], LANES):
            place = slice(c, c + LANES)
            total = sum_three(near, came, far, 0, place) + sides[i][:, :, place].astype(F32)
            there = slice(first + c, first + c + LANES)
            outputs[0][:, there] = total[0]
            for step in range(1, 4):
                outputs[step][:, there] = total[step].astype(BF16)
        first += near.shape[3]


def norm_kernel(mine_ref, one_ref, two_ref, three_ref, weight_ref, gains_ref, low_ref, message_ref):
    wide, narrow = lax.axis_index("wide"), lax.axis_index("narrow")
    columns = mine_ref.shape[1]
    squares = jnp.zeros((BLOCK, LANES), F32)
    products = jnp.zeros((BLOCK, LANES), F32)
    here = run(narrow * BLOCK, BLOCK)
    for c in range(0, columns, LANES):
        place = slice(c, c + LANES)
        total = mine_ref[:, place]
        for ref in (one_ref, two_ref, three_ref):
            total = total + ref[:, place].astype(F32)
        low = total.astype(BF16)
        low_ref[:, place] = low
        value = low.astype(F32)
        square = value * value
        squares = squares + (square if c < columns - LANES else jnp.where(narrow == 0, square, 0.0))
        at = expand_column(c)
        if at is not None:
            weight = weight_ref[here, at : at + LANES].astype(BF16).astype(F32)
            products = products + value * weight
    first = wide * 64 + narrow * BLOCK
    lanes = lax.broadcasted_iota(jnp.int32, (BLOCK, D), 1)
    diagonal = lanes == lax.broadcasted_iota(jnp.int32, (BLOCK, D), 0) + first
    gain = jnp.sum(jnp.where(diagonal, gains_ref[0:1, :D], 0.0), axis=1, keepdims=True)
    first_raw = jnp.sum(products, axis=1, keepdims=True) / gain
    total = jnp.sum(squares) + jnp.sum(first_raw * first_raw)
    places = jnp.sum(jnp.where(diagonal, first_raw, 0.0), axis=0, keepdims=True)
    message_ref[...] = jnp.full(message_ref.shape, total, F32)
    for k in range(D // LANES):
        message_ref[k : k + 1, :] = places[:, k * LANES : (k + 1) * LANES]


def expand_column(c):
    right = HALF + SPLIT
    turn = right + HALF
    if c < right:
        return c
    if turn <= c < turn + HALF - SPLIT:
        return c - HALF
    return None


def adam_kernel(message_ref, own_ref, side_ref, other_ref, *refs):
    states, vectors, outputs, vector_outputs, norm_ref = refs[:12], refs[12:20], refs[20:35], refs[35:45], refs[45]
    results, blocks, sem = refs[46:61], refs[61], refs[62]
    wide, narrow = lax.axis_index("wide"), lax.axis_index("narrow")
    norm = jnp.sqrt(message_ref[4:5, :])
    norm_ref[0, 0] = jnp.max(norm)
    clip = CLIP_LIMIT / jnp.maximum(norm, CLIP_LIMIT)
    right = HALF + SPLIT
    turn = right + HALF
    blocks[narrow] = own_ref[...]
    blocks[narrow ^ 1] = other_ref[0]
    blocks[narrow ^ 2] = side_ref[...]
    blocks[narrow ^ 3] = other_ref[1]

    def update(which, gradient, rows, place):
        weight, momentum, variance, average = [ref[rows, place] for ref in states[4 * which : 4 * which + 4]]
        updates = adam_update(
            weight, gradient.astype(F32), momentum, variance, average, clip, RATE_MATRIX, DECAY_MATRIX
        )
        for ref, value in zip(results[5 * which : 5 * which + 5], updates):
            ref[rows, place] = value

    def do_member(member, carry):
        thin = run(member * BLOCK, BLOCK)
        for c in range(0, turn + HALF - SPLIT + ROW, LANES):
            gradient = blocks[member, :, c : c + LANES]
            at = expand_column(c)
            if at is not None:
                update(0, gradient, thin, slice(at, at + LANES))
            elif c < turn:
                k, at = (c - right) // D, (c - right) % D
                update(1, gradient, run(member * 48 + k * BLOCK, BLOCK), slice(at, at + LANES))
            else:
                at = c - turn - (HALF - SPLIT)
                update(2, gradient, thin, slice(at, at + LANES))
        for i in range(15):
            rows = run(member * 48, 48) if 5 <= i < 10 else thin
            pltpu.make_async_copy(results[i].at[rows, :], outputs[i].at[rows, :], sem.at[i]).start()
        return carry

    lax.fori_loop(0, 4, do_member, 0)
    own = blocks[0, :, turn + HALF - SPLIT + ROW :].astype(F32)
    gains = jnp.where(wide == 0, message_ref[0:2, :], jnp.where(wide == 1, message_ref[2:4, :], own[0:2, :]))
    for which, gradient in ((0, gains), (1, own[2:3, :64])):
        weight, momentum, variance, average = [ref[...] for ref in vectors[4 * which : 4 * which + 4]]
        updates = adam_update(
            weight, gradient, momentum, variance, average, clip[:, : gradient.shape[1]], RATE_VECTOR, 0.0
        )
        for ref, value in zip(vector_outputs[5 * which : 5 * which + 5], updates):
            ref[...] = value
    for i in range(15):
        pltpu.make_async_copy(results[i], outputs[i], sem.at[i]).wait()


def call_kernel(kernel, name, args, in_specs, out_types, scratch, flops, limit=VMEM_LIMIT):
    vmem = pl.BlockSpec(memory_space=pltpu.VMEM)
    specs = [kind[1] if isinstance(kind, tuple) else vmem for kind in out_types]
    types = [
        kind[0] if isinstance(kind, tuple) else pltpu.VMEM(kind.shape, kind.dtype) for kind in out_types
    ]
    in_specs = [vmem if spec is None else spec for spec in in_specs]
    args = [
        pltpu.with_memory_space_constraint(value, pltpu.HBM) if spec.memory_space == pltpu.HBM else value
        for value, spec in zip(args, in_specs)
    ]
    results = pl.pallas_call(
        kernel,
        name=name,
        in_specs=in_specs,
        out_specs=specs,
        out_shape=types,
        scratch_shapes=scratch,
        compiler_params=pltpu.CompilerParams(vmem_limit_bytes=limit),
        cost_estimate=pl.CostEstimate(flops=int(flops), bytes_accessed=int(flops / 500), transcendentals=0),
    )(*args)
    return list(results)


def swap_with(value, axis, size, bit):
    return lax.ppermute(value, axis, [(i, i ^ bit) for i in range(size)])


def after(value, *others):
    return lax.optimization_barrier((value,) + others)[0]


def sum_core(keep_far, came):
    return (keep_far.astype(F32) + came[1].astype(F32)).astype(BF16)


def adam_update(weight, gradient, momentum, variance, average, clip_scale, step_rate, decay_rate):
    ema_rate = min(EMA_DECAY, (1.0 + STEP) / (10.0 + STEP))
    clipped = clip_scale * gradient
    moment = BETA_FIRST * momentum + (1.0 - BETA_FIRST) * clipped
    square = BETA_SECOND * variance + (1.0 - BETA_SECOND) * clipped * clipped
    first_hat = moment * (1.0 / (1.0 - BETA_FIRST**STEP))
    second_hat = square * (1.0 / (1.0 - BETA_SECOND**STEP))
    updated = weight - step_rate * (
        first_hat / (jnp.sqrt(second_hat) + ADAM_EPS) + decay_rate * weight
    )
    smoothed = ema_rate * average + (1.0 - ema_rate) * updated
    return (clipped, moment, square, updated, smoothed)


def on_device(
    activations,
    cotangent,
    doc_lengths,
    expand_weight,
    expand_momentum,
    expand_variance,
    expand_average,
    shrink_weight,
    shrink_momentum,
    shrink_variance,
    shrink_average,
    spatial_weight,
    spatial_momentum,
    spatial_variance,
    spatial_average,
    norm_gains,
    gains_momentum,
    gains_variance,
    gains_average,
    spatial_bias,
    bias_momentum,
    bias_variance,
    bias_average,
):
    narrow_size, wide_size = lax.axis_size("narrow"), lax.axis_size("wide")
    wide, narrow = lax.axis_index("wide"), lax.axis_index("narrow")
    group_rows, quarter = activations.shape[0], activations.shape[1]
    rows = group_rows // narrow_size
    tokens = rows * ROW
    tree = (wide_size, narrow_size) == (8, 4)
    smem = pl.BlockSpec(memory_space=pltpu.SMEM)
    anywhere = pl.BlockSpec(memory_space=pl.ANY)
    stored = pl.BlockSpec(memory_space=pltpu.HBM)
    shape = jax.ShapeDtypeStruct
    dma = pltpu.SemaphoreType.DMA
    part = shape((rows, quarter, D), BF16)
    product = 2 * tokens * HALF * D
    cross_x = lambda value: swap_with(value, "wide", wide_size, 1)
    cross_y = lambda value: swap_with(value, "narrow", narrow_size, 2)
    cross_core = lambda value: swap_with(value, "narrow", narrow_size, 1)

    def trade(core_part, pair):
        side = cross_y(pair)
        return [cross_core(core_part), side, cross_core(side)]

    def stack(values):
        kind = shape((len(values), *values[0].shape), values[0].dtype)
        return call_kernel(stack_kernel, "stack", values, [None] * len(values), [kind], [], product // 64)[0]

    def add(*values):
        kind = shape(values[0].shape, values[0].dtype)
        return call_kernel(add_kernel, "add", values, [None] * len(values), [kind], [], product // 64)[0]

    pair = shape((2, *part.shape), BF16)

    cut_types = [(pair, stored), (shape((2, *pair.shape), BF16), stored)]
    if tree:
        core_cut, pair_cut, first_own = call_kernel(
            open_kernel,
            "open",
            [
                activations,
                cotangent,
                expand_weight,
                spatial_weight,
                norm_gains.reshape(2, LANES),
                spatial_bias.reshape(1, 64),
            ],
            [stored] * 6,
            cut_types + [shape((32, HALF + ROW + VECTOR_LANES), BF16)],
            [pltpu.VMEM((32, HALF), F32), pltpu.VMEM((32, ROW), F32), pltpu.VMEM((2, LANES), F32)]
            + [pltpu.VMEM((1, 64), F32), dma((4,)), dma((6,))],
            product // 64,
        )
        over_z = lambda own: [swap_with(own, "wide", wide_size, 2 * s) for s in range(1, 4)]
        came_z = over_z(first_own)
        side_came = cross_y(pair_cut)
        expand_own, shrink_own = call_kernel(
            pack_second_kernel,
            "pack_second",
            [expand_weight, shrink_weight],
            [stored, stored],
            [shape((32, HALF), BF16)] * 2,
            [pltpu.VMEM((32, HALF), F32), pltpu.VMEM((96, D), F32), dma((2,))],
            product // 64,
        )
        *came_z, core_came, _, expand_own = lax.optimization_barrier(
            (*came_z, cross_core(core_cut), pair_cut, expand_own)
        )
        first_near = stack([first_own, *came_z])
        first_across = cross_x(first_near)
        expand_own = after(expand_own, first_near)
        *came_z, side_came = lax.optimization_barrier((*over_z(expand_own), side_came))
        expand_near = stack([expand_own, *came_z])
        expand_across = cross_x(after(expand_near, first_across))
        shrink_own = after(shrink_own, expand_near)
        shrink_came = over_z(shrink_own)
        near_core = cross_core(after(first_near, expand_near))
        across_core = cross_core(after(first_across, expand_near))
        forward_came = cross_core(after(side_came, expand_near))
        first_pieces = [after(first_near, expand_near), first_across, near_core, across_core]
        small_pieces = first_pieces[:2]
        near_other = cross_core(expand_near)
        count = len(PIECES)
    else:
        gather = lambda value: lax.all_gather(value.astype(BF16), "wide", axis=0, tiled=True)
        expand_low = gather(expand_weight)
        gains_low, bias_low = gather(norm_gains), gather(spatial_bias)
        small = jnp.concatenate(
            [
                gains_low.reshape(8, 2, 128),
                jnp.pad(bias_low.reshape(8, 1, 64), ((0, 0), (0, 0), (0, 64))),
                jnp.zeros((8, 13, 128), BF16),
            ],
            axis=1,
        )
        first_pieces = [expand_low[:, HALF:], gather(spatial_weight)]
        small_pieces = [small, small]
        expand_pieces, shrink_pieces = [expand_low[:, :HALF]], [gather(shrink_weight)]
        core_cut, pair_cut = call_kernel(
            cut_kernel, "cut", [activations, cotangent], [stored] * 2, cut_types, [dma((6,))], product // 64
        )
        core_came, side_came, forward_came = trade(core_cut, pair_cut)
        count = 2

    low_d, low_half = shape((rows, ROW, D), BF16), shape((rows, ROW, HALF), BF16)
    thin = shape((rows, ROW, 128), F32)
    weight_type = shape((D, HALF), BF16)

    normed, xhat, scale, gate_normed, slope, rstd, spatial_low, gains, bias_col, gate_weight = call_kernel(
        functools.partial(gating_kernel, tree, count, narrow_size),
        "gating",
        [activations, core_came, side_came, forward_came] + list(first_pieces) + list(small_pieces),
        [stored] + [anywhere] * (narrow_size - 1 + count + 2),
        [low_d, low_d, thin, low_half, low_half, thin]
        + [shape((ROW, ROW), BF16), shape((8, D + HALF), F32), shape((ROW, 128), F32), weight_type],
        [
            pltpu.VMEM((8, BLOCK, 128), BF16),
            pltpu.VMEM((narrow_size, *part.shape), BF16),
            pltpu.VMEM((ROW, HALF), F32),
            pltpu.VMEM((ROW, 128), F32),
            dma((4,)),
        ],
        product // 64,
    )

    bias_late = bias_col
    if tree:
        *shrink_came, expand_across, _ = lax.optimization_barrier((*shrink_came, expand_across, normed))
        shrink_near = stack([shrink_own, *shrink_came])
        shrink_across = cross_x(shrink_near)
        expand_pieces = [expand_near, expand_across, near_other, cross_core(expand_across)]
        bias_late = after(bias_col, shrink_near)
    mixed = call_kernel(
        mixing_kernel,
        "mixing",
        [doc_lengths, spatial_low, gate_normed, bias_late],
        [smem] + [None] * 3,
        [low_half],
        [],
        product // 64,
    )[0]
    normed_late = normed
    if tree:
        expand_pieces[3], normed_late, _ = lax.optimization_barrier((expand_pieces[3], normed, mixed))
    content, content_slope, content_weight, cots_turned, cots = call_kernel(
        functools.partial(content_up_kernel, tree, narrow_size),
        "content_up",
        [normed_late, cotangent, core_came, side_came, forward_came, *expand_pieces],
        [None, stored] + [anywhere] * (narrow_size - 1 + len(expand_pieces)),
        [low_half, low_half, weight_type, shape((D, tokens), BF16), shape((tokens, D), BF16)],
        [dma((2,))],
        product // 64,
    )
    if tree:
        shrink_across, _ = lax.optimization_barrier((shrink_across, content))
        shrink_pieces = [shrink_near, shrink_across, cross_core(shrink_near), cross_core(shrink_across)]

    def raw_outputs(column_list, plain):
        if tree:
            return [
                shape(size, BF16)
                for columns in column_list
                for size in ((2, 4, BLOCK, columns), (2, 4, BLOCK, columns), (2, 2, 4, BLOCK, columns))
            ]
        return [shape(size, F32) for size in plain]

    gated, content_grad, grad_mixed, bias_part, shrink_low, *shrink_raws = call_kernel(
        functools.partial(content_down_kernel, tree, len(shrink_pieces)),
        "content_down",
        [doc_lengths, content, content_slope, mixed, cots, cots_turned, *shrink_pieces],
        [smem] + [None] * 5 + [anywhere] * len(shrink_pieces),
        [low_half, low_half, low_half, shape((ROW, 128), F32), shape((HALF, D), BF16)]
        + raw_outputs((HALF,), ((HALF, D),)),
        [pltpu.VMEM((tokens, 128), F32), pltpu.VMEM((HALF, D), BF16), dma(())],
        product // 64,
    )
    if tree:
        came = {"shrink": cross_core(shrink_raws[2])}
    sum_scratch = [pltpu.VMEM((D, tokens), BF16), pltpu.VMEM((D, D), F32)]
    content_raws = call_kernel(
        functools.partial(content_sum_kernel, tree),
        "content_sum",
        [normed, content_grad],
        [None] * 2,
        raw_outputs((HALF,), ((D, HALF),)),
        sum_scratch,
        product // 64,
    )
    mixed_late = grad_mixed
    if tree:
        came["shrink"], content_raws[0] = lax.optimization_barrier((came["shrink"], content_raws[0]))
        came["content"] = cross_core(content_raws[2])
        far = {"shrink": sum_core(shrink_raws[1], came["shrink"])}
        came_far = {"shrink": cross_y(far["shrink"])}
        mixed_late = after(grad_mixed, far["shrink"])
    square_sum = call_kernel(
        spatial_sum_kernel,
        "spatial_sum",
        [doc_lengths, mixed_late, gate_normed],
        [smem, None, None],
        [shape((ROW, ROW), F32)],
        [],
        product // 64,
    )[0]
    if tree:
        came["content"], square_sum = lax.optimization_barrier((came["content"], square_sum))
        far["content"] = sum_core(content_raws[1], came["content"])
        came_far["content"] = cross_x(far["content"])
        mixed_late = after(grad_mixed, far["content"])

    gate_grad, vectors = call_kernel(
        gate_back_kernel,
        "gate_back",
        [doc_lengths, mixed_late, gate_normed, slope, rstd, spatial_low, gains, bias_part],
        [smem] + [None] * 7,
        [low_half, shape((8, BLOCK, 128), F32)],
        [
            pltpu.VMEM((ROW, ROW), BF16),
            pltpu.VMEM((ROW, HALF), BF16),
            pltpu.VMEM((ROW, 128), F32),
            pltpu.VMEM((ROW, 128), F32),
            pltpu.VMEM((8, HALF), F32),
            pltpu.VMEM((8, HALF), F32),
        ],
        product // 64,
    )
    normed_late = normed
    if tree:
        came_far["shrink"], normed_late = lax.optimization_barrier((came_far["shrink"], normed))
    second_raws = call_kernel(
        functools.partial(gate_sum_kernel, tree),
        "gate_sum",
        [normed_late, gate_grad, square_sum, vectors],
        [None] * 4,
        raw_outputs((SPLIT, HALF - SPLIT + ROW + VECTOR_LANES), ((D, HALF), (ROW, ROW), (8, BLOCK, 128))),
        sum_scratch,
        product // 64,
    )
    def side_step(terms, widths):
        kinds = [shape((4, BLOCK, width), BF16) for width in widths]
        return call_kernel(side_kernel, "side", terms, [None] * 6, kinds, [], product // 64)

    gated_late = gated
    if tree:
        second_raws[2], second_raws[5], came_far["content"] = lax.optimization_barrier(
            (second_raws[2], second_raws[5], came_far["content"])
        )
        second_came = [cross_core(second_raws[i]) for i in (2, 5)]
        first_terms = [content_raws[0], came["content"], came_far["content"]]
        first_terms += [shrink_raws[0], came["shrink"], came_far["shrink"]]
        first_sides = side_step(first_terms, (HALF, HALF))
        first_came_side = [cross_y(first_sides[0]), cross_x(first_sides[1])]
        gated_late = after(gated, second_raws[0], *first_sides)
    part_scratch = pltpu.VMEM((narrow_size, *part.shape), BF16)
    layer_own, layer_core, layer_pair = call_kernel(
        layer_kernel,
        "layer",
        [gated_late, shrink_low],
        [None] * 2,
        [part, part, pair],
        [part_scratch],
        product // 64,
    )
    grad_late = gate_grad
    if tree:
        *second_came, layer_own = lax.optimization_barrier((*second_came, layer_own))
        second_far = [sum_core(second_raws[1], second_came[0]), sum_core(second_raws[4], second_came[1])]
        second_came_far = [cross_x(second_far[0]), cross_y(second_far[1])]
        grad_late = after(gate_grad, *second_far)
    grad_own, core_back, pair_back = call_kernel(
        back_kernel,
        "back",
        [grad_late, content_grad, gate_weight, content_weight, xhat, scale, gains, layer_core, layer_pair],
        [None] * 9,
        [part, pair, shape((2, *pair.shape), BF16)],
        [part_scratch],
        product // 64,
    )

    def give(cots_base, acts_base, returned):
        whole = (group_rows, quarter, D)
        return call_kernel(
            give_kernel,
            "give",
            [cots_base, acts_base, grad_own, layer_own, *returned],
            [None] * 7,
            [(shape(whole, F32), stored), (shape(whole, BF16), stored)],
            [
                pltpu.VMEM((narrow_size, *part.shape), F32),
                pltpu.VMEM((narrow_size, *part.shape), BF16),
                dma((2, narrow_size)),
            ],
            product // 64,
        )

    if tree:
        columns = HALF + HALF + SPLIT + (HALF - SPLIT) + ROW + VECTOR_LANES
        tied = lax.optimization_barrier((*second_came_far, *first_came_side, grad_own))
        second_came_far, first_came_side, grad_own = tied[:2], tied[2:4], tied[4]
        second_terms = [second_raws[0], second_came[0], second_came_far[0]]
        second_terms += [second_raws[3], second_came[1], second_came_far[1]]
        second_sides = side_step(second_terms, (SPLIT, HALF - SPLIT + ROW + VECTOR_LANES))
        second_came_side = [cross_y(second_sides[0]), cross_x(second_sides[1])]
        terms = first_terms[:3] + second_terms[:3] + first_terms[3:] + second_terms[3:]
        came_side = [first_came_side[0], second_came_side[0], first_came_side[1], second_came_side[1]]
        mine, *sent = call_kernel(
            fold_kernel,
            "fold",
            terms + came_side,
            [None] * 16,
            [shape((BLOCK, columns), F32)] + [shape((BLOCK, columns), BF16)] * 3,
            [],
            product // 64,
        )
        came_z = [swap_with(sent[s - 1], "wide", wide_size, 2 * s) for s in range(1, 4)]
        matrices = [expand_weight, expand_momentum, expand_variance, expand_average]
        matrices += [shrink_weight, shrink_momentum, shrink_variance, shrink_average]
        matrices += [spatial_weight, spatial_momentum, spatial_variance, spatial_average]
        fetched = [*matrices, cotangent, activations]
        states = call_kernel(
            fetch_kernel,
            "fetch",
            list(lax.optimization_barrier((*fetched, sent[0]))[:14]),
            [stored] * 14,
            [shape(value.shape, value.dtype) for value in fetched],
            [dma((14,))],
            product // 64,
        )
        states, bases = states[:12], states[12:]
        side_back = cross_y(after(pair_back, sent[0]))
        core_back = cross_core(after(core_back, sent[0]))
        *came_z, first_state = lax.optimization_barrier((*came_z, states[0]))
        low, message = call_kernel(
            norm_kernel,
            "norm",
            [mine, *came_z, first_state, gains],
            [None] * 6,
            [shape((BLOCK, columns), BF16), shape((8, LANES), F32)],
            [],
            product // 64,
        )
        side = cross_y(low)
        message = add(message, cross_core(message))
        message = add(message, cross_x(message))
        *arrived, side, side_back = lax.optimization_barrier((*over_z(message), side, side_back))
        message = add(message, *arrived)
        other = cross_core(stack([low, side]))
        returned = [core_back, side_back, cross_core(side_back)]
        input_grad, layer_out = give(*bases, returned)
        arrived, layer_out, input_grad = lax.optimization_barrier((cross_y(message), layer_out, input_grad))
        message = add(message, arrived)
        as_rows = lambda value: value.reshape(-1, min(value.shape[0], LANES))
        vector_states = [norm_gains, gains_momentum, gains_variance, gains_average]
        vector_states += [spatial_bias, bias_momentum, bias_variance, bias_average]
        vector_kinds = [shape((2, LANES), F32)] * 5 + [shape((1, 64), F32)] * 5
        *updates, norm_row = call_kernel(
            adam_kernel,
            "adam",
            [message, low, side, other, *states] + [as_rows(value) for value in vector_states],
            [None] * 24,
            [(shape(value.shape, F32), stored) for value in (matrices[0], matrices[4], matrices[8]) for _ in range(5)]
            + [(kind, pl.BlockSpec(memory_space=pltpu.VMEM)) for kind in vector_kinds]
            + [(shape((1, 1), F32), smem)],
            [pltpu.VMEM(value.shape, F32) for value in (matrices[0], matrices[4], matrices[8]) for _ in range(5)]
            + [pltpu.VMEM((4, BLOCK, columns), BF16), dma((15,))],
            product // 64,
        )
        grad_norm = norm_row[0, 0]
        results = [layer_out, input_grad, grad_norm, *updates[:15]]
        return tuple(results + [value.reshape(-1) for value in updates[15:]])

    returned = trade(core_back, pair_back)
    input_grad, layer_out = give(cotangent, activations, returned)
    gains_size, bias_size = norm_gains.shape[0], spatial_bias.shape[0]
    vectors = lax.psum(second_raws[2], ("narrow", "wide"))
    totals = lax.psum(
        (jnp.concatenate([content_raws[0], second_raws[0]], axis=1), shrink_raws[0], second_raws[1]), "narrow"
    )
    expand_shard, shrink_shard, spatial_shard = [
        lax.psum_scatter(total, "wide", scatter_dimension=0, tiled=True) for total in totals
    ]
    second_shard = lax.dynamic_slice_in_dim(vectors[:, :2].reshape(-1), wide * gains_size, gains_size)
    bias_shard = lax.dynamic_slice_in_dim(vectors[:, 2, :64].reshape(-1), wide * bias_size, bias_size)
    low_weight = expand_weight.astype(BF16).astype(F32)
    height = expand_weight.shape[0]
    first_gain = lax.dynamic_slice_in_dim(gains[0], wide * height, height)
    first_raw = jnp.sum(low_weight * expand_shard, axis=1) / first_gain
    squares = [expand_shard, shrink_shard, spatial_shard, second_shard, bias_shard, first_raw]
    square_total = lax.psum(sum(jnp.sum(value * value) for value in squares), "wide")
    first_all = lax.all_gather(first_raw, "wide", axis=0, tiled=True)
    first_all = jnp.concatenate([first_all, jnp.zeros((HALF,), F32)])
    gains_shard = second_shard + lax.dynamic_slice_in_dim(first_all, wide * gains_size, gains_size)
    grad_norm = jnp.sqrt(square_total)
    clip_scale = CLIP_LIMIT / jnp.maximum(grad_norm, CLIP_LIMIT)
    results = [layer_out, input_grad, grad_norm]
    for weight, shard, momentum, variance, average, rate, decay in (
        (expand_weight, expand_shard, expand_momentum, expand_variance, expand_average, RATE_MATRIX, DECAY_MATRIX),
        (shrink_weight, shrink_shard, shrink_momentum, shrink_variance, shrink_average, RATE_MATRIX, DECAY_MATRIX),
        (spatial_weight, spatial_shard, spatial_momentum, spatial_variance, spatial_average, RATE_MATRIX, DECAY_MATRIX),
        (norm_gains, gains_shard, gains_momentum, gains_variance, gains_average, RATE_VECTOR, 0.0),
        (spatial_bias, bias_shard, bias_momentum, bias_variance, bias_average, RATE_VECTOR, 0.0),
    ):
        results += adam_update(weight, shard, momentum, variance, average, clip_scale, rate, decay)
    return tuple(results)


def solution(mesh):
    tokens, matrix, vector = P("wide", "narrow", None), P("wide", None), P("wide")
    return jax.shard_map(
        on_device,
        mesh=mesh,
        in_specs=(tokens, tokens) + (matrix,) * 13 + (vector,) * 8,
        out_specs=(tokens, tokens, P()) + (matrix,) * 15 + (vector,) * 10,
        check_vma=False,
    )
```
